32 devices in a mesh: fsdp: 8 (over z, y), seq: 4 (over x, core).
Axes of the slice: x: 2, y: 2, z: 4, core: 2. Of those that a mesh axis runs over, the one named last changes fastest.
Arguments:
- tokens: bfloat16 [12288, 1024], P(('fsdp', 'seq')), may hold values from -6 to 6
- cotangent: bfloat16 [12288, 1024], P(('fsdp', 'seq')), may hold values from -6 to 6
- ln1_gain: bfloat16 [1024], P('fsdp'), may hold values from 0.099609375 to 1.8984375
- ln1_bias: bfloat16 [1024], P('fsdp'), may hold values from -1.5 to 1.5
- w_qkv: bfloat16 [1024, 3072], P('fsdp'), may hold values from -0.1875 to 0.1875
- b_qv: bfloat16 [2048], P('fsdp'), may hold values from -2.5 to 2.5
- w_out: bfloat16 [1024, 1024], P('fsdp'), may hold values from -0.375 to 0.375
- b_out: bfloat16 [1024], P('fsdp'), may hold values from -1.5 to 1.5
- ln2_gain: bfloat16 [1024], P('fsdp'), may hold values from 0.099609375 to 1.8984375
- ln2_bias: bfloat16 [1024], P('fsdp'), may hold values from -1.5 to 1.5
- w_fc: bfloat16 [1024, 4096], P('fsdp'), may hold values from -0.1875 to 0.1875
- b_fc: bfloat16 [4096], P('fsdp'), may hold values from -2.5 to 2.5
- w_proj: bfloat16 [4096, 1024], P('fsdp'), may hold values from -0.09375 to 0.09375
- b_proj: bfloat16 [1024], P('fsdp'), may hold values from -1.5 to 1.5
Outputs:
- output: bfloat16 [12288, 1024], P(('fsdp', 'seq'))
- grad_tokens: bfloat16 [12288, 1024], P(('fsdp', 'seq'))
- grad_ln1_gain: float32 [1024], P('fsdp')
- grad_ln1_bias: float32 [1024], P('fsdp')
- grad_w_qkv: float32 [1024, 3072], P('fsdp')
- grad_b_qv: float32 [2048], P('fsdp')
- grad_w_out: float32 [1024, 1024], P('fsdp')
- grad_b_out: float32 [1024], P('fsdp')
- grad_ln2_gain: float32 [1024], P('fsdp')
- grad_ln2_bias: float32 [1024], P('fsdp')
- grad_w_fc: float32 [1024, 4096], P('fsdp')
- grad_b_fc: float32 [4096], P('fsdp')
- grad_w_proj: float32 [4096, 1024], P('fsdp')
- grad_b_proj: float32 [1024], P('fsdp')
- rms_values: float32 [3], replicated
The draws below stay inside these ranges and needn't reach their ends.
All inputs are finite; a program needn't handle non-finite values.
Results may differ from the reference program's by a relative error of at most 0.015.
Values may be sent and summed in bfloat16 or wider, within the bound.
A program may use at most 192 MiB of HBM per device.

```python
import jax
import jax.numpy as jnp
from jax import lax

D = 1024
HEADS = 16
FF = 4096
BLK = 256
HD = 64
LENGTH = 1536
SEQS = 8
TOKENS = 12288


def draw_tokens(key, part):
    key = jax.random.fold_in(key, 7)
    position = jnp.arange(TOKENS, dtype=jnp.int32)
    sequence = (position // LENGTH).astype(jnp.float32) / SEQS
    within = (position % LENGTH).astype(jnp.float32) / LENGTH
    row_scale = 0.2 * 4.0 ** (sequence + within)
    random_part = jax.random.truncated_normal(key, -2.0, 2.0, (TOKENS, D), jnp.float32)
    values = random_part * row_scale[:, None]
    return jnp.clip(values, -6.0, 6.0).astype(jnp.bfloat16)


def strengthened(result, rng, source, target, shards_of, factor):
    owner, partner = [(jnp.arange(result.shape[dim]) // (result.shape[dim] // shards_of)).reshape([-1 if axis == dim else 1 for axis in range(result.ndim)]) for dim in (source, target)]
    chosen = jax.random.permutation(rng, shards_of)[partner]
    strong = (owner == chosen) | (owner == (partner + shards_of // 2) % shards_of)
    return jnp.where(strong, factor * result, result)


def block_scale(key, extent, shards, least, top_value):
    def one(axis_at, parts):
        draws = jax.random.uniform(jax.random.fold_in(jax.random.fold_in(key, 6), axis_at), (parts,), jnp.float32, least / len(shards), top_value / len(shards))
        return jnp.repeat(jnp.exp(draws), extent[axis_at] // parts).reshape((-1,) + (1,) * (len(extent) - axis_at - 1))

    level = one(*shards[0])
    for cut in shards[1:]:
        level = level * one(*cut)
    return level


def centred(key, extent, deviation, reach, split=(), kind=jnp.bfloat16):
    drawn = jax.random.normal(key, extent, jnp.float32) * deviation
    if len(split) > 0:
        drawn = block_scale(key, extent, split, -0.22, 0.18) * drawn
    return jnp.clip(drawn, min=-reach, max=reach).astype(kind)


def bell_draw_with(rng, shape, deviation, limit, pieces, heavy, kind=jnp.bfloat16):
    array = deviation * jax.random.normal(rng, shape, jnp.float32)
    if pieces:
        array = array * block_scale(rng, shape, pieces, -0.22, 0.18)
    return jnp.clip(strengthened(array, jax.random.fold_in(rng, 3), *heavy), -limit, limit).astype(kind)


def setup_inputs(seed: int = 0) -> dict:
    keys = jax.random.split(jax.random.key(seed), 15)
    tokens = draw_tokens(jax.random.fold_in(keys[14], 71), 0)
    cotangent = bell_draw_with(keys[1], (TOKENS, D), 1.0, 6.0, ((0, 32),), (0, 1, 32, 2.75))
    ln1_gain = jnp.clip(1.0 + 0.18 * jax.random.normal(keys[2], (D,), jnp.float32), 0.099609375, 1.8984375).astype(jnp.bfloat16)
    ln1_bias = centred(keys[3], (D,), 0.3, 1.5, ((0, 8),))
    w_qkv = centred(keys[4], (D, 3 * D), D ** -0.5, 0.1875, ((0, 8),))
    b_qv = centred(keys[5], (2 * D,), 0.5, 2.5, ((0, 8),))
    w_out = centred(keys[6], (D, D), (D // 4) ** -0.5, 0.375, ((0, 8),))
    b_out = centred(keys[7], (D,), 0.3, 1.5, ((0, 8),))
    ln2_gain = jnp.clip(1.0 + 0.18 * jax.random.normal(keys[8], (D,), jnp.float32), 0.099609375, 1.8984375).astype(jnp.bfloat16)
    ln2_bias = centred(keys[9], (D,), 0.3, 1.5, ((0, 8),))
    w_fc = centred(keys[10], (D, FF), D ** -0.5, 0.1875, ((0, 8),))
    b_fc = centred(keys[11], (FF,), 0.5, 2.5, ((0, 8),))
    w_proj = centred(keys[12], (FF, D), FF ** -0.5, 0.09375, ((0, 8),))
    b_proj = centred(keys[13], (D,), 0.3, 1.5, ((0, 8),))
    return dict(tokens=tokens, cotangent=cotangent, ln1_gain=ln1_gain, ln1_bias=ln1_bias, w_qkv=w_qkv, b_qv=b_qv, w_out=w_out, b_out=b_out, ln2_gain=ln2_gain, ln2_bias=ln2_bias, w_fc=w_fc, b_fc=b_fc, w_proj=w_proj, b_proj=b_proj)


EPSILON = 1e-05
exact_mode = lax.Precision.HIGHEST

@jax.custom_vjp
def low(v):
    return lax.optimization_barrier(v.astype(jnp.bfloat16)).astype(jnp.float32)

@jax.custom_vjp
def low_back(v):
    return v

def low_keep(v):
    return (low(v), None)

def low_pass(kept, grad):
    return (grad,)

def back_keep(v):
    return (v, None)

def back_low(kept, grad):
    return (low(grad),)
low.defvjp(low_keep, low_pass)
low_back.defvjp(back_keep, back_low)

def layer_norm(values, gain_vec, shift):
    centre = values - lax.optimization_barrier(jnp.mean(values, axis=-1, keepdims=True))
    spread = lax.optimization_barrier(jnp.mean(centre * centre, axis=-1, keepdims=True))
    return centre * lax.rsqrt(spread + EPSILON) * gain_vec + shift

def attend(queries, keys_all, values_all):
    length = queries.shape[0]
    block_rows = min(512, length)
    score_scale = HD ** (-0.5)
    key_block = jnp.arange(length, dtype=jnp.int32) // BLK

    def one_block(block_start):
        query_rows = lax.dynamic_slice_in_dim(queries, block_start, block_rows, 0)
        scores = jnp.einsum('qhd,khd->hqk', query_rows, keys_all, precision=exact_mode) * score_scale
        scores = low_back(scores)
        query_block = (block_start + jnp.arange(block_rows, dtype=jnp.int32)) // BLK
        allowed = key_block[None, :] <= query_block[:, None]
        scores = jnp.where(allowed[None], scores, -jnp.inf)
        largest = lax.optimization_barrier(jnp.max(scores, axis=-1, keepdims=True))
        weights = jnp.exp(scores - largest)
        soft_probs = weights / lax.optimization_barrier(jnp.sum(weights, axis=-1, keepdims=True))
        return jnp.einsum('hqk,khd->qhd', low(soft_probs), values_all, precision=exact_mode)
    starts = jnp.arange(length // block_rows, dtype=jnp.int32) * block_rows
    blocks = lax.map(jax.checkpoint(one_block), starts)
    return blocks.reshape(length, HEADS * HD)

def forward(seq_tokens, ln1_gain, ln1_bias, w_qkv, b_qv, w_out, b_out, ln2_gain, ln2_bias, w_fc, b_fc, w_proj, b_proj):
    length = seq_tokens.shape[0]
    normed_one = low(layer_norm(seq_tokens, ln1_gain, ln1_bias))
    bias_full = jnp.concatenate([b_qv[:D], jnp.zeros((D,), jnp.float32), b_qv[D:]])
    projected = low_back(low(jnp.dot(normed_one, w_qkv, precision=exact_mode) + bias_full))
    queries = projected[:, :D].reshape(length, HEADS, HD)
    keys_all = projected[:, D:2 * D].reshape(length, HEADS, HD)
    values_all = projected[:, 2 * D:].reshape(length, HEADS, HD)
    mixed_rows = low_back(low(attend(queries, keys_all, values_all)))
    branch = jnp.dot(mixed_rows, w_out, precision=exact_mode) + b_out
    middle = seq_tokens + low_back(branch)
    normed_two = low(layer_norm(middle, ln2_gain, ln2_bias))
    before = low_back(jnp.dot(normed_two, w_fc, precision=exact_mode) + b_fc)
    activated = low(jax.nn.gelu(before, approximate=True))
    feed_out = jnp.dot(activated, w_proj, precision=exact_mode) + b_proj
    output = middle + low_back(feed_out)
    squares = jnp.stack([jnp.sum(seq_tokens * seq_tokens), jnp.sum(middle * middle), jnp.sum(output * output)])
    return (output, squares)

def reference(tokens, cotangent, ln1_gain, ln1_bias, w_qkv, b_qv, w_out, b_out, ln2_gain, ln2_bias, w_fc, b_fc, w_proj, b_proj):
    params = tuple((weight_arg.astype(jnp.float32) for weight_arg in (ln1_gain, ln1_bias, w_qkv, b_qv, w_out, b_out, ln2_gain, ln2_bias, w_fc, b_fc, w_proj, b_proj)))
    token_seqs = tokens.astype(jnp.float32).reshape(SEQS, LENGTH, D)
    cot_seqs = cotangent.astype(jnp.float32).reshape(SEQS, LENGTH, D)

    def scan_step(running, item_pair):
        grad_sums, stat_sums = running
        seq_tokens, cot_rows = item_pair
        seq_out, pullback, squares = jax.vjp(forward, seq_tokens, *params, has_aux=True)
        pulled = pullback(cot_rows)
        grad_sums = tuple((earlier_sum + new_part for earlier_sum, new_part in zip(grad_sums, pulled[1:])))
        return ((grad_sums, stat_sums + squares), (seq_out, pulled[0]))
    zero_grads = tuple((jnp.zeros_like(weight_arg) for weight_arg in params))
    (grad_sums, stat_sums), (seq_outs, grad_rows) = lax.scan(scan_step, (zero_grads, jnp.zeros((3,), jnp.float32)), (token_seqs, cot_seqs))
    rms_values = jnp.sqrt(stat_sums / (TOKENS * D))
    return (seq_outs.reshape(TOKENS, D).astype(jnp.bfloat16), grad_rows.reshape(TOKENS, D).astype(jnp.bfloat16), grad_sums[0], grad_sums[1], grad_sums[2], grad_sums[3], grad_sums[4], grad_sums[5], grad_sums[6], grad_sums[7], grad_sums[8], grad_sums[9], grad_sums[10], grad_sums[11], rms_values)
```

```python
import functools

import jax
import jax.numpy as jnp
from jax import lax
from jax.experimental import pallas as pl
from jax.experimental.pallas import tpu as pltpu
from jax.sharding import PartitionSpec as P

BLK = 256
HD = 64
EPSILON = 1e-05
MESH = pl.DeviceIdType.MESH
f32, bf16 = jnp.float32, jnp.bfloat16

def geometry():
    F, S = lax.axis_size("fsdp"), lax.axis_size("seq")
    H = 4 if F % 4 == 0 else 1
    L = F // H
    X = S // 2
    return F, S, H, L, X

class Place:
    def __init__(self):
        self.F, self.S, self.H, self.L, self.X = geometry()
        self.f, self.s = lax.axis_index("fsdp"), lax.axis_index("seq")
        self.h, self.l = self.f // self.L, self.f % self.L
        self.x, self.c = self.s // 2, self.s % 2
    def shard(self, k, j):
        return lax.rem(self.h + self.H - k, self.H) * self.L + lax.rem(self.l + self.L - j, self.L)
    def hi(self, k):
        return (lax.rem(self.h + k, self.H) * self.L + self.l, self.s)
    def lo(self, j):
        return (self.h * self.L + lax.rem(self.l + j, self.L), self.s)
    def across(self, i):
        return (self.f, lax.rem(self.x + i, self.X) * 2 + self.c)
    def sibling(self):
        return (self.f, self.x * 2 + 1 - self.c)
    def everyone(self):
        return ([self.hi(k) for k in range(1, self.H)] + [self.lo(j) for j in range(1, self.L)]
                + [self.across(i) for i in range(1, self.X)] + [self.sibling()])

def greet(place):
    barrier = pltpu.get_barrier_semaphore()
    peers = place.everyone()
    for peer in peers:
        pl.semaphore_signal(barrier, inc=1, device_id=peer, device_id_type=MESH)
    pl.semaphore_wait(barrier, len(peers))

def ag_kernel(count, *refs):
    shards, small = refs[:count], refs[count]
    wholes, smalls = refs[count + 1:2 * count + 1], refs[2 * count + 1]
    own_sem, send_sem, hi_sem, lo_sem, x_sem, core_sem, sm_hi_sem, sm_lo_sem = refs[2 * count + 2:]
    p = Place()
    greet(p)
    sent = []
    def push(src, dst, sem, peer):
        cp = pltpu.make_async_remote_copy(src_ref=src, dst_ref=dst, send_sem=send_sem.at[0], recv_sem=sem, device_id=peer, device_id_type=MESH)
        cp.start(); sent.append(cp)
    def arrived(dst, sem):
        pltpu.make_async_copy(dst, dst, sem).wait()
    width = 5 - p.X
    only = p.x * (3 // (p.X - 1)) if p.X > 1 else 0
    def cols(w, start, n):
        C = shards[w].shape[-1]
        return pl.ds(pl.multiple_of(p.c * (C // 2) + start * (C // 8), 128), n * (C // 8))
    def half(w):
        C = shards[w].shape[-1]
        return pl.ds(pl.multiple_of(p.c * (C // 2), 128), C // 2)
    def other_half(w):
        C = shards[w].shape[-1]
        return pl.ds(pl.multiple_of((1 - p.c) * (C // 2), 128), C // 2)
    own = []
    for w in range(count):
        cp = pltpu.make_async_copy(shards[w], wholes[w].at[p.f], own_sem.at[w]); cp.start(); own.append(cp)
    def start_hi(w):
        mine = cols(w, p.x, width)
        for k in range(1, p.H):
            push(shards[w].at[:, mine], wholes[w].at[p.f, :, mine], hi_sem.at[w, k - 1], p.hi(k))
        for j in range(1, p.L):
            push(shards[w].at[:, mine], wholes[w].at[p.f, :, mine], lo_sem.at[w, j - 1, 0], p.lo(j))
    def pieces():
        return [(j, k) for j in range(p.L) for k in range(p.H) if (j, k) != (0, 0)]
    def after(w, j, k):
        piece = wholes[w].at[p.shard(k, j)]
        for i in range(1, p.X):
            e = cols(w, only, 1)
            push(piece.at[:, e], piece.at[:, e], x_sem.at[w, i - 1, j * p.H + k - 1], p.across(i))
    def finish_hi(w, k):
        mine = cols(w, p.x, width)
        piece = wholes[w].at[p.shard(k, 0), :, mine]
        arrived(piece, hi_sem.at[w, k - 1])
        for j in range(1, p.L):
            push(piece, piece, lo_sem.at[w, j - 1, k], p.lo(j))
        after(w, 0, k)
    def finish_lo(w, k):
        mine = cols(w, p.x, width)
        for j in range(1, p.L):
            arrived(wholes[w].at[p.shard(k, j), :, mine], lo_sem.at[w, j - 1, k])
            after(w, j, k)
    def finish_x(w):
        for (j, k) in pieces():
            for i in range(1, p.X):
                src_x = lax.rem(p.x + p.X - i, p.X)
                e = cols(w, src_x * (3 // (p.X - 1)), 1)
                arrived(wholes[w].at[p.shard(k, j), :, e], x_sem.at[w, i - 1, j * p.H + k - 1])
            piece = wholes[w].at[p.shard(k, j), :, half(w)]
            push(piece, piece, core_sem.at[w, j * p.H + k - 1], p.sibling())
    def finish_core(w):
        for (j, k) in pieces():
            arrived(wholes[w].at[p.shard(k, j), :, other_half(w)], core_sem.at[w, j * p.H + k - 1])
    cp = pltpu.make_async_copy(small, smalls.at[p.f], own_sem.at[count]); cp.start(); own.append(cp)
    for k in range(1, p.H):
        push(small, smalls.at[p.f], sm_hi_sem.at[k - 1], p.hi(k))
    for j in range(1, p.L):
        push(small, smalls.at[p.f], sm_lo_sem.at[j - 1, 0], p.lo(j))
    start_hi(0)
    for k in range(1, p.H):
        piece = smalls.at[p.shard(k, 0)]
        arrived(piece, sm_hi_sem.at[k - 1])
        for j in range(1, p.L):
            push(piece, piece, sm_lo_sem.at[j - 1, k], p.lo(j))
    for t in range(count + 2):
        for k in range(p.H):
            if t < count and k > 0:
                finish_hi(t, k)
            if t + 1 < count and k == 1:
                start_hi(t + 1)
            if 0 < t <= count:
                finish_lo(t - 1, k)
        if 0 < t <= count:
            finish_x(t - 1)
        if 1 < t:
            finish_core(t - 2)
    for j in range(1, p.L):
        for k in range(p.H):
            arrived(smalls.at[p.shard(k, j)], sm_lo_sem.at[j - 1, k])
    for cp in own: cp.wait()
    for cp in sent: cp.wait_send()

def gather_all(shards, small):
    F, S, H, L, X = geometry()
    n = len(shards)
    return pl.pallas_call(
        functools.partial(ag_kernel, n),
        out_shape=[jax.ShapeDtypeStruct((F,) + a.shape, a.dtype) for a in list(shards) + [small]],
        in_specs=[pl.BlockSpec(memory_space=pl.ANY)] * (n + 1),
        out_specs=[pl.BlockSpec(memory_space=pl.ANY)] * (n + 1),
        scratch_shapes=[pltpu.SemaphoreType.DMA((n + 1,)), pltpu.SemaphoreType.DMA((1,)),
            pltpu.SemaphoreType.DMA((n, H - 1)), pltpu.SemaphoreType.DMA((n, L - 1, H)),
            pltpu.SemaphoreType.DMA((n, X - 1, F - 1)), pltpu.SemaphoreType.DMA((n, F - 1)),
            pltpu.SemaphoreType.DMA((H - 1,)), pltpu.SemaphoreType.DMA((L - 1, H))],
        compiler_params=pltpu.CompilerParams(collective_id=1, has_side_effects=True),
    )(*shards, small)


def rs_kernel(n, *refs):
    given, small = refs[:n], refs[n]
    outs, small_out = refs[n + 1:2 * n + 1], refs[2 * n + 1]
    rest = list(refs[2 * n + 2:])
    def take(k):
        got = rest[:k]; del rest[:k]; return got
    parts, from_x, from_lo, from_hi, value, from_x_end, half_out = (take(n) for _ in range(7))
    sm_core, sm_x, sm_sum, sm_lo, sm_hi = take(5)
    load_sem, send_sem, x_sem, lo_sem, hi_sem, end_sem, out_sem, core_sem, sm_sem, smx_sem, smlo_sem, smhi_sem = rest
    loads = [pltpu.make_async_copy(given[w], parts[w], load_sem.at[w]) for w in range(n)]
    for load in loads: load.start()
    p = Place()
    greet(p)
    H, L, X = p.H, p.L, p.X
    width = 5 - X
    step = 3 // (X - 1) if X > 1 else 0
    sent = []
    def push(src, dst, sem, peer):
        cp = pltpu.make_async_remote_copy(src_ref=src, dst_ref=dst, send_sem=send_sem.at[0], recv_sem=sem, device_id=peer, device_id_type=MESH)
        cp.start(); sent.append(cp)
    def arrived(dst, sem):
        pltpu.make_async_copy(dst, dst, sem).wait()
    def unit(w): return parts[w].shape[-1] // 4
    def span(w, start, count):
        return pl.ds(pl.multiple_of(start * unit(w), 128), count * unit(w))
    def other_x(i): return lax.rem(p.x + i, X)
    def shard(k, j):
        return lax.rem(p.h + k, H) * L + lax.rem(p.l + j, L)
    def s1(w):
        loads[w].wait()
        for j in list(range(1, L)) + [0]:
            for k in range(H):
                for i in range(1, X):
                    f = shard(k, j)
                    push(parts[w].at[f, :, span(w, other_x(i) * step, 1)], from_x[w].at[i - 1, f], x_sem.at[w, i - 1, j * H + k], p.across(i))
    def add_x(w, k, j):
        f = shard(k, j)
        for i in range(1, X):
            arrived(from_x[w].at[i - 1, f], x_sem.at[w, i - 1, j * H + k])
        if X > 1:
            cols = span(w, p.x * step, 1)
            total = parts[w][f, :, cols].astype(f32)
            for i in range(1, X):
                total = total + from_x[w][i - 1, f].astype(f32)
            parts[w][f, :, cols] = total.astype(bf16)
    def s2(w):
        for j in range(1, L):
            for k in list(range(1, H)) + [0]:
                add_x(w, k, j)
                f = shard(k, j)
                push(parts[w].at[f, :, span(w, p.x, width)], from_lo[w].at[j - 1, lax.rem(p.h + k, H)], lo_sem.at[w, j - 1, k], p.lo(j))
    def s3(w):
        for k in list(range(1, H)) + [0]:
            add_x(w, k, 0)
            h = lax.rem(p.h + k, H)
            f = h * L + p.l
            cols = span(w, p.x, width)
            total = parts[w][f, :, cols].astype(f32)
            for j in range(1, L):
                arrived(from_lo[w].at[j - 1, h], lo_sem.at[w, j - 1, k])
                total = total + from_lo[w][j - 1, h].astype(f32)
            parts[w][f, :, cols] = total.astype(bf16)
            if k > 0:
                push(parts[w].at[f, :, cols], from_hi[w].at[k - 1], hi_sem.at[w, k - 1], p.hi(k))
    def s4(w):
        cols = span(w, p.x, width)
        total = parts[w][p.f, :, cols].astype(f32)
        for k in range(1, H):
            arrived(from_hi[w].at[k - 1], hi_sem.at[w, k - 1])
            total = total + from_hi[w][k - 1].astype(f32)
        value[w][:, cols] = total.astype(bf16)
        for i in range(1, X):
            push(value[w].at[:, cols], from_x_end[w].at[i - 1, :, cols], end_sem.at[w, i - 1], p.across(i))
    def s5(w):
        mine = span(w, p.x * step, 1)
        half_out[w][:, mine] = value[w][:, mine].astype(f32)
        for i in range(1, X):
            src = lax.rem(p.x + X - i, X)
            cols = span(w, src, width)
            arrived(from_x_end[w].at[i - 1, :, cols], end_sem.at[w, i - 1])
            theirs = span(w, src * step, 1)
            half_out[w][:, theirs] = from_x_end[w][i - 1, :, theirs].astype(f32)
        if X < 4:
            both = pl.ds(unit(w), (4 - X) * unit(w))
            total = value[w][:, both].astype(f32)
            for i in range(1, X):
                total = total + from_x_end[w][i - 1, :, both].astype(f32)
            half_out[w][:, both] = total
        there = outs[w].at[:, pl.ds(pl.multiple_of(p.c * 4 * unit(w), 128), 4 * unit(w))]
        push(half_out[w], there, core_sem.at[w], p.sibling())
        pltpu.make_async_copy(half_out[w], there, out_sem.at[w]).start()
    def s6(w):
        arrived(half_out[w], core_sem.at[w])
        arrived(half_out[w], out_sem.at[w])
    def t0():
        push(small, sm_core, sm_sem.at[0], p.sibling())
    def t1():
        arrived(sm_core, sm_sem.at[0])
        sm_x[p.x] = small[...] + sm_core[...]
        for i in range(1, X):
            push(sm_x.at[p.x], sm_x.at[p.x], smx_sem.at[i - 1], p.across(i))
    def t2():
        for i in range(1, X):
            arrived(sm_x.at[lax.rem(p.x + X - i, X)], smx_sem.at[i - 1])
        total = sm_x[0]
        for i in range(1, X): total = total + sm_x[i]
        sm_sum[...] = total
        for j in range(1, L):
            for k in range(H):
                h = lax.rem(p.h + k, H)
                push(sm_sum.at[shard(k, j)], sm_lo.at[j - 1, h], smlo_sem.at[j - 1, k], p.lo(j))
    def t3():
        for k in range(H):
            h = lax.rem(p.h + k, H)
            f = h * L + p.l
            total = sm_sum[f]
            for j in range(1, L):
                arrived(sm_lo.at[j - 1, h], smlo_sem.at[j - 1, k])
                total = total + sm_lo[j - 1, h]
            sm_core[f] = total
            if k > 0:
                push(sm_core.at[f], sm_hi.at[k - 1], smhi_sem.at[k - 1], p.hi(k))
    def t4():
        total = sm_core[p.f]
        for k in range(1, H):
            arrived(sm_hi.at[k - 1], smhi_sem.at[k - 1])
            total = total + sm_hi[k - 1]
        small_out[...] = total
    s1(0)
    stages = [s2, s3, s4, s5]
    for t in range(n + 3):
        for d, stage in enumerate(stages):
            if 0 <= t - d < n: stage(t - d)
            if d == 0 and t + 1 < n: s1(t + 1)
        if t == 0: t0()
        if t == 1: t1()
        if t == 2: t2()
        if t == 3: t3()
        if t == 4: t4()
    for w in range(n): s6(w)
    for cp in sent: cp.wait_send()

def reduce_all(parts, small):
    F, S, H, L, X = geometry()
    n = len(parts)
    width = 5 - X
    V = pltpu.VMEM
    def each(shape_of, dt):
        return [V(shape_of(a.shape[1], a.shape[2] // 4), dt) for a in parts]
    D = pltpu.SemaphoreType.DMA
    lead = max(X - 1, 1)
    res = pl.pallas_call(
        functools.partial(rs_kernel, n),
        out_shape=[jax.ShapeDtypeStruct((a.shape[1], 2 * a.shape[2]), f32) for a in parts] + [jax.ShapeDtypeStruct(small.shape[1:], f32)],
        in_specs=[pl.BlockSpec(memory_space=pl.ANY)] * n + [pl.BlockSpec(memory_space=pltpu.VMEM)],
        out_specs=[pl.BlockSpec(memory_space=pl.ANY)] * n + [pl.BlockSpec(memory_space=pltpu.VMEM)],
        scratch_shapes=[V(a.shape, bf16) for a in parts] + each(lambda r, u: (lead, F, r, u), bf16) + each(lambda r, u: (L - 1, H, r, width * u), bf16)
          + each(lambda r, u: (H - 1, r, width * u), bf16) + each(lambda r, u: (r, 4 * u), bf16) + each(lambda r, u: (lead, r, 4 * u), bf16)
          + each(lambda r, u: (r, 4 * u), f32)
          + [V(small.shape, f32), V((X,) + small.shape, f32), V(small.shape, f32), V((L - 1, H) + small.shape[1:], f32), V((H - 1,) + small.shape[1:], f32)]
          + [D((n,)), D((1,)), D((n, lead, F)), D((n, L - 1, H)), D((n, H - 1)), D((n, lead)), D((n,)), D((n,)), D((1,)), D((lead,)), D((L - 1, H)), D((H - 1,))],
        compiler_params=pltpu.CompilerParams(collective_id=2, has_side_effects=True, vmem_limit_bytes=60 * 2**20),
    )(*parts, small)
    return res[:n], res[n]


def layer_norm(values, gain_vec, shift):
    centre = values - jnp.mean(values, axis=-1, keepdims=True)
    spread = jnp.mean(centre * centre, axis=-1, keepdims=True)
    return centre * lax.rsqrt(spread + EPSILON) * gain_vec + shift


def gelu_tanh(values):
    return jax.nn.gelu(values, approximate=True)


def block_scores(query_rows, keys_all, block_start, key_block):
    block_rows = query_rows.shape[0]
    scores = jnp.einsum(
        "qhd,khd->hqk", query_rows, keys_all, preferred_element_type=jnp.float32
    ) * HD ** (-0.5)
    query_block = (block_start + jnp.arange(block_rows, dtype=jnp.int32)) // BLK
    allowed = key_block[None, :] <= query_block[:, None]
    return jnp.where(allowed[None], scores, -jnp.inf)


def attend_forward(queries, keys_all, values_all):
    length = queries.shape[0]
    block_rows = min(512, length)
    key_block = jnp.arange(length, dtype=jnp.int32) // BLK

    def one_block(block_start):
        query_rows = lax.dynamic_slice_in_dim(queries, block_start, block_rows, 0)
        scores = block_scores(query_rows, keys_all, block_start, key_block)
        largest = jnp.max(scores, axis=-1, keepdims=True)
        weights = jnp.exp(scores - largest)
        row_total = jnp.sum(weights, axis=-1, keepdims=True)
        soft_probs = (weights / row_total).astype(jnp.bfloat16)
        mixed_block = jnp.einsum(
            "hqk,khd->qhd", soft_probs, values_all, preferred_element_type=jnp.float32
        )
        return (mixed_block.astype(jnp.bfloat16), (largest + jnp.log(row_total))[..., 0])

    starts = jnp.arange(length // block_rows, dtype=jnp.int32) * block_rows
    mixed_blocks, log_total = lax.map(one_block, starts)
    return (mixed_blocks.reshape(length, -1), log_total)


def attend_backward(queries, keys_all, values_all, log_total, grad_mixed):
    length = queries.shape[0]
    block_rows = min(512, length)
    key_block = jnp.arange(length, dtype=jnp.int32) // BLK

    def one_block(running, block_index):
        grad_keys, grad_values = running
        block_start = block_index * block_rows
        query_rows = lax.dynamic_slice_in_dim(queries, block_start, block_rows, 0)
        grad_rows = lax.dynamic_slice_in_dim(grad_mixed, block_start, block_rows, 0)
        scores = block_scores(query_rows, keys_all, block_start, key_block)
        soft_probs = jnp.exp(scores - log_total[block_index][..., None])
        grad_probs = jnp.einsum(
            "qhd,khd->hqk", grad_rows, values_all, preferred_element_type=jnp.float32
        )
        inner_sum = jnp.sum(soft_probs * grad_probs, axis=-1, keepdims=True)
        grad_scores = (soft_probs * (grad_probs - inner_sum)).astype(jnp.bfloat16)
        grad_query = jnp.einsum(
            "hqk,khd->qhd", grad_scores, keys_all, preferred_element_type=jnp.float32
        ) * HD ** (-0.5)
        grad_keys = grad_keys + jnp.einsum(
            "hqk,qhd->khd", grad_scores, query_rows, preferred_element_type=jnp.float32
        ) * HD ** (-0.5)
        grad_values = grad_values + jnp.einsum(
            "hqk,qhd->khd",
            soft_probs.astype(jnp.bfloat16),
            grad_rows,
            preferred_element_type=jnp.float32,
        )
        return ((grad_keys, grad_values), grad_query)

    zero_keys = jnp.zeros(keys_all.shape, jnp.float32)
    block_ids = jnp.arange(length // block_rows, dtype=jnp.int32)
    (grad_keys, grad_values), grad_queries = lax.scan(one_block, (zero_keys, zero_keys), block_ids)
    return (
        grad_queries.reshape(length, -1),
        grad_keys.reshape(length, -1),
        grad_values.reshape(length, -1),
    )


def on_device(
    tokens, cotangent, ln1_gain, ln1_bias, w_qkv, b_qv, w_out, b_out,
    ln2_gain, ln2_bias, w_fc, b_fc, w_proj, b_proj,
):
    F, S, H, L, X = geometry()
    row_count, D = tokens.shape
    vectors = [ln1_gain, ln1_bias, b_qv, b_out, ln2_gain, ln2_bias, b_fc, b_proj]
    sizes = [v.shape[0] for v in vectors]
    flat = jnp.concatenate(vectors)
    small_rows = -(-flat.shape[0] // 2048) * 16
    flat = jnp.pad(flat, (0, small_rows * 128 - flat.shape[0])).reshape(small_rows, 128)
    weight_qkv, weight_out, weight_fc, weight_proj, smalls = gather_all(
        [w_qkv, w_out, w_fc, w_proj], flat
    )
    weight_qkv, weight_out, weight_fc, weight_proj = (
        a.reshape(-1, a.shape[-1]) for a in (weight_qkv, weight_out, weight_fc, weight_proj)
    )
    smalls = smalls.reshape(F, -1).astype(f32)
    whole_vectors, at = [], 0
    for size in sizes:
        whole_vectors.append(smalls[:, at : at + size].reshape(-1))
        at += size
    gain_one, shift_one, bias_qv, bias_out, gain_two, shift_two, bias_fc, bias_proj = whole_vectors
    cell_count = row_count * D * S * F
    inputs = tokens.astype(f32)
    sum_input = jnp.sum(inputs * inputs)
    normed_one = layer_norm(inputs, gain_one, shift_one).astype(bf16)
    bias_full = jnp.concatenate([bias_qv[:D], jnp.zeros((D,), f32), bias_qv[D:]])
    projected = (
        jnp.dot(normed_one, weight_qkv, preferred_element_type=f32) + bias_full
    ).astype(bf16)
    by_heads = lax.all_to_all(
        projected.reshape(row_count, 3, D), "seq", split_axis=2, concat_axis=0, tiled=True
    )
    length = by_heads.shape[0]
    head_count = by_heads.shape[2] // HD
    queries = by_heads[:, 0].reshape(length, head_count, HD)
    keys_all = by_heads[:, 1].reshape(length, head_count, HD)
    values_all = by_heads[:, 2].reshape(length, head_count, HD)
    mixed_heads, log_total = attend_forward(queries, keys_all, values_all)
    mixed_tokens = lax.all_to_all(mixed_heads, "seq", split_axis=0, concat_axis=1, tiled=True)
    middle = inputs + jnp.dot(mixed_tokens, weight_out, preferred_element_type=f32) + bias_out
    sum_middle = jnp.sum(middle * middle)
    normed_two = layer_norm(middle, gain_two, shift_two).astype(bf16)
    before = jnp.dot(normed_two, weight_fc, preferred_element_type=f32) + bias_fc
    activated, gelu_pull = jax.vjp(gelu_tanh, before)
    activated = activated.astype(bf16)
    feed_out = jnp.dot(activated, weight_proj, preferred_element_type=f32) + bias_proj
    stream = middle + feed_out
    sum_stream = jnp.sum(stream * stream)
    output = stream.astype(bf16)
    grad_out = cotangent.astype(f32)
    grad_bias_proj = jnp.sum(grad_out, axis=0)
    grad_act = jnp.einsum("td,fd->tf", cotangent, weight_proj, preferred_element_type=f32)
    grad_before = gelu_pull(grad_act)[0].astype(bf16)
    grad_bias_fc = jnp.sum(grad_before, axis=0, dtype=f32)
    grad_normed_two = jnp.einsum("tf,df->td", grad_before, weight_fc, preferred_element_type=f32)
    _, pull_two = jax.vjp(layer_norm, middle, gain_two, shift_two)
    grad_mid_norm, grad_gain_two, grad_shift_two = pull_two(grad_normed_two)
    grad_middle = grad_out + grad_mid_norm
    grad_branch = grad_middle.astype(bf16)
    grad_bias_out = jnp.sum(grad_branch, axis=0, dtype=f32)
    grad_mixed = jnp.einsum(
        "td,id->ti", grad_branch, weight_out, preferred_element_type=f32
    ).astype(bf16)
    grad_heads = lax.all_to_all(grad_mixed, "seq", split_axis=1, concat_axis=0, tiled=True)
    grad_queries, grad_keys, grad_values = attend_backward(
        queries, keys_all, values_all, log_total, grad_heads.reshape(length, head_count, HD)
    )
    stacked = jnp.stack([grad_queries, grad_keys, grad_values], axis=1).astype(bf16)
    grad_projected = lax.all_to_all(
        stacked, "seq", split_axis=0, concat_axis=2, tiled=True
    ).reshape(row_count, 3 * D)
    grad_bias_qv = jnp.concatenate(
        [
            jnp.sum(grad_projected[:, :D], axis=0, dtype=f32),
            jnp.sum(grad_projected[:, 2 * D :], axis=0, dtype=f32),
        ]
    )
    grad_normed_one = jnp.einsum(
        "te,de->td", grad_projected, weight_qkv, preferred_element_type=f32
    )
    _, pull_one = jax.vjp(layer_norm, inputs, gain_one, shift_one)
    grad_in_norm, grad_gain_one, grad_shift_one = pull_one(grad_normed_one)
    grad_tokens = (grad_middle + grad_in_norm).astype(bf16)

    core = lax.axis_index("seq") % 2
    pairs = [(s, s + 1 - 2 * (s % 2)) for s in range(S)]

    def half_grad(rows, columns):
        wide = columns.shape[1] // 2
        mine = lax.dynamic_slice_in_dim(columns, core * wide, wide, 1)
        theirs = lax.dynamic_slice_in_dim(columns, (1 - core) * wide, wide, 1)
        both_rows = jnp.concatenate([rows, lax.ppermute(rows, "seq", pairs)], axis=0)
        both_columns = jnp.concatenate([mine, lax.ppermute(theirs, "seq", pairs)], axis=0)
        grad = jnp.einsum("ta,tb->ab", both_rows, both_columns, preferred_element_type=f32)
        return grad.astype(bf16).reshape(F, -1, wide)

    halves = [
        half_grad(activated, cotangent),
        half_grad(normed_two, grad_before),
        half_grad(mixed_tokens, grad_branch),
        half_grad(normed_one, grad_projected),
    ]
    small_grads = [
        g.reshape(F, -1)
        for g in (
            grad_gain_one, grad_shift_one, grad_bias_qv, grad_bias_out,
            grad_gain_two, grad_shift_two, grad_bias_fc, grad_bias_proj,
        )
    ]
    sums = jnp.stack([sum_input, sum_middle, sum_stream])
    width = sum(sizes) + 3
    total_rows = -(-width // 1024) * 8
    small_grads = jnp.concatenate(
        small_grads
        + [jnp.broadcast_to(sums, (F, 3)), jnp.zeros((F, total_rows * 128 - width), f32)],
        axis=1,
    ).reshape(F, total_rows, 128)
    (grad_w_proj, grad_w_fc, grad_w_out, grad_w_qkv), reduced = reduce_all(halves, small_grads)
    reduced = reduced.reshape(-1)
    vectors_out, at = [], 0
    for size in sizes:
        vectors_out.append(reduced[at : at + size])
        at += size
    rms_values = jnp.sqrt(reduced[at : at + 3] / float(cell_count))
    return (
        output, grad_tokens, vectors_out[0], vectors_out[1], grad_w_qkv, vectors_out[2],
        grad_w_out, vectors_out[3], vectors_out[4], vectors_out[5], grad_w_fc, vectors_out[6],
        grad_w_proj, vectors_out[7], rms_values,
    )


def solution(mesh):
    in_specs = (
        P(("fsdp", "seq"), None),
        P(("fsdp", "seq"), None),
        P("fsdp"),
        P("fsdp"),
        P("fsdp", None),
        P("fsdp"),
        P("fsdp", None),
        P("fsdp"),
        P("fsdp"),
        P("fsdp"),
        P("fsdp", None),
        P("fsdp"),
        P("fsdp", None),
        P("fsdp"),
    )
    out_specs = (
        P(("fsdp", "seq"), None),
        P(("fsdp", "seq"), None),
        P("fsdp"),
        P("fsdp"),
        P("fsdp", None),
        P("fsdp"),
        P("fsdp", None),
        P("fsdp"),
        P("fsdp"),
        P("fsdp"),
        P("fsdp", None),
        P("fsdp"),
        P("fsdp", None),
        P("fsdp"),
        P(),
    )
    return jax.shard_map(
        on_device, mesh=mesh, in_specs=in_specs, out_specs=out_specs, check_vma=False
    )
```

```python
import functools

import jax
import jax.numpy as jnp
from jax import lax
from jax.experimental import pallas as pl
from jax.experimental.pallas import tpu as pltpu
from jax.sharding import PartitionSpec as P

BLK = 256
HD = 64
EPSILON = 1e-05
MESH = pl.DeviceIdType.MESH
f32, bf16 = jnp.float32, jnp.bfloat16

def geometry():
    F, S = lax.axis_size("fsdp"), lax.axis_size("seq")
    return F, S, 4, F // 4, S // 2


class Place:
    def __init__(self):
        self.F, self.S, self.H, self.L, self.X = geometry()
        self.f, self.s = lax.axis_index("fsdp"), lax.axis_index("seq")
        self.h, self.l = self.f // self.L, self.f % self.L
        self.x, self.c = self.s // 2, self.s % 2

    def shard(self, k, j):
        return lax.rem(self.h + self.H - k, self.H) * self.L + lax.rem(self.l + self.L - j, self.L)

    def hi(self, k):
        return (lax.rem(self.h + k, self.H) * self.L + self.l, self.s)

    def lo(self, j):
        return (self.h * self.L + lax.rem(self.l + j, self.L), self.s)

    def across(self, i):
        return (self.f, lax.rem(self.x + i, self.X) * 2 + self.c)

    def sibling(self):
        return (self.f, self.x * 2 + 1 - self.c)

    def everyone(self):
        return (
            [self.hi(k) for k in range(1, self.H)]
            + [self.lo(j) for j in range(1, self.L)]
            + [(self.f, lax.rem(self.s + i, self.S)) for i in range(1, self.S)]
        )


def greet(place):
    barrier = pltpu.get_barrier_semaphore()
    peers = place.everyone()
    for peer in peers:
        pl.semaphore_signal(barrier, inc=1, device_id=peer, device_id_type=MESH)
    pl.semaphore_wait(barrier, len(peers))


def vector(ref, places, name):
    at, size = places[name]
    parts = []
    for f in range(ref.shape[0]):
        pos = at
        while pos < at + size:
            row, lane = divmod(pos, 128)
            count = min(128 - lane, at + size - pos)
            parts.append(ref[f, row : row + 1, lane : lane + count])
            pos += count
    return jnp.concatenate(parts, axis=1)


def normalised(x):
    centre = x - jnp.mean(x, axis=-1, keepdims=True)
    return centre * lax.rsqrt(jnp.mean(centre * centre, axis=-1, keepdims=True) + EPSILON)


def gelu_and_slope(u):
    root = 0.7978845608028654
    square = u * u
    t = jnp.tanh(u * (root + root * 0.044715 * square))
    half = 0.5 * (1.0 + t)
    return u * half, half + u * (0.5 * (1.0 - t * t)) * (root + 3.0 * root * 0.044715 * square)


NT = (((1,), (1,)), ((), ()))
TN = (((0,), (0,)), ((), ()))


def head_lanes(shape, parity):
    lane = lax.broadcasted_iota(jnp.int32, shape, 1)
    return (lane // HD) == parity

def pick(rows, parity):
    return jnp.where(head_lanes(rows.shape, parity), rows, jnp.zeros_like(rows))

def turn(rows):
    return rows.astype(f32).T

def attend_block(i, wide, qkv, vT, scores, oT, lse):
    rows = pl.ds(i * BLK, BLK)
    @pl.loop(0, wide // HD)
    def _(h):
        pair = pl.multiple_of(h // 2 * 128, 128)
        q = pick(qkv[rows, pl.ds(pair, 128)], h % 2) * jnp.asarray(HD ** -0.5, bf16)
        top = jnp.full((8, BLK), -jnp.inf, f32)
        for j in range(i + 1):
            k = qkv[pl.ds(j * BLK, BLK), pl.ds(pl.multiple_of(wide + pair, 128), 128)]
            s = lax.dot_general(k, q, NT, preferred_element_type=f32)
            scores[pl.ds(j * BLK, BLK), :] = s
            top = jnp.maximum(top, jnp.max(s.reshape(BLK // 8, 8, BLK), axis=0))
        top = jnp.max(top, axis=0, keepdims=True)
        total = jnp.zeros((8, BLK), f32)
        out = jnp.zeros((HD, BLK), f32)
        for j in range(i + 1):
            p = jnp.exp(scores[pl.ds(j * BLK, BLK), :] - top)
            total = total + jnp.sum(p.reshape(BLK // 8, 8, BLK), axis=0)
            out = out + jnp.dot(vT[pl.ds(pl.multiple_of(h * HD, HD), HD), pl.ds(j * BLK, BLK)], p.astype(bf16), preferred_element_type=f32)
        total = jnp.sum(total, axis=0, keepdims=True)
        oT[pl.ds(pl.multiple_of(h * HD, HD), HD), :] = out * (1.0 / total)
        lse[pl.ds(h, 1), rows] = top + jnp.log(total)

def attend_back_block(i, wide, qkv, grad, kT, lse, delta, dqT, dk, dv):
    rows = pl.ds(i * BLK, BLK)
    @pl.loop(0, wide // HD)
    def _(h):
        pair = pl.multiple_of(h // 2 * 128, 128)
        here = pl.ds(pair, 128)
        q = pick(qkv[rows, here], h % 2) * jnp.asarray(HD ** -0.5, bf16)
        g = pick(grad[rows, here], h % 2)
        low = lse[pl.ds(h, 1), rows]
        mean = delta[pl.ds(h, 1), rows]
        out = jnp.zeros((HD, BLK), f32)
        for j in range(i + 1):
            keys = pl.ds(j * BLK, BLK)
            k = qkv[keys, pl.ds(pl.multiple_of(wide + pair, 128), 128)]
            v = qkv[keys, pl.ds(pl.multiple_of(2 * wide + pair, 128), 128)]
            p = jnp.exp(lax.dot_general(k, q, NT, preferred_element_type=f32) - low)
            dp = lax.dot_general(v, g, NT, preferred_element_type=f32)
            ds = (p * (dp - mean)).astype(bf16)
            dvj = jnp.dot(p.astype(bf16), g, preferred_element_type=f32)
            dkj = jnp.dot(ds, q, preferred_element_type=f32)
            dv[keys, here] += dvj
            dk[keys, here] += dkj
            out = out + jnp.dot(kT[pl.ds(pl.multiple_of(h * HD, HD), HD), keys], ds, preferred_element_type=f32)
        dqT[pl.ds(pl.multiple_of(h * HD, HD), HD), :] = out * HD ** -0.5


def forward_kernel(places, *refs):
    refs = list(refs)

    def take(count):
        got = refs[:count]
        del refs[:count]
        return got

    tokens, small = take(2)
    shards = take(4)
    big_outs = take(4)
    (small_out, one_out, qkv_out, lse_out, heads_out, mixed_out, middle_out, two_out, act_out,
     slope_out, result_out, stats_out) = take(12)
    wholes = take(4)
    (smalls, smalls_f, one, split, qkv, vT, scores, oT, lse, heads, mixed, middle, two, act, slope,
     result, stats, vectors, wide_bias) = take(19)
    (own_sem, send_sem, save_sem, hi_sem, lo_sem, x_sem, core_sem, sm_hi_sem, sm_lo_sem, there_sem,
     back_sem) = refs
    p = Place()
    S, H, L, X, F = p.S, p.H, p.L, p.X, p.F
    rows_here, D = tokens.shape
    wide = D // S
    sent, saved = [], []

    def push(src, dst, sem, peer):
        cp = pltpu.make_async_remote_copy(
            src_ref=src, dst_ref=dst, send_sem=send_sem.at[0], recv_sem=sem, device_id=peer,
            device_id_type=MESH,
        )
        cp.start()
        sent.append(cp)

    def arrived(dst, sem):
        pltpu.make_async_copy(dst, dst, sem).wait()

    def save(src, dst):
        cp = pltpu.make_async_copy(src, dst, save_sem.at[len(saved)])
        cp.start()
        saved.append(cp)

    own = []
    for w in range(4):
        own.append(pltpu.make_async_copy(shards[w], wholes[w].at[p.f], own_sem.at[w]))
    own.append(pltpu.make_async_copy(small, smalls.at[p.f], own_sem.at[4]))
    for cp in own:
        cp.start()
    greet(p)

    width = 5 - X
    step = 3 // (X - 1) if X > 1 else 0

    def cols(w, start, count):
        C = shards[w].shape[-1]
        return pl.ds(pl.multiple_of(p.c * (C // 2) + start * (C // 8), 128), count * (C // 8))

    def half(w, core):
        C = shards[w].shape[-1]
        return pl.ds(pl.multiple_of(core * (C // 2), 128), C // 2)

    def start_hi(w):
        mine = cols(w, p.x, width)
        for k in range(1, H):
            push(shards[w].at[:, mine], wholes[w].at[p.f, :, mine], hi_sem.at[w, k - 1], p.hi(k))
        for j in range(1, L):
            push(shards[w].at[:, mine], wholes[w].at[p.f, :, mine], lo_sem.at[w, j - 1, 0], p.lo(j))

    def over_x(w, j, k):
        piece = wholes[w].at[p.shard(k, j), :, cols(w, p.x * step, 1)]
        for i in range(1, X):
            push(piece, piece, x_sem.at[w, i - 1, j * H + k - 1], p.across(i))

    def finish_hi(w, k):
        piece = wholes[w].at[p.shard(k, 0), :, cols(w, p.x, width)]
        arrived(piece, hi_sem.at[w, k - 1])
        for j in range(1, L):
            push(piece, piece, lo_sem.at[w, j - 1, k], p.lo(j))
        over_x(w, 0, k)

    def finish_lo(w, k):
        for j in range(1, L):
            arrived(wholes[w].at[p.shard(k, j), :, cols(w, p.x, width)], lo_sem.at[w, j - 1, k])
            over_x(w, j, k)

    def finish_x(w, j, k):
        for i in range(1, X):
            theirs = lax.rem(p.x + X - i, X) * step
            arrived(wholes[w].at[p.shard(k, j), :, cols(w, theirs, 1)], x_sem.at[w, i - 1, j * H + k - 1])
        piece = wholes[w].at[p.shard(k, j), :, half(w, p.c)]
        push(piece, piece, core_sem.at[w, j * H + k - 1], p.sibling())

    def finish_core(w):
        for j in range(L):
            for k in range(H):
                if (j, k) != (0, 0):
                    arrived(wholes[w].at[p.shard(k, j), :, half(w, 1 - p.c)], core_sem.at[w, j * H + k - 1])
        own[w].wait()
        save(wholes[w], big_outs[w])

    def queue_of(w):
        todo = []
        for k in range(1, H):
            todo.append(functools.partial(finish_hi, w, k))
            todo.append(functools.partial(finish_lo, w, k - 1))
        todo.append(functools.partial(finish_lo, w, H - 1))
        for k in range(1, H):
            todo.append(functools.partial(finish_x, w, 0, k))
        for j in range(1, L):
            for k in range(H):
                todo.append(functools.partial(finish_x, w, j, k))
        todo.append(functools.partial(finish_core, w))
        return todo

    def run(todo, count):
        for _ in range(min(count, len(todo))):
            todo.pop(0)()

    for k in range(1, H):
        push(small, smalls.at[p.f], sm_hi_sem.at[k - 1], p.hi(k))
    for j in range(1, L):
        push(small, smalls.at[p.f], sm_lo_sem.at[j - 1, 0], p.lo(j))
    start_hi(0)
    for k in range(1, H):
        piece = smalls.at[p.shard(k, 0)]
        arrived(piece, sm_hi_sem.at[k - 1])
        for j in range(1, L):
            push(piece, piece, sm_lo_sem.at[j - 1, k], p.lo(j))
    for j in range(1, L):
        for k in range(H):
            arrived(smalls.at[p.shard(k, j)], sm_lo_sem.at[j - 1, k])
    own[4].wait()
    smalls_f[...] = smalls[...].astype(f32)
    save(smalls, small_out)
    vec = functools.partial(vector, smalls_f, places)

    chunk = 128
    stats[...] = jnp.zeros_like(stats)
    gain, shift = vec("ln1_gain"), vec("ln1_bias")

    @pl.loop(0, rows_here // chunk)
    def _(t):
        at = pl.ds(pl.multiple_of(t * chunk, chunk), chunk)
        x = tokens[at, :].astype(f32)
        stats[0:1, :] += jnp.sum(x * x, axis=0, keepdims=True)
        one[at, :] = (normalised(x) * gain + shift).astype(bf16)

    save(one, one_out)
    first, second, third, fourth = (queue_of(w) for w in range(4))
    run(first, 1)
    start_hi(1)
    run(first, 4)
    start_hi(2)
    run(first, len(first))

    bias_qv = vec("b_qv")

    def project(kind, target):
        at = pl.multiple_of(kind * D + target * wide, 128)
        w = wholes[0][:, :, pl.ds(at, wide)].reshape(D, wide)
        return jnp.dot(one[...], w, preferred_element_type=f32)

    vectors[0:1, :] = bias_qv[:, :D]
    vectors[1:2, :] = bias_qv[:, D:]

    def heads_of(target):
        lanes = pl.ds(pl.multiple_of(target * wide, 128), wide)
        return [
            (project(0, target) + vectors[0:1, lanes]).astype(bf16),
            project(1, target).astype(bf16),
            (project(2, target) + vectors[1:2, lanes]).astype(bf16),
        ]

    mine = pl.ds(pl.multiple_of(p.s * rows_here, 128), rows_here)
    for i in list(range(1, S)) + [0]:
        target = lax.rem(p.s + i, S)
        for kind, values in enumerate(heads_of(target)):
            if i == 0:
                qkv[mine, kind * wide : (kind + 1) * wide] = values
            else:
                split[i - 1, :, kind * wide : (kind + 1) * wide] = values
        if i:
            push(split.at[i - 1], qkv.at[mine, :], there_sem.at[i - 1], (p.f, target))
    run(second, 7)
    run(third, 1)
    run(second, len(second))
    run(third, 3)
    start_hi(3)
    run(third, 1)
    for i in range(1, S):
        source = lax.rem(p.s + S - i, S)
        arrived(qkv.at[pl.ds(pl.multiple_of(source * rows_here, 128), rows_here), :], there_sem.at[i - 1])
    save(qkv, qkv_out)

    length = qkv.shape[0]
    blocks = length // BLK
    for b in range(blocks):
        at = pl.ds(b * BLK, BLK)
        vT[:, at] = turn(qkv[at, 2 * wide :]).astype(bf16)
    lse[...] = jnp.zeros_like(lse)
    sent_back = 0
    for i in range(blocks):
        attend_block(i, wide, qkv, vT, scores, oT, lse)
        heads[pl.ds(i * BLK, BLK), :] = turn(oT[...]).astype(bf16)
        while (sent_back + 1) * rows_here <= (i + 1) * BLK:
            rows = pl.ds(sent_back * rows_here, rows_here)
            lanes = pl.ds(pl.multiple_of(p.s * wide, 128), wide)

            @pl.when(p.s != sent_back)
            def _():
                pltpu.make_async_remote_copy(
                    src_ref=heads.at[rows], dst_ref=mixed.at[:, lanes], send_sem=send_sem.at[1],
                    recv_sem=back_sem.at[p.s], device_id=(p.f, jnp.int32(sent_back)),
                    device_id_type=MESH,
                ).start()

            @pl.when(p.s == sent_back)
            def _():
                mixed[:, lanes] = heads[rows, :]

            sent_back += 1
        run(third, 2)
    save(heads, heads_out)
    save(lse, lse_out)
    run(third, 3)
    for i in range(1, S):
        source = lax.rem(p.s + S - i, S)
        arrived(mixed.at[:, pl.ds(pl.multiple_of(source * wide, 128), wide)], back_sem.at[source])
    save(mixed, mixed_out)

    tile = 256
    vectors[0:1, :] = vec("b_out")

    @pl.loop(0, D // tile)
    def _(t):
        at = pl.ds(pl.multiple_of(t * tile, tile), tile)
        w = wholes[1][:, :, at].reshape(D, tile)
        branch = jnp.dot(mixed[...], w, preferred_element_type=f32) + vectors[0:1, at]
        middle[:, at] = tokens[:, at].astype(f32) + branch

    save(middle, middle_out)
    gain_two, shift_two = vec("ln2_gain"), vec("ln2_bias")

    @pl.loop(0, rows_here // chunk)
    def _(t):
        at = pl.ds(pl.multiple_of(t * chunk, chunk), chunk)
        x = middle[at, :]
        stats[1:2, :] += jnp.sum(x * x, axis=0, keepdims=True)
        two[at, :] = (normalised(x) * gain_two + shift_two).astype(bf16)

    save(two, two_out)
    run(third, len(third))
    run(fourth, 2)
    wide_bias[0:1, :] = vec("b_fc")

    FF = act.shape[1]

    @pl.loop(0, FF // tile)
    def _(t):
        at = pl.ds(pl.multiple_of(t * tile, tile), tile)
        w = wholes[2][:, :, at].reshape(D, tile)
        u = jnp.dot(two[...], w, preferred_element_type=f32) + wide_bias[0:1, at]
        act_rows, slope_rows = gelu_and_slope(u)
        act[:, at] = act_rows.astype(bf16)
        slope[:, at] = slope_rows.astype(bf16)

    save(act, act_out)
    save(slope, slope_out)
    run(fourth, len(fourth))
    vectors[0:1, :] = vec("b_proj")

    @pl.loop(0, D // tile)
    def _(t):
        at = pl.ds(pl.multiple_of(t * tile, tile), tile)
        w = wholes[3][:, :, at].reshape(FF, tile)
        stream = middle[:, at] + (jnp.dot(act[...], w, preferred_element_type=f32) + vectors[0:1, at])
        stats[2:3, at] = jnp.sum(stream * stream, axis=0, keepdims=True)
        result[:, at] = stream.astype(bf16)

    save(result, result_out)
    save(stats, stats_out)
    for cp in sent:
        cp.wait_send()
    for i in range(1, S):
        arrived(heads.at[pl.ds(0, rows_here)], send_sem.at[1])
    for cp in saved:
        cp.wait()


def forward(tokens, packed, places, shards):
    F, S, H, L, X = geometry()
    rows_here, D = tokens.shape
    wide, length, FF = D // S, rows_here * S, shards[2].shape[1]
    heads = max(8, wide // HD)
    lead = max(X - 1, 1)
    any_spec = pl.BlockSpec(memory_space=pl.ANY)
    V, D_SEM = pltpu.VMEM, pltpu.SemaphoreType.DMA
    shaped = jax.ShapeDtypeStruct
    wholes = [(F,) + a.shape for a in shards]
    outs = [shaped(s, bf16) for s in wholes] + [
        shaped((F,) + packed.shape, bf16),
        shaped((rows_here, D), bf16),
        shaped((length, 3 * wide), bf16),
        shaped((heads, length), f32),
        shaped((length, wide), bf16),
        shaped((rows_here, D), bf16),
        shaped((rows_here, D), f32),
        shaped((rows_here, D), bf16),
        shaped((rows_here, FF), bf16),
        shaped((rows_here, FF), bf16),
        shaped((rows_here, D), bf16),
        shaped((8, D), f32),
    ]
    return pl.pallas_call(
        functools.partial(forward_kernel, places),
        out_shape=outs,
        in_specs=[pl.BlockSpec(memory_space=pltpu.VMEM)] + [any_spec] * 5,
        out_specs=[any_spec] * len(outs),
        scratch_shapes=[V(s, bf16) for s in wholes]
        + [
            V((F,) + packed.shape, bf16),
            V((F,) + packed.shape, f32),
            V((rows_here, D), bf16),
            V((S - 1, rows_here, 3 * wide), bf16),
            V((length, 3 * wide), bf16),
            V((wide, length), bf16),
            V((length, BLK), f32),
            V((wide, BLK), f32),
            V((heads, length), f32),
            V((length, wide), bf16),
            V((rows_here, D), bf16),
            V((rows_here, D), f32),
            V((rows_here, D), bf16),
            V((rows_here, FF), bf16),
            V((rows_here, FF), bf16),
            V((rows_here, D), bf16),
            V((8, D), f32),
            V((8, D), f32),
            V((8, FF), f32),
            D_SEM((5,)),
            D_SEM((2,)),
            D_SEM((len(outs),)),
            D_SEM((4, H - 1)),
            D_SEM((4, L - 1, H)),
            D_SEM((4, lead, F - 1)),
            D_SEM((4, F - 1)),
            D_SEM((H - 1,)),
            D_SEM((L - 1, H)),
            D_SEM((S - 1,)),
            D_SEM((S,)),
        ],
        compiler_params=pltpu.CompilerParams(
            collective_id=1, has_side_effects=True, vmem_limit_bytes=60 * 2**20
        ),
    )(tokens, packed, *shards)


def rs_kernel(n, *refs):
    given, small = refs[:n], refs[n]
    outs, small_out = refs[n + 1:2 * n + 1], refs[2 * n + 1]
    rest = list(refs[2 * n + 2:])
    def take(k):
        got = rest[:k]; del rest[:k]; return got
    parts, from_x, from_lo, from_hi, value, from_x_end, half_out = (take(n) for _ in range(7))
    sm_core, sm_x, sm_sum, sm_lo, sm_hi = take(5)
    load_sem, send_sem, x_sem, lo_sem, hi_sem, end_sem, out_sem, core_sem, sm_sem, smx_sem, smlo_sem, smhi_sem = rest
    loads = [pltpu.make_async_copy(given[w], parts[w], load_sem.at[w]) for w in range(n)]
    for load in loads: load.start()
    p = Place()
    greet(p)
    H, L, X = p.H, p.L, p.X
    width = 5 - X
    step = 3 // (X - 1) if X > 1 else 0
    sent = []
    def push(src, dst, sem, peer):
        cp = pltpu.make_async_remote_copy(src_ref=src, dst_ref=dst, send_sem=send_sem.at[0], recv_sem=sem, device_id=peer, device_id_type=MESH)
        cp.start(); sent.append(cp)
    def arrived(dst, sem):
        pltpu.make_async_copy(dst, dst, sem).wait()
    def unit(w): return parts[w].shape[-1] // 4
    def span(w, start, count):
        return pl.ds(pl.multiple_of(start * unit(w), 128), count * unit(w))
    def other_x(i): return lax.rem(p.x + i, X)
    def shard(k, j):
        return lax.rem(p.h + k, H) * L + lax.rem(p.l + j, L)
    def s1(w):
        loads[w].wait()
        for j in list(range(1, L)) + [0]:
            for k in range(H):
                for i in range(1, X):
                    f = shard(k, j)
                    push(parts[w].at[f, :, span(w, other_x(i) * step, 1)], from_x[w].at[i - 1, f], x_sem.at[w, i - 1, j * H + k], p.across(i))
    def add_x(w, k, j):
        f = shard(k, j)
        for i in range(1, X):
            arrived(from_x[w].at[i - 1, f], x_sem.at[w, i - 1, j * H + k])
        if X > 1:
            cols = span(w, p.x * step, 1)
            total = parts[w][f, :, cols].astype(f32)
            for i in range(1, X):
                total = total + from_x[w][i - 1, f].astype(f32)
            parts[w][f, :, cols] = total.astype(bf16)
    def s2(w):
        for j in range(1, L):
            for k in list(range(1, H)) + [0]:
                add_x(w, k, j)
                f = shard(k, j)
                push(parts[w].at[f, :, span(w, p.x, width)], from_lo[w].at[j - 1, lax.rem(p.h + k, H)], lo_sem.at[w, j - 1, k], p.lo(j))
    def s3(w):
        for k in list(range(1, H)) + [0]:
            add_x(w, k, 0)
            h = lax.rem(p.h + k, H)
            f = h * L + p.l
            cols = span(w, p.x, width)
            total = parts[w][f, :, cols].astype(f32)
            for j in range(1, L):
                arrived(from_lo[w].at[j - 1, h], lo_sem.at[w, j - 1, k])
                total = total + from_lo[w][j - 1, h].astype(f32)
            parts[w][f, :, cols] = total.astype(bf16)
            if k > 0:
                push(parts[w].at[f, :, cols], from_hi[w].at[k - 1], hi_sem.at[w, k - 1], p.hi(k))
    def s4(w):
        cols = span(w, p.x, width)
        total = parts[w][p.f, :, cols].astype(f32)
        for k in range(1, H):
            arrived(from_hi[w].at[k - 1], hi_sem.at[w, k - 1])
            total = total + from_hi[w][k - 1].astype(f32)
        value[w][:, cols] = total.astype(bf16)
        for i in range(1, X):
            push(value[w].at[:, cols], from_x_end[w].at[i - 1, :, cols], end_sem.at[w, i - 1], p.across(i))
    def s5(w):
        mine = span(w, p.x * step, 1)
        half_out[w][:, mine] = value[w][:, mine].astype(f32)
        for i in range(1, X):
            src = lax.rem(p.x + X - i, X)
            cols = span(w, src, width)
            arrived(from_x_end[w].at[i - 1, :, cols], end_sem.at[w, i - 1])
            theirs = span(w, src * step, 1)
            half_out[w][:, theirs] = from_x_end[w][i - 1, :, theirs].astype(f32)
        if X < 4:
            both = pl.ds(unit(w), (4 - X) * unit(w))
            total = value[w][:, both].astype(f32)
            for i in range(1, X):
                total = total + from_x_end[w][i - 1, :, both].astype(f32)
            half_out[w][:, both] = total
        there = outs[w].at[:, pl.ds(pl.multiple_of(p.c * 4 * unit(w), 128), 4 * unit(w))]
        push(half_out[w], there, core_sem.at[w], p.sibling())
        pltpu.make_async_copy(half_out[w], there, out_sem.at[w]).start()
    def s6(w):
        arrived(half_out[w], core_sem.at[w])
        arrived(half_out[w], out_sem.at[w])
    def t0():
        push(small, sm_core, sm_sem.at[0], p.sibling())
    def t1():
        arrived(sm_core, sm_sem.at[0])
        sm_x[p.x] = small[...] + sm_core[...]
        for i in range(1, X):
            push(sm_x.at[p.x], sm_x.at[p.x], smx_sem.at[i - 1], p.across(i))
    def t2():
        for i in range(1, X):
            arrived(sm_x.at[lax.rem(p.x + X - i, X)], smx_sem.at[i - 1])
        total = sm_x[0]
        for i in range(1, X): total = total + sm_x[i]
        sm_sum[...] = total
        for j in range(1, L):
            for k in range(H):
                h = lax.rem(p.h + k, H)
                push(sm_sum.at[shard(k, j)], sm_lo.at[j - 1, h], smlo_sem.at[j - 1, k], p.lo(j))
    def t3():
        for k in range(H):
            h = lax.rem(p.h + k, H)
            f = h * L + p.l
            total = sm_sum[f]
            for j in range(1, L):
                arrived(sm_lo.at[j - 1, h], smlo_sem.at[j - 1, k])
                total = total + sm_lo[j - 1, h]
            sm_core[f] = total
            if k > 0:
                push(sm_core.at[f], sm_hi.at[k - 1], smhi_sem.at[k - 1], p.hi(k))
    def t4():
        total = sm_core[p.f]
        for k in range(1, H):
            arrived(sm_hi.at[k - 1], smhi_sem.at[k - 1])
            total = total + sm_hi[k - 1]
        small_out[...] = total
    s1(0)
    stages = [s2, s3, s4, s5]
    for t in range(n + 3):
        for d, stage in enumerate(stages):
            if 0 <= t - d < n: stage(t - d)
            if d == 0 and t + 1 < n: s1(t + 1)
        if t == 0: t0()
        if t == 1: t1()
        if t == 2: t2()
        if t == 3: t3()
        if t == 4: t4()
    for w in range(n): s6(w)
    for cp in sent: cp.wait_send()

def reduce_all(parts, small):
    F, S, H, L, X = geometry()
    n = len(parts)
    width = 5 - X
    V = pltpu.VMEM
    def each(shape_of, dt):
        return [V(shape_of(a.shape[1], a.shape[2] // 4), dt) for a in parts]
    D = pltpu.SemaphoreType.DMA
    lead = max(X - 1, 1)
    res = pl.pallas_call(
        functools.partial(rs_kernel, n),
        out_shape=[jax.ShapeDtypeStruct((a.shape[1], 2 * a.shape[2]), f32) for a in parts] + [jax.ShapeDtypeStruct(small.shape[1:], f32)],
        in_specs=[pl.BlockSpec(memory_space=pl.ANY)] * n + [pl.BlockSpec(memory_space=pltpu.VMEM)],
        out_specs=[pl.BlockSpec(memory_space=pl.ANY)] * n + [pl.BlockSpec(memory_space=pltpu.VMEM)],
        scratch_shapes=[V(a.shape, bf16) for a in parts] + each(lambda r, u: (lead, F, r, u), bf16) + each(lambda r, u: (L - 1, H, r, width * u), bf16)
          + each(lambda r, u: (H - 1, r, width * u), bf16) + each(lambda r, u: (r, 4 * u), bf16) + each(lambda r, u: (lead, r, 4 * u), bf16)
          + each(lambda r, u: (r, 4 * u), f32)
          + [V(small.shape, f32), V((X,) + small.shape, f32), V(small.shape, f32), V((L - 1, H) + small.shape[1:], f32), V((H - 1,) + small.shape[1:], f32)]
          + [D((n,)), D((1,)), D((n, lead, F)), D((n, L - 1, H)), D((n, H - 1)), D((n, lead)), D((n,)), D((n,)), D((1,)), D((lead,)), D((L - 1, H)), D((H - 1,))],
        compiler_params=pltpu.CompilerParams(collective_id=2, has_side_effects=True, vmem_limit_bytes=60 * 2**20),
    )(*parts, small)
    return res[:n], res[n]


def attention_back(qkv, grad, heads_out, lse):
    length, wide = grad.shape

    def kernel(qkv, grad, mixed, lse, out, kT, delta, dqT, dk, dv):
        dk[...] = jnp.zeros_like(dk)
        dv[...] = jnp.zeros_like(dv)
        shape = (lse.shape[0], wide)
        chosen = lax.broadcasted_iota(jnp.int32, shape, 1) // HD == lax.broadcasted_iota(jnp.int32, shape, 0)
        chosen = jnp.where(chosen, 1.0, 0.0).astype(bf16)
        for b in range(length // BLK):
            at = pl.ds(b * BLK, BLK)
            kT[:, at] = turn(qkv[at, wide : 2 * wide]).astype(bf16)
            product = grad[at, :].astype(f32) * mixed[at, :].astype(f32)
            high = product.astype(bf16)
            low = (product - high.astype(f32)).astype(bf16)
            delta[:, at] = lax.dot_general(chosen, high, NT, preferred_element_type=f32) + lax.dot_general(
                chosen, low, NT, preferred_element_type=f32
            )
        for i in range(length // BLK):
            attend_back_block(i, wide, qkv, grad, kT, lse, delta, dqT, dk, dv)
            out[i * BLK : (i + 1) * BLK, 0:wide] = turn(dqT[...]).astype(bf16)
        out[:, wide : 2 * wide] = dk[...].astype(bf16)
        out[:, 2 * wide :] = dv[...].astype(bf16)

    V = pltpu.VMEM
    return pl.pallas_call(
        kernel,
        out_shape=jax.ShapeDtypeStruct((length, 3 * wide), bf16),
        scratch_shapes=[
            V((wide, length), bf16), V(lse.shape, f32), V((wide, BLK), f32), V((length, wide), f32),
            V((length, wide), f32),
        ],
        compiler_params=pltpu.CompilerParams(vmem_limit_bytes=48 * 2**20),
    )(qkv, grad, heads_out, lse)


def layer_norm(values, gain_vec, shift):
    centre = values - jnp.mean(values, axis=-1, keepdims=True)
    spread = jnp.mean(centre * centre, axis=-1, keepdims=True)
    return centre * lax.rsqrt(spread + EPSILON) * gain_vec + shift


def on_device(
    tokens, cotangent, ln1_gain, ln1_bias, w_qkv, b_qv, w_out, b_out,
    ln2_gain, ln2_bias, w_fc, b_fc, w_proj, b_proj,
):
    F, S, H, L, X = geometry()
    row_count, D = tokens.shape
    named = dict(
        b_fc=b_fc, b_qv=b_qv, ln1_gain=ln1_gain, ln1_bias=ln1_bias, b_out=b_out,
        ln2_gain=ln2_gain, ln2_bias=ln2_bias, b_proj=b_proj,
    )
    places, at = {}, 0
    for name, value in named.items():
        places[name] = (at, value.shape[0])
        at += value.shape[0]
    flat = jnp.concatenate(list(named.values()))
    small_rows = -(-at // 2048) * 16
    flat = jnp.pad(flat, (0, small_rows * 128 - at)).reshape(small_rows, 128)
    (weight_qkv, weight_out, weight_fc, weight_proj, smalls, normed_one, qkv, lse, heads_out,
     mixed_tokens, middle, normed_two, activated, slope, output, stats) = forward(
        tokens, flat, places, [w_qkv, w_out, w_fc, w_proj]
    )
    weight_qkv, weight_out, weight_fc, weight_proj = (
        a.reshape(-1, a.shape[-1]) for a in (weight_qkv, weight_out, weight_fc, weight_proj)
    )
    smalls = smalls.reshape(F, -1).astype(f32)
    whole = {n: smalls[:, a : a + size].reshape(-1) for n, (a, size) in places.items()}
    cell_count = row_count * D * S * F
    inputs = tokens.astype(f32)
    grad_out = cotangent.astype(f32)
    grads = dict(b_proj=jnp.sum(grad_out, axis=0))
    grad_act = jnp.einsum("td,fd->tf", cotangent, weight_proj, preferred_element_type=f32)
    grad_before = (slope.astype(f32) * grad_act).astype(bf16)
    grads["b_fc"] = jnp.sum(grad_before, axis=0, dtype=f32)
    grad_normed_two = jnp.einsum("tf,df->td", grad_before, weight_fc, preferred_element_type=f32)
    _, pull_two = jax.vjp(layer_norm, middle, whole["ln2_gain"], whole["ln2_bias"])
    grad_mid_norm, grads["ln2_gain"], grads["ln2_bias"] = pull_two(grad_normed_two)
    grad_middle = grad_out + grad_mid_norm
    grad_branch = grad_middle.astype(bf16)
    grads["b_out"] = jnp.sum(grad_branch, axis=0, dtype=f32)
    grad_mixed = jnp.einsum(
        "td,id->ti", grad_branch, weight_out, preferred_element_type=f32
    ).astype(bf16)
    grad_heads = lax.all_to_all(grad_mixed, "seq", split_axis=1, concat_axis=0, tiled=True)
    grad_qkv = attention_back(qkv, grad_heads, heads_out, lse)
    grad_projected = lax.all_to_all(
        grad_qkv.reshape(-1, 3, D // S), "seq", split_axis=0, concat_axis=2, tiled=True
    ).reshape(row_count, 3 * D)
    grads["b_qv"] = jnp.concatenate(
        [
            jnp.sum(grad_projected[:, :D], axis=0, dtype=f32),
            jnp.sum(grad_projected[:, 2 * D :], axis=0, dtype=f32),
        ]
    )
    grad_normed_one = jnp.einsum(
        "te,de->td", grad_projected, weight_qkv, preferred_element_type=f32
    )
    _, pull_one = jax.vjp(layer_norm, inputs, whole["ln1_gain"], whole["ln1_bias"])
    grad_in_norm, grads["ln1_gain"], grads["ln1_bias"] = pull_one(grad_normed_one)
    grad_tokens = (grad_middle + grad_in_norm).astype(bf16)

    core = lax.axis_index("seq") % 2
    pairs = [(s, s + 1 - 2 * (s % 2)) for s in range(S)]

    def half_grad(rows, columns):
        wide = columns.shape[1] // 2
        mine = lax.dynamic_slice_in_dim(columns, core * wide, wide, 1)
        theirs = lax.dynamic_slice_in_dim(columns, (1 - core) * wide, wide, 1)
        both_rows = jnp.concatenate([rows, lax.ppermute(rows, "seq", pairs)], axis=0)
        both_columns = jnp.concatenate([mine, lax.ppermute(theirs, "seq", pairs)], axis=0)
        grad = jnp.einsum("ta,tb->ab", both_rows, both_columns, preferred_element_type=f32)
        return grad.astype(bf16).reshape(F, -1, wide)

    halves = [
        half_grad(activated, cotangent),
        half_grad(normed_two, grad_before),
        half_grad(mixed_tokens, grad_branch),
        half_grad(normed_one, grad_projected),
    ]
    sums = jnp.sum(stats[:3], axis=1)
    width = at + 3
    total_rows = -(-width // 1024) * 8
    small_grads = jnp.concatenate(
        [grads[name].reshape(F, -1) for name in places]
        + [jnp.broadcast_to(sums, (F, 3)), jnp.zeros((F, total_rows * 128 - width), f32)],
        axis=1,
    ).reshape(F, total_rows, 128)
    (grad_w_proj, grad_w_fc, grad_w_out, grad_w_qkv), reduced = reduce_all(halves, small_grads)
    reduced = reduced.reshape(-1)
    got = {name: reduced[a : a + size] for name, (a, size) in places.items()}
    rms_values = jnp.sqrt(reduced[at : at + 3] / float(cell_count))
    return (
        output, grad_tokens, got["ln1_gain"], got["ln1_bias"], grad_w_qkv, got["b_qv"],
        grad_w_out, got["b_out"], got["ln2_gain"], got["ln2_bias"], grad_w_fc, got["b_fc"],
        grad_w_proj, got["b_proj"], rms_values,
    )


def solution(mesh):
    in_specs = (
        P(("fsdp", "seq"), None),
        P(("fsdp", "seq"), None),
        P("fsdp"),
        P("fsdp"),
        P("fsdp", None),
        P("fsdp"),
        P("fsdp", None),
        P("fsdp"),
        P("fsdp"),
        P("fsdp"),
        P("fsdp", None),
        P("fsdp"),
        P("fsdp", None),
        P("fsdp"),
    )
    out_specs = (
        P(("fsdp", "seq"), None),
        P(("fsdp", "seq"), None),
        P("fsdp"),
        P("fsdp"),
        P("fsdp", None),
        P("fsdp"),
        P("fsdp", None),
        P("fsdp"),
        P("fsdp"),
        P("fsdp"),
        P("fsdp", None),
        P("fsdp"),
        P("fsdp", None),
        P("fsdp"),
        P(),
    )
    return jax.shard_map(
        on_device, mesh=mesh, in_specs=in_specs, out_specs=out_specs, check_vma=False
    )
```

```python
import functools
import math

import jax
import jax.numpy as jnp
from jax import lax
from jax.experimental import pallas as pl
from jax.experimental.pallas import tpu as pltpu
from jax.sharding import PartitionSpec as P

BLK = 256
HD = 64
EPSILON = 1e-05
MESH = pl.DeviceIdType.MESH
f32, bf16 = jnp.float32, jnp.bfloat16

def geometry():
    F, S = lax.axis_size("fsdp"), lax.axis_size("seq")
    return F, S, 4, F // 4, S // 2


class Place:
    def __init__(self):
        self.F, self.S, self.H, self.L, self.X = geometry()
        self.f, self.s = lax.axis_index("fsdp"), lax.axis_index("seq")
        self.h, self.l = self.f // self.L, self.f % self.L
        self.x, self.c = self.s // 2, self.s % 2

    def shard(self, k, j):
        return lax.rem(self.h + self.H - k, self.H) * self.L + lax.rem(self.l + self.L - j, self.L)

    def hi(self, k):
        return (lax.rem(self.h + k, self.H) * self.L + self.l, self.s)

    def lo(self, j):
        return (self.h * self.L + lax.rem(self.l + j, self.L), self.s)

    def across(self, i):
        return (self.f, lax.rem(self.x + i, self.X) * 2 + self.c)

    def sibling(self):
        return (self.f, self.x * 2 + 1 - self.c)

    def everyone(self):
        return (
            [self.hi(k) for k in range(1, self.H)]
            + [self.lo(j) for j in range(1, self.L)]
            + [(self.f, lax.rem(self.s + i, self.S)) for i in range(1, self.S)]
        )


def greet(place):
    barrier = pltpu.get_barrier_semaphore()
    peers = place.everyone()
    for peer in peers:
        pl.semaphore_signal(barrier, inc=1, device_id=peer, device_id_type=MESH)
    pl.semaphore_wait(barrier, len(peers))


def vector(ref, places, name):
    at, size = places[name]
    parts = []
    for f in range(ref.shape[0]):
        pos = at
        while pos < at + size:
            row, lane = divmod(pos, 128)
            count = min(128 - lane, at + size - pos)
            parts.append(ref[f, row : row + 1, lane : lane + count])
            pos += count
    return jnp.concatenate(parts, axis=1)


def normalised(x):
    centre = x - jnp.mean(x, axis=-1, keepdims=True)
    return centre * lax.rsqrt(jnp.mean(centre * centre, axis=-1, keepdims=True) + EPSILON)


def gelu_and_slope(u):
    root = 0.7978845608028654
    square = u * u
    t = jnp.tanh(u * (root + root * 0.044715 * square))
    half = 0.5 * (1.0 + t)
    return u * half, half + u * (0.5 * (1.0 - t * t)) * (root + 3.0 * root * 0.044715 * square)


NT = (((1,), (1,)), ((), ()))
TN = (((0,), (0,)), ((), ()))


def head_lanes(shape, parity):
    lane = lax.broadcasted_iota(jnp.int32, shape, 1)
    return (lane // HD) == parity

def pick(rows, parity):
    return jnp.where(head_lanes(rows.shape, parity), rows, jnp.zeros_like(rows))

def turn(rows):
    return rows.astype(f32).T

def attend_block(i, wide, qkv, vT, scores, oT, lse):
    rows = pl.ds(i * BLK, BLK)
    @pl.loop(0, wide // HD)
    def _(h):
        pair = pl.multiple_of(h // 2 * 128, 128)
        q = pick(qkv[rows, pl.ds(pair, 128)], h % 2) * jnp.asarray(HD ** -0.5, bf16)
        top = jnp.full((8, BLK), -jnp.inf, f32)
        for j in range(i + 1):
            k = qkv[pl.ds(j * BLK, BLK), pl.ds(pl.multiple_of(wide + pair, 128), 128)]
            s = lax.dot_general(k, q, NT, preferred_element_type=f32)
            scores[pl.ds(j * BLK, BLK), :] = s
            top = jnp.maximum(top, jnp.max(s.reshape(BLK // 8, 8, BLK), axis=0))
        top = jnp.max(top, axis=0, keepdims=True)
        total = jnp.zeros((8, BLK), f32)
        out = jnp.zeros((HD, BLK), f32)
        for j in range(i + 1):
            p = jnp.exp(scores[pl.ds(j * BLK, BLK), :] - top)
            total = total + jnp.sum(p.reshape(BLK // 8, 8, BLK), axis=0)
            out = out + jnp.dot(vT[pl.ds(pl.multiple_of(h * HD, HD), HD), pl.ds(j * BLK, BLK)], p.astype(bf16), preferred_element_type=f32)
        total = jnp.sum(total, axis=0, keepdims=True)
        oT[pl.ds(pl.multiple_of(h * HD, HD), HD), :] = out * (1.0 / total)
        lse[pl.ds(h, 1), rows] = top + jnp.log(total)

def attend_back_block(i, pair, wide, qkv, grad, kT, lse, delta, dqT, dk, dv):
    rows = pl.ds(i * BLK, BLK)
    here = pl.ds(pair * 128, 128)

    @pl.loop(0, 128 // HD)
    def _(parity):
        h = pair * (128 // HD) + parity
        out_rows = pl.ds(pl.multiple_of(parity * HD, HD), HD)
        q = pick(qkv[rows, here], parity) * jnp.asarray(HD**-0.5, bf16)
        g = pick(grad[rows, here], parity)
        low = lse[pl.ds(h, 1), rows]
        mean = delta[pl.ds(h, 1), rows]
        out = jnp.zeros((HD, BLK), f32)
        for j in range(i + 1):
            keys = pl.ds(j * BLK, BLK)
            k = qkv[keys, wide + pair * 128 : wide + (pair + 1) * 128]
            v = qkv[keys, 2 * wide + pair * 128 : 2 * wide + (pair + 1) * 128]
            p = jnp.exp(lax.dot_general(k, q, NT, preferred_element_type=f32) - low)
            dp = lax.dot_general(v, g, NT, preferred_element_type=f32)
            ds = (p * (dp - mean)).astype(bf16)
            dv[keys, :] += jnp.dot(p.astype(bf16), g, preferred_element_type=f32)
            dk[keys, :] += jnp.dot(ds, q, preferred_element_type=f32)
            kT_rows = kT[pl.ds(pl.multiple_of(h * HD, HD), HD), keys]
            out = out + jnp.dot(kT_rows, ds, preferred_element_type=f32)
        dqT[out_rows, :] = out * HD**-0.5


def forward_kernel(places, *refs):
    refs = list(refs)

    def take(count):
        got = refs[:count]
        del refs[:count]
        return got

    tokens, cot, small = take(3)
    shards = take(4)
    big_outs = take(4)
    (small_out, one_out, qkv_out, lse_out, heads_out, mixed_out, middle_out, two_out, act_out,
     slope_out, result_out, stats_out, cot_out) = take(13)
    wholes = take(4)
    (smalls, smalls_f, one, split, qkv, vT, scores, oT, lse, heads, mixed, middle, two, act, slope,
     result, stats, vectors, wide_bias) = take(19)
    (own_sem, send_sem, save_sem, hi_sem, lo_sem, x_sem, core_sem, sm_hi_sem, sm_lo_sem, there_sem,
     back_sem, pair_sem) = refs
    p = Place()
    S, H, L, X, F = p.S, p.H, p.L, p.X, p.F
    rows_here, D = tokens.shape
    wide = D // S
    sent, saved = [], []

    def push(src, dst, sem, peer):
        cp = pltpu.make_async_remote_copy(
            src_ref=src, dst_ref=dst, send_sem=send_sem.at[0], recv_sem=sem, device_id=peer,
            device_id_type=MESH,
        )
        cp.start()
        sent.append(cp)

    def arrived(dst, sem):
        pltpu.make_async_copy(dst, dst, sem).wait()

    def save(src, dst):
        cp = pltpu.make_async_copy(src, dst, save_sem.at[len(saved)])
        cp.start()
        saved.append(cp)

    def share(src, dst, index):
        save(src, dst.at[0:rows_here])
        push(src, dst.at[rows_here:], pair_sem.at[index], p.sibling())

    own = []
    for w in range(4):
        own.append(pltpu.make_async_copy(shards[w], wholes[w].at[p.f], own_sem.at[w]))
    own.append(pltpu.make_async_copy(small, smalls.at[p.f], own_sem.at[4]))
    for cp in own:
        cp.start()
    greet(p)

    width = 5 - X
    step = 3 // (X - 1) if X > 1 else 0

    def cols(w, start, count):
        C = shards[w].shape[-1]
        return pl.ds(pl.multiple_of(p.c * (C // 2) + start * (C // 8), 128), count * (C // 8))

    def half(w, core):
        C = shards[w].shape[-1]
        return pl.ds(pl.multiple_of(core * (C // 2), 128), C // 2)

    def start_hi(w):
        mine = cols(w, p.x, width)
        for k in range(1, H):
            push(shards[w].at[:, mine], wholes[w].at[p.f, :, mine], hi_sem.at[w, k - 1], p.hi(k))
        for j in range(1, L):
            push(shards[w].at[:, mine], wholes[w].at[p.f, :, mine], lo_sem.at[w, j - 1, 0], p.lo(j))

    def over_x(w, j, k):
        piece = wholes[w].at[p.shard(k, j), :, cols(w, p.x * step, 1)]
        for i in range(1, X):
            push(piece, piece, x_sem.at[w, i - 1, j * H + k - 1], p.across(i))

    def finish_hi(w, k):
        piece = wholes[w].at[p.shard(k, 0), :, cols(w, p.x, width)]
        arrived(piece, hi_sem.at[w, k - 1])
        for j in range(1, L):
            push(piece, piece, lo_sem.at[w, j - 1, k], p.lo(j))
        over_x(w, 0, k)

    def finish_lo(w, k):
        for j in range(1, L):
            arrived(wholes[w].at[p.shard(k, j), :, cols(w, p.x, width)], lo_sem.at[w, j - 1, k])
            over_x(w, j, k)

    def finish_x(w, j, k):
        for i in range(1, X):
            theirs = lax.rem(p.x + X - i, X) * step
            arrived(wholes[w].at[p.shard(k, j), :, cols(w, theirs, 1)], x_sem.at[w, i - 1, j * H + k - 1])
        piece = wholes[w].at[p.shard(k, j), :, half(w, p.c)]
        push(piece, piece, core_sem.at[w, j * H + k - 1], p.sibling())

    def finish_core(w):
        for j in range(L):
            for k in range(H):
                if (j, k) != (0, 0):
                    arrived(wholes[w].at[p.shard(k, j), :, half(w, 1 - p.c)], core_sem.at[w, j * H + k - 1])
        own[w].wait()
        save(wholes[w], big_outs[w])

    def queue_of(w):
        todo = []
        for k in range(1, H):
            todo.append(functools.partial(finish_hi, w, k))
            todo.append(functools.partial(finish_lo, w, k - 1))
        todo.append(functools.partial(finish_lo, w, H - 1))
        for k in range(1, H):
            todo.append(functools.partial(finish_x, w, 0, k))
        for j in range(1, L):
            for k in range(H):
                todo.append(functools.partial(finish_x, w, j, k))
        todo.append(functools.partial(finish_core, w))
        return todo

    def run(todo, count):
        for _ in range(min(count, len(todo))):
            todo.pop(0)()

    save(cot.at[:, pl.ds(pl.multiple_of(p.c * (D // 2), 128), D // 2)], cot_out.at[0:rows_here])
    push(
        cot.at[:, pl.ds(pl.multiple_of((1 - p.c) * (D // 2), 128), D // 2)],
        cot_out.at[rows_here:], pair_sem.at[4], p.sibling(),
    )
    for k in range(1, H):
        push(small, smalls.at[p.f], sm_hi_sem.at[k - 1], p.hi(k))
    for j in range(1, L):
        push(small, smalls.at[p.f], sm_lo_sem.at[j - 1, 0], p.lo(j))
    start_hi(0)
    for k in range(1, H):
        piece = smalls.at[p.shard(k, 0)]
        arrived(piece, sm_hi_sem.at[k - 1])
        for j in range(1, L):
            push(piece, piece, sm_lo_sem.at[j - 1, k], p.lo(j))
    for j in range(1, L):
        for k in range(H):
            arrived(smalls.at[p.shard(k, j)], sm_lo_sem.at[j - 1, k])
    own[4].wait()
    smalls_f[...] = smalls[...].astype(f32)
    save(smalls_f, small_out)
    vec = functools.partial(vector, smalls_f, places)

    chunk = 128
    stats[...] = jnp.zeros_like(stats)
    gain, shift = vec("ln1_gain"), vec("ln1_bias")

    @pl.loop(0, rows_here // chunk)
    def _(t):
        at = pl.ds(pl.multiple_of(t * chunk, chunk), chunk)
        x = tokens[at, :].astype(f32)
        stats[0:1, :] += jnp.sum(x * x, axis=0, keepdims=True)
        one[at, :] = (normalised(x) * gain + shift).astype(bf16)

    share(one, one_out, 0)
    first, second, third, fourth = (queue_of(w) for w in range(4))
    run(first, 1)
    start_hi(1)
    run(first, 4)
    start_hi(2)
    run(first, len(first))

    bias_qv = vec("b_qv")

    def project(kind, target):
        at = pl.multiple_of(kind * D + target * wide, 128)
        w = wholes[0][:, :, pl.ds(at, wide)].reshape(D, wide)
        return jnp.dot(one[...], w, preferred_element_type=f32)

    vectors[0:1, :] = bias_qv[:, :D]
    vectors[1:2, :] = bias_qv[:, D:]

    def heads_of(target):
        lanes = pl.ds(pl.multiple_of(target * wide, 128), wide)
        return [
            (project(0, target) + vectors[0:1, lanes]).astype(bf16),
            project(1, target).astype(bf16),
            (project(2, target) + vectors[1:2, lanes]).astype(bf16),
        ]

    mine = pl.ds(pl.multiple_of(p.s * rows_here, 128), rows_here)
    for i in list(range(1, S)) + [0]:
        target = lax.rem(p.s + i, S)
        for kind, values in enumerate(heads_of(target)):
            if i == 0:
                qkv[mine, kind * wide : (kind + 1) * wide] = values
            else:
                split[i - 1, :, kind * wide : (kind + 1) * wide] = values
        if i:
            push(split.at[i - 1], qkv.at[mine, :], there_sem.at[i - 1], (p.f, target))
    run(second, 7)
    run(third, 1)
    run(second, len(second))
    run(third, 3)
    start_hi(3)
    run(third, 1)
    for i in range(1, S):
        source = lax.rem(p.s + S - i, S)
        arrived(qkv.at[pl.ds(pl.multiple_of(source * rows_here, 128), rows_here), :], there_sem.at[i - 1])
    save(qkv, qkv_out)

    length = qkv.shape[0]
    blocks = length // BLK
    for b in range(blocks):
        at = pl.ds(b * BLK, BLK)
        vT[:, at] = turn(qkv[at, 2 * wide :]).astype(bf16)
    lse[...] = jnp.zeros_like(lse)
    sent_back = 0
    for i in range(blocks):
        attend_block(i, wide, qkv, vT, scores, oT, lse)
        heads[pl.ds(i * BLK, BLK), :] = turn(oT[...]).astype(bf16)
        while (sent_back + 1) * rows_here <= (i + 1) * BLK:
            rows = pl.ds(sent_back * rows_here, rows_here)
            lanes = pl.ds(pl.multiple_of(p.s * wide, 128), wide)

            @pl.when(p.s != sent_back)
            def _():
                pltpu.make_async_remote_copy(
                    src_ref=heads.at[rows], dst_ref=mixed.at[:, lanes], send_sem=send_sem.at[1],
                    recv_sem=back_sem.at[p.s], device_id=(p.f, jnp.int32(sent_back)),
                    device_id_type=MESH,
                ).start()

            @pl.when(p.s == sent_back)
            def _():
                mixed[:, lanes] = heads[rows, :]

            sent_back += 1
        run(third, 2)
    save(heads, heads_out)
    save(lse, lse_out)
    run(third, 3)
    for i in range(1, S):
        source = lax.rem(p.s + S - i, S)
        arrived(mixed.at[:, pl.ds(pl.multiple_of(source * wide, 128), wide)], back_sem.at[source])
    share(mixed, mixed_out, 1)

    tile = 256
    vectors[0:1, :] = vec("b_out")

    @pl.loop(0, D // tile)
    def _(t):
        at = pl.ds(pl.multiple_of(t * tile, tile), tile)
        w = wholes[1][:, :, at].reshape(D, tile)
        branch = jnp.dot(mixed[...], w, preferred_element_type=f32) + vectors[0:1, at]
        middle[:, at] = tokens[:, at].astype(f32) + branch

    save(middle, middle_out)
    gain_two, shift_two = vec("ln2_gain"), vec("ln2_bias")

    @pl.loop(0, rows_here // chunk)
    def _(t):
        at = pl.ds(pl.multiple_of(t * chunk, chunk), chunk)
        x = middle[at, :]
        stats[1:2, :] += jnp.sum(x * x, axis=0, keepdims=True)
        two[at, :] = (normalised(x) * gain_two + shift_two).astype(bf16)

    share(two, two_out, 2)
    run(third, len(third))
    run(fourth, 2)
    wide_bias[0:1, :] = vec("b_fc")

    FF = act.shape[1]

    @pl.loop(0, FF // tile)
    def _(t):
        at = pl.ds(pl.multiple_of(t * tile, tile), tile)
        w = wholes[2][:, :, at].reshape(D, tile)
        u = jnp.dot(two[...], w, preferred_element_type=f32) + wide_bias[0:1, at]
        act_rows, slope_rows = gelu_and_slope(u)
        act[:, at] = act_rows.astype(bf16)
        slope[:, at] = slope_rows.astype(bf16)

    share(act, act_out, 3)
    save(slope, slope_out)
    run(fourth, len(fourth))
    vectors[0:1, :] = vec("b_proj")

    @pl.loop(0, D // tile)
    def _(t):
        at = pl.ds(pl.multiple_of(t * tile, tile), tile)
        w = wholes[3][:, :, at].reshape(FF, tile)
        stream = middle[:, at] + (jnp.dot(act[...], w, preferred_element_type=f32) + vectors[0:1, at])
        stats[2:3, at] = jnp.sum(stream * stream, axis=0, keepdims=True)
        result[:, at] = stream.astype(bf16)

    save(result, result_out)
    save(stats, stats_out)
    for index, there in enumerate((one_out, mixed_out, two_out, act_out, cot_out)):
        arrived(there.at[rows_here:], pair_sem.at[index])
    for cp in sent:
        cp.wait_send()
    for i in range(1, S):
        arrived(heads.at[pl.ds(0, rows_here)], send_sem.at[1])
    for cp in saved:
        cp.wait()


def forward(tokens, cotangent, packed, places, shards):
    F, S, H, L, X = geometry()
    rows_here, D = tokens.shape
    wide, length, FF = D // S, rows_here * S, shards[2].shape[1]
    heads = max(8, wide // HD)
    lead = max(X - 1, 1)
    any_spec = pl.BlockSpec(memory_space=pl.ANY)
    V, D_SEM = pltpu.VMEM, pltpu.SemaphoreType.DMA
    shaped = jax.ShapeDtypeStruct
    wholes = [(F,) + a.shape for a in shards]
    outs = [shaped(s, bf16) for s in wholes] + [
        shaped((F,) + packed.shape, f32),
        shaped((2 * rows_here, D), bf16),
        shaped((length, 3 * wide), bf16),
        shaped((heads, length), f32),
        shaped((length, wide), bf16),
        shaped((2 * rows_here, D), bf16),
        shaped((rows_here, D), f32),
        shaped((2 * rows_here, D), bf16),
        shaped((2 * rows_here, FF), bf16),
        shaped((rows_here, FF), bf16),
        shaped((rows_here, D), bf16),
        shaped((8, D), f32),
        shaped((2 * rows_here, D // 2), bf16),
    ]
    return pl.pallas_call(
        functools.partial(forward_kernel, places),
        out_shape=outs,
        in_specs=[pl.BlockSpec(memory_space=pltpu.VMEM)] + [any_spec] * 6,
        out_specs=[any_spec] * len(outs),
        scratch_shapes=[V(s, bf16) for s in wholes]
        + [
            V((F,) + packed.shape, bf16),
            V((F,) + packed.shape, f32),
            V((rows_here, D), bf16),
            V((S - 1, rows_here, 3 * wide), bf16),
            V((length, 3 * wide), bf16),
            V((wide, length), bf16),
            V((length, BLK), f32),
            V((wide, BLK), f32),
            V((heads, length), f32),
            V((length, wide), bf16),
            V((rows_here, D), bf16),
            V((rows_here, D), f32),
            V((rows_here, D), bf16),
            V((rows_here, FF), bf16),
            V((rows_here, FF), bf16),
            V((rows_here, D), bf16),
            V((8, D), f32),
            V((8, D), f32),
            V((8, FF), f32),
            D_SEM((5,)),
            D_SEM((2,)),
            D_SEM((len(outs) + 8,)),
            D_SEM((4, H - 1)),
            D_SEM((4, L - 1, H)),
            D_SEM((4, lead, F - 1)),
            D_SEM((4, F - 1)),
            D_SEM((H - 1,)),
            D_SEM((L - 1, H)),
            D_SEM((S - 1,)),
            D_SEM((S,)),
            D_SEM((5,)),
        ],
        compiler_params=pltpu.CompilerParams(
            collective_id=1, has_side_effects=True, vmem_limit_bytes=60 * 2**20
        ),
    )(tokens, cotangent, packed, *shards)


def backward_kernel(places, *refs):
    refs = list(refs)

    def take(count):
        got = refs[:count]
        del refs[:count]
        return got

    cot, = take(1)
    (tokens, smalls, wq_in, wo_in, wf_in, wp_in, one_in, qkv_in, lse_in, heads_in, mixed_in,
     middle_in, two_in, act_in, slope_in, stats, cot_in) = take(17)
    grad_tokens, = take(1)
    outs = take(4)
    small_out, = take(1)
    parts, from_x, from_lo, from_hi, value, from_x_end, half_out = (take(4) for _ in range(7))
    (cot_pair, gbh, gb_other, grad_middle, branch, branch_pair, leaving, grad_heads, grad_qkv,
     grad_proj, proj_pair, sums, fc_sum, smalls_f, stats_v) = take(15)
    sm_mine, sm_core, sm_x, sm_sum, sm_lo, sm_hi = take(6)
    (load_sem, slot_sem, send_sem, x_sem, lo_sem, hi_sem, end_sem, out_sem, core_sem, pair_sem, to_sem,
     from_sem, sm_sem, smx_sem, smlo_sem, smhi_sem, gb_sem) = refs
    p = Place()
    S, H, L, X, F = p.S, p.H, p.L, p.X, p.F
    R, D = cot.shape
    FF = fc_sum.shape[1]
    wide = D // S
    N = R * S
    width = 5 - X
    step = 3 // (X - 1) if X > 1 else 0
    sent = []

    def push(src, dst, sem, peer):
        pltpu.make_async_remote_copy(
            src_ref=src, dst_ref=dst, send_sem=send_sem.at[0], recv_sem=sem, device_id=peer,
            device_id_type=MESH,
        ).start()
        sent.append(math.prod(src.shape) * src.dtype.itemsize)

    def arrived(dst, sem):
        pltpu.make_async_copy(dst, dst, sem).wait()

    loads = {}

    def load(index, src, dst):
        loads[index] = pltpu.make_async_copy(src, dst, load_sem.at[index])
        loads[index].start()

    def unit(w):
        return parts[w].shape[-1] // 4

    def span(w, start, count):
        return pl.ds(pl.multiple_of(start * unit(w), 128), count * unit(w))

    def group(w):
        return max(1, 128 // parts[w].shape[1])

    def ahead(k, j):
        return lax.rem(p.h + k, H) * L + lax.rem(p.l + j, L)

    rel = [(j, k) for j in list(range(1, L)) + [0] for k in list(range(1, H)) + [0]]

    def order(w):
        if group(w) == 1:
            return [ahead(k, j) for j, k in rel]
        return [t * group(w) for t in range(F // group(w))]

    def send_x(w, f):
        g = group(w)
        for i in range(1, X):
            push(
                parts[w].at[pl.ds(f, g), :, span(w, lax.rem(p.x + i, X) * step, 1)],
                from_x[w].at[i - 1, pl.ds(f, g)], x_sem.at[w, i - 1, f // g], p.across(i),
            )

    def add_x(w, f):
        g = group(w)
        cols = span(w, p.x * step, 1)
        for i in range(1, X):
            arrived(from_x[w].at[i - 1, pl.ds(f, g)], x_sem.at[w, i - 1, f // g])
        if X > 1:
            total = parts[w][pl.ds(f, g), :, cols].astype(f32)
            for i in range(1, X):
                total = total + from_x[w][i - 1, pl.ds(f, g)].astype(f32)
            parts[w][pl.ds(f, g), :, cols] = total.astype(bf16)

    def send_lo(w, j, k, add):
        f = ahead(k, j)
        if add:
            add_x(w, f)
        push(
            parts[w].at[f, :, span(w, p.x, width)], from_lo[w].at[j - 1, lax.rem(p.h + k, H)],
            lo_sem.at[w, j - 1, k], p.lo(j),
        )

    def add_lo(w, k, add):
        f = ahead(k, 0)
        if add:
            add_x(w, f)
        cols = span(w, p.x, width)
        total = parts[w][f, :, cols].astype(f32)
        for j in range(1, L):
            came = from_lo[w].at[j - 1, lax.rem(p.h + k, H)]
            arrived(came, lo_sem.at[w, j - 1, k])
            total = total + came[...].astype(f32)
        parts[w][f, :, cols] = total.astype(bf16)
        if k > 0:
            push(parts[w].at[f, :, cols], from_hi[w].at[k - 1], hi_sem.at[w, k - 1], p.hi(k))

    def add_hi(w):
        cols = span(w, p.x, width)
        total = parts[w][p.f, :, cols].astype(f32)
        for k in range(1, H):
            arrived(from_hi[w].at[k - 1], hi_sem.at[w, k - 1])
            total = total + from_hi[w][k - 1].astype(f32)
        value[w][:, cols] = total.astype(bf16)
        for i in range(1, X):
            push(
                value[w].at[:, cols], from_x_end[w].at[i - 1, :, cols], end_sem.at[w, i - 1],
                p.across(i),
            )

    def finish(w):
        mine = span(w, p.x * step, 1)
        half_out[w][:, mine] = value[w][:, mine].astype(f32)
        for i in range(1, X):
            source = lax.rem(p.x + X - i, X)
            cols = span(w, source, width)
            arrived(from_x_end[w].at[i - 1, :, cols], end_sem.at[w, i - 1])
            theirs = span(w, source * step, 1)
            half_out[w][:, theirs] = from_x_end[w][i - 1, :, theirs].astype(f32)
        if X < 4:
            both = pl.ds(unit(w), (4 - X) * unit(w))
            total = value[w][:, both].astype(f32)
            for i in range(1, X):
                total = total + from_x_end[w][i - 1, :, both].astype(f32)
            half_out[w][:, both] = total
        there = outs[w].at[:, pl.ds(pl.multiple_of(p.c * 4 * unit(w), 128), 4 * unit(w))]
        push(half_out[w], there, core_sem.at[w], p.sibling())
        pltpu.make_async_copy(half_out[w], there, out_sem.at[w]).start()

    to_lo, to_hi, to_x, to_end = [], [], [], []
    for w in range(4):
        add = group(w) == 1
        todo = [] if add else [functools.partial(add_x, w, f) for f in order(w)]
        to_lo.append(todo + [functools.partial(send_lo, w, j, k, add) for j, k in rel if j > 0])
        to_hi.append([functools.partial(add_lo, w, k, add) for j, k in rel if j == 0])
        to_x.append([functools.partial(add_hi, w)])
        to_end.append([functools.partial(finish, w)])

    def run(todo, count):
        for _ in range(min(count, len(todo))):
            todo.pop(0)()

    load(0, cot_in, cot_pair)
    load(1, smalls, smalls_f)
    load(2, stats, stats_v)
    greet(p)

    tile = FF // F
    grad_middle[...] = jnp.zeros_like(grad_middle)
    loads[0].wait()

    def feed_forward(wp, wf, act, slope):
        tiles = order(0)

        def fetch(t, f):
            slot = t % 2
            cols = pl.ds(pl.multiple_of(f * tile, 128), tile)
            return [
                pltpu.make_async_copy(wp_in.at[f], wp.at[slot], slot_sem.at[slot, 0]),
                pltpu.make_async_copy(wf_in.at[:, :, cols], wf.at[slot], slot_sem.at[slot, 1]),
                pltpu.make_async_copy(act_in.at[:, cols], act.at[slot], slot_sem.at[slot, 2]),
                pltpu.make_async_copy(slope_in.at[:, cols], slope.at[slot], slot_sem.at[slot, 3]),
            ]

        coming = fetch(0, tiles[0])
        for cp in coming:
            cp.start()
        for t, f in enumerate(tiles):
            for cp in coming:
                cp.wait()
            if t + 1 < len(tiles):
                coming = fetch(t + 1, tiles[t + 1])
                for cp in coming:
                    cp.start()
            slot = t % 2
            parts[0][f] = lax.dot_general(
                act[slot], cot_pair[...], TN, preferred_element_type=f32
            ).astype(bf16)
            send_x(0, f)
            grad_act = lax.dot_general(cot[...], wp[slot], NT, preferred_element_type=f32)
            before = (slope[slot].astype(f32) * grad_act).astype(bf16)
            fc_sum[0:1, pl.ds(pl.multiple_of(f * tile, 128), tile)] = jnp.sum(
                before.astype(f32), axis=0, keepdims=True
            )
            at = pl.ds(pl.multiple_of(lax.rem(f, F // 2) * tile, 128), tile)

            @pl.when(f // (F // 2) == p.c)
            def _():
                gbh[0:R, at] = before

            @pl.when(f // (F // 2) != p.c)
            def _():
                gb_other[:, at] = before
                pltpu.make_async_remote_copy(
                    src_ref=gb_other.at[:, at], dst_ref=gbh.at[R : 2 * R, at], send_sem=gb_sem.at[0],
                    recv_sem=gb_sem.at[1], device_id=p.sibling(), device_id_type=MESH,
                ).start()

            grad_middle[...] += lax.dot_general(
                before, wf[slot].reshape(D, tile), NT, preferred_element_type=f32
            )
            if t > 0:
                run(to_lo[0], 1)

    pl.run_scoped(
        feed_forward,
        pltpu.VMEM((2,) + wp_in.shape[1:], bf16),
        pltpu.VMEM((2,) + wf_in.shape[:2] + (tile,), bf16),
        pltpu.VMEM((2, 2 * R, tile), bf16),
        pltpu.VMEM((2, R, tile), bf16),
    )

    chunk = 128
    sums[...] = jnp.zeros_like(sums)
    loads[1].wait()
    loads[2].wait()

    def norm_back(rows, grad, gain, first):
        centre = rows - jnp.mean(rows, axis=-1, keepdims=True)
        scale = lax.rsqrt(jnp.mean(centre * centre, axis=-1, keepdims=True) + EPSILON)
        n = centre * scale
        sums[first : first + 1, :] += jnp.sum(grad * n, axis=0, keepdims=True)
        sums[first + 1 : first + 2, :] += jnp.sum(grad, axis=0, keepdims=True)
        scaled = grad * gain
        return scale * (
            scaled
            - jnp.mean(scaled, axis=-1, keepdims=True)
            - n * jnp.mean(scaled * n, axis=-1, keepdims=True)
        )

    def weight_grad(w, rows_pair, columns_pair, todo, every):
        g, r = group(w), parts[w].shape[1]
        for t, f in enumerate(order(w)):
            at = pl.ds(pl.multiple_of(f * r, 128), g * r)
            grad = lax.dot_general(
                rows_pair[:, at], columns_pair[...], TN, preferred_element_type=f32
            )
            parts[w][pl.ds(f, g)] = grad.astype(bf16).reshape(g, r, grad.shape[1])
            send_x(w, f)
            if t % every == every - 1:
                run(todo, 1)

    def attention_output(middle, wo, two, mixed):
        load(3, middle_in, middle)
        load(4, wo_in, wo)
        load(5, two_in, two)
        load(6, mixed_in, mixed)
        gain = vector(smalls_f, places, "ln2_gain")
        loads[3].wait()

        @pl.loop(0, R // chunk)
        def _(t):
            at = pl.ds(pl.multiple_of(t * chunk, chunk), chunk)
            out = cot[at, :].astype(f32)
            sums[5:6, :] += jnp.sum(out, axis=0, keepdims=True)
            total = out + norm_back(middle[at, :], grad_middle[at, :], gain, 0)
            grad_middle[at, :] = total
            rounded = total.astype(bf16)
            branch[at, :] = rounded
            sums[4:5, :] += jnp.sum(rounded.astype(f32), axis=0, keepdims=True)

        half = D // 2
        branch_pair[0:R, :] = branch[:, pl.ds(pl.multiple_of(p.c * half, 128), half)]
        push(
            branch.at[:, pl.ds(pl.multiple_of((1 - p.c) * half, 128), half)],
            branch_pair.at[R : 2 * R, :], pair_sem.at[0], p.sibling(),
        )
        loads[4].wait()
        r = wo.shape[1]
        mine = pl.ds(pl.multiple_of(p.s * R, 128), R)
        for i in list(range(1, S)) + [0]:
            target = lax.rem(p.s + i, S)
            rows = wo[pl.ds(target * (wide // r), wide // r)].reshape(wide, D)
            grad = lax.dot_general(branch[...], rows, NT, preferred_element_type=f32).astype(bf16)
            if i:
                leaving[i - 1] = grad
                push(leaving.at[i - 1], grad_heads.at[mine, :], to_sem.at[i - 1], (p.f, target))
            else:
                grad_heads[mine, :] = grad
        loads[5].wait()
        arrived(gbh.at[R : 2 * R, :], gb_sem.at[1])
        run(to_lo[0], len(to_lo[0]))
        todo = []
        while to_hi[0] or to_lo[1]:
            todo += to_hi[0][:1] + to_lo[1][:1]
            del to_hi[0][:1], to_lo[1][:1]
        weight_grad(1, two, gbh, todo, 1)
        loads[6].wait()
        arrived(branch_pair.at[R : 2 * R, :], pair_sem.at[0])
        weight_grad(2, mixed, branch_pair, todo, 1)
        run(todo, len(todo))

    pl.run_scoped(
        attention_output,
        pltpu.VMEM((R, D), f32),
        pltpu.VMEM(wo_in.shape, bf16),
        pltpu.VMEM((2 * R, D), bf16),
        pltpu.VMEM((2 * R, D), bf16),
    )

    pairs = wide // 128

    def attention(qkv, heads, lse, kT, delta, dqT, dk, dv):
        load(7, qkv_in, qkv)
        load(8, heads_in, heads)
        load(9, lse_in, lse)
        for i in range(1, S):
            source = lax.rem(p.s + S - i, S)
            arrived(grad_heads.at[pl.ds(pl.multiple_of(source * R, 128), R), :], to_sem.at[i - 1])
        for index in (7, 8, 9):
            loads[index].wait()
        shape = (lse.shape[0], wide)
        chosen = lax.broadcasted_iota(jnp.int32, shape, 1) // HD == lax.broadcasted_iota(jnp.int32, shape, 0)
        chosen = jnp.where(chosen, 1.0, 0.0).astype(bf16)
        for b in range(N // BLK):
            at = pl.ds(b * BLK, BLK)
            kT[:, at] = turn(qkv[at, wide : 2 * wide]).astype(bf16)
            product = grad_heads[at, :].astype(f32) * heads[at, :].astype(f32)
            high = product.astype(bf16)
            low = (product - high.astype(f32)).astype(bf16)
            delta[:, at] = lax.dot_general(chosen, high, NT, preferred_element_type=f32) + lax.dot_general(
                chosen, low, NT, preferred_element_type=f32
            )
        todo = to_x[0] + to_lo[2] + to_end[0] + to_hi[1][:2]
        rest = to_hi[1][2:] + to_hi[2] + to_x[1] + to_x[2] + to_end[1] + to_end[2]
        share = -(-len(todo) // (pairs * (N // BLK)))
        for pair in range(pairs):
            dk[...] = jnp.zeros_like(dk)
            dv[...] = jnp.zeros_like(dv)
            for i in range(N // BLK):
                attend_back_block(i, pair, wide, qkv, grad_heads, kT, lse, delta, dqT, dk, dv)
                grad_qkv[pair, pl.ds(i * BLK, BLK), 0:128] = turn(dqT[...]).astype(bf16)
                run(todo, share)
            grad_qkv[pair, :, 128:256] = dk[...].astype(bf16)
            grad_qkv[pair, :, 256:384] = dv[...].astype(bf16)
            for i in list(range(1, S)) + [0]:
                target = lax.rem(p.s + i, S)
                rows = pl.ds(pl.multiple_of(target * R, 128), R)
                for kind in range(3):
                    lanes = pl.ds(pl.multiple_of(kind * D + p.s * wide + pair * 128, 128), 128)
                    block = grad_qkv.at[pair, rows, kind * 128 : (kind + 1) * 128]
                    if i:
                        push(block, grad_proj.at[:, lanes], from_sem.at[i - 1, pair, kind], (p.f, target))
                    else:
                        grad_proj[:, lanes] = block[...]
        run(todo, len(todo))
        run(rest, 4)
        late.extend(rest)

    late = []
    pl.run_scoped(
        attention,
        pltpu.VMEM((N, 3 * wide), bf16),
        pltpu.VMEM((N, wide), bf16),
        pltpu.VMEM(lse_in.shape, f32),
        pltpu.VMEM((wide, N), bf16),
        pltpu.VMEM(lse_in.shape, f32),
        pltpu.VMEM((128, BLK), f32),
        pltpu.VMEM((N, 128), f32),
        pltpu.VMEM((N, 128), f32),
    )

    def projections(wq, one, tokens_v, result, qv_sum):
        load(10, wq_in, wq)
        load(11, one_in, one)
        load(12, tokens, tokens_v)
        for i in range(1, S):
            source = lax.rem(p.s + S - i, S)
            for pair in range(pairs):
                for kind in range(3):
                    lanes = pl.ds(pl.multiple_of(kind * D + source * wide + pair * 128, 128), 128)
                    arrived(grad_proj.at[:, lanes], from_sem.at[i - 1, pair, kind])
        half = 3 * D // 2
        push(
            grad_proj.at[:, pl.ds(pl.multiple_of((1 - p.c) * half, 128), half)],
            proj_pair.at[R : 2 * R, :], pair_sem.at[1], p.sibling(),
        )
        proj_pair[0:R, :] = grad_proj[:, pl.ds(pl.multiple_of(p.c * half, 128), half)]
        qv_sum[0:1, 0:D] = jnp.sum(grad_proj[:, 0:D].astype(f32), axis=0, keepdims=True)
        qv_sum[0:1, D:] = jnp.sum(grad_proj[:, 2 * D :].astype(f32), axis=0, keepdims=True)
        loads[11].wait()
        arrived(proj_pair.at[R : 2 * R, :], pair_sem.at[1])
        todo = [lambda: None] + to_lo[3] + late
        weight_grad(3, one, proj_pair, todo, 1)
        run(todo, len(todo))
        loads[10].wait()
        rows = 256
        r = wq.shape[1]

        @pl.loop(0, D // rows)
        def _(t):
            w = wq[pl.ds(t * (rows // r), rows // r)].reshape(rows, 3 * D)
            result[:, pl.ds(pl.multiple_of(t * rows, rows), rows)] = lax.dot_general(
                grad_proj[...], w, NT, preferred_element_type=f32
            )

        run(to_hi[3], 2)
        loads[12].wait()
        gain = vector(smalls_f, places, "ln1_gain")

        @pl.loop(0, R // chunk)
        def _(t):
            at = pl.ds(pl.multiple_of(t * chunk, chunk), chunk)
            moved = norm_back(tokens_v[at, :].astype(f32), result[at, :], gain, 2)
            tokens_v[at, :] = (grad_middle[at, :] + moved).astype(bf16)

        cp = pltpu.make_async_copy(tokens_v, grad_tokens, load_sem.at[13])
        cp.start()
        values = dict(
            ln2_gain=sums[0:1, :], ln2_bias=sums[1:2, :], ln1_gain=sums[2:3, :],
            ln1_bias=sums[3:4, :], b_out=sums[4:5, :], b_proj=sums[5:6, :], b_fc=fc_sum[0:1, :],
            b_qv=qv_sum[0:1, :],
        )
        sm_mine[...] = jnp.zeros_like(sm_mine)
        last = 0
        for name, (start, size) in places.items():
            whole = values[name]
            for f in range(F):
                pos = start
                while pos < start + size:
                    row, lane = divmod(pos, 128)
                    count = min(128 - lane, start + size - pos)
                    at = f * size + pos - start
                    sm_mine[f, row : row + 1, lane : lane + count] = whole[:, at : at + count]
                    pos += count
            last = max(last, start + size)
        row = -(-last // 128)
        lane = lax.broadcasted_iota(jnp.int32, (1, 128), 1)
        line = jnp.zeros((1, 128), f32)
        for i in range(3):
            line = jnp.where(lane == i, jnp.sum(stats_v[i : i + 1, :], axis=1, keepdims=True), line)
        for f in range(F):
            sm_mine[f, row : row + 1, :] = line
        push(sm_mine, sm_core, sm_sem.at[0], p.sibling())
        run(to_hi[3], len(to_hi[3]))
        run(to_x[3], 1)
        arrived(sm_core, sm_sem.at[0])
        sm_x[p.x] = sm_mine[...] + sm_core[...]
        for i in range(1, X):
            push(sm_x.at[p.x], sm_x.at[p.x], smx_sem.at[i - 1], p.across(i))
        cp.wait()

    pl.run_scoped(
        projections,
        pltpu.VMEM(wq_in.shape, bf16),
        pltpu.VMEM((2 * R, D), bf16),
        pltpu.VMEM((R, D), bf16),
        pltpu.VMEM((R, D), f32),
        pltpu.VMEM((8, 2 * D), f32),
    )
    for i in range(1, X):
        arrived(sm_x.at[lax.rem(p.x + X - i, X)], smx_sem.at[i - 1])
    total = sm_x[0]
    for i in range(1, X):
        total = total + sm_x[i]
    sm_sum[...] = total
    for j in range(1, L):
        for k in range(H):
            h = lax.rem(p.h + k, H)
            push(sm_sum.at[ahead(k, j)], sm_lo.at[p.l, h], smlo_sem.at[j - 1, k], p.lo(j))
    run(to_end[3], 1)
    for k in list(range(1, H)) + [0]:
        h = lax.rem(p.h + k, H)
        sm_lo[p.l, h] = sm_sum[h * L + p.l]
        for j in range(1, L):
            arrived(sm_lo.at[lax.rem(p.l + L - j, L), h], smlo_sem.at[j - 1, k])
        total = sm_lo[0, h]
        for j in range(1, L):
            total = total + sm_lo[j, h]
        if k > 0:
            sm_core[h] = total
            push(sm_core.at[h], sm_hi.at[p.h], smhi_sem.at[k - 1], p.hi(k))
        else:
            sm_hi[p.h] = total
    for k in range(1, H):
        arrived(sm_hi.at[lax.rem(p.h + H - k, H)], smhi_sem.at[k - 1])
    total = sm_hi[0]
    for k in range(1, H):
        total = total + sm_hi[k]
    small_out[...] = total
    for w in range(4):
        arrived(half_out[w], core_sem.at[w])
        arrived(half_out[w], out_sem.at[w])
    arrived(gb_other, gb_sem.at[0])
    left = sum(sent)
    for rows in (2 * R, 256, 16):
        for lanes in (gbh.shape[1], 128):
            block = gbh.at[0:rows, 0:lanes]
            for _ in range(left // (2 * rows * lanes)):
                arrived(block, send_sem.at[0])
            left %= 2 * rows * lanes
    assert left == 0


def backward(cotangent, tokens, places, saved):
    F, S, H, L, X = geometry()
    R, D = tokens.shape
    wide, N, FF = D // S, R * S, saved[3].shape[2]
    pairs = wide // 128
    lead = max(X - 1, 1)
    width = 5 - X
    shapes = [(F, saved[i].shape[1], saved[i].shape[2] // 2) for i in (4, 3, 2, 1)]
    used = max(a + size for a, size in places.values())
    small_rows = -(-(-(-used // 128) + 1) // 8) * 8
    any_spec = pl.BlockSpec(memory_space=pl.ANY)
    vmem_spec = pl.BlockSpec(memory_space=pltpu.VMEM)
    V, D_SEM, shaped = pltpu.VMEM, pltpu.SemaphoreType.DMA, jax.ShapeDtypeStruct

    def each(shape_of, kind):
        return [V(shape_of(r, c // 4), kind) for f, r, c in shapes]

    res = pl.pallas_call(
        functools.partial(backward_kernel, places),
        out_shape=[shaped((R, D), bf16)]
        + [shaped((r, 2 * c), f32) for f, r, c in shapes]
        + [shaped((small_rows, 128), f32)],
        in_specs=[vmem_spec] + [any_spec] * 17,
        out_specs=[any_spec] * 5 + [vmem_spec],
        scratch_shapes=[V(s, bf16) for s in shapes]
        + each(lambda r, u: (lead, F, r, u), bf16)
        + each(lambda r, u: (L - 1, H, r, width * u), bf16)
        + each(lambda r, u: (H - 1, r, width * u), bf16)
        + each(lambda r, u: (r, 4 * u), bf16)
        + each(lambda r, u: (lead, r, 4 * u), bf16)
        + each(lambda r, u: (r, 4 * u), f32)
        + [
            V((2 * R, D // 2), bf16),
            V((2 * R, FF // 2), bf16),
            V((R, FF // 2), bf16),
            V((R, D), f32),
            V((R, D), bf16),
            V((2 * R, D // 2), bf16),
            V((S - 1, R, wide), bf16),
            V((N, wide), bf16),
            V((pairs, N, 384), bf16),
            V((R, 3 * D), bf16),
            V((2 * R, 3 * D // 2), bf16),
            V((8, D), f32),
            V((8, FF), f32),
            V(saved[0].shape, f32),
            V((8, D), f32),
            V((F, small_rows, 128), f32),
            V((F, small_rows, 128), f32),
            V((X, F, small_rows, 128), f32),
            V((F, small_rows, 128), f32),
            V((L, H, small_rows, 128), f32),
            V((max(H, F), small_rows, 128), f32),
            D_SEM((14,)),
            D_SEM((2, 4)),
            D_SEM((1,)),
            D_SEM((4, lead, F)),
            D_SEM((4, L - 1, H)),
            D_SEM((4, H - 1)),
            D_SEM((4, lead)),
            D_SEM((4,)),
            D_SEM((4,)),
            D_SEM((2,)),
            D_SEM((S - 1,)),
            D_SEM((S - 1, pairs, 3)),
            D_SEM((1,)),
            D_SEM((lead,)),
            D_SEM((L - 1, H)),
            D_SEM((H - 1,)),
            D_SEM((2,)),
        ],
        compiler_params=pltpu.CompilerParams(
            collective_id=2, has_side_effects=True, vmem_limit_bytes=63 * 2**20
        ),
    )(cotangent, tokens, *saved)
    return res[0], res[1:5], res[5]


def on_device(
    tokens, cotangent, ln1_gain, ln1_bias, w_qkv, b_qv, w_out, b_out,
    ln2_gain, ln2_bias, w_fc, b_fc, w_proj, b_proj,
):
    F, S = lax.axis_size("fsdp"), lax.axis_size("seq")
    row_count, D = tokens.shape
    named = dict(
        b_fc=b_fc, b_qv=b_qv, ln1_gain=ln1_gain, ln1_bias=ln1_bias, b_out=b_out,
        ln2_gain=ln2_gain, ln2_bias=ln2_bias, b_proj=b_proj,
    )
    places, at = {}, 0
    for name, value in named.items():
        places[name] = (at, value.shape[0])
        at += value.shape[0]
    small_rows = -(-at // 2048) * 16
    total = small_rows * 128
    flat = sum(
        jnp.pad(value, (a, total - a - size))
        for value, (a, size) in zip(named.values(), places.values())
    ).reshape(small_rows, 128)
    outs = forward(tokens, cotangent, flat, places, [w_qkv, w_out, w_fc, w_proj])
    wholes, saved, output, stats, cot_pair = outs[:4], outs[5:14], outs[14], outs[15], outs[16]
    grad_tokens, (grad_w_proj, grad_w_fc, grad_w_out, grad_w_qkv), reduced = backward(
        cotangent, tokens, places, [outs[4], *wholes, *saved, stats, cot_pair]
    )
    reduced = reduced.reshape(-1)
    got = {name: reduced[a : a + size] for name, (a, size) in places.items()}
    at = -(-at // 128) * 128
    rms_values = jnp.sqrt(reduced[at : at + 3] / float(row_count * D * S * F))
    return (
        output, grad_tokens, got["ln1_gain"], got["ln1_bias"], grad_w_qkv, got["b_qv"],
        grad_w_out, got["b_out"], got["ln2_gain"], got["ln2_bias"], grad_w_fc, got["b_fc"],
        grad_w_proj, got["b_proj"], rms_values,
    )


def solution(mesh):
    in_specs = (
        P(("fsdp", "seq"), None),
        P(("fsdp", "seq"), None),
        P("fsdp"),
        P("fsdp"),
        P("fsdp", None),
        P("fsdp"),
        P("fsdp", None),
        P("fsdp"),
        P("fsdp"),
        P("fsdp"),
        P("fsdp", None),
        P("fsdp"),
        P("fsdp", None),
        P("fsdp"),
    )
    out_specs = (
        P(("fsdp", "seq"), None),
        P(("fsdp", "seq"), None),
        P("fsdp"),
        P("fsdp"),
        P("fsdp", None),
        P("fsdp"),
        P("fsdp", None),
        P("fsdp"),
        P("fsdp"),
        P("fsdp"),
        P("fsdp", None),
        P("fsdp"),
        P("fsdp", None),
        P("fsdp"),
        P(),
    )
    return jax.shard_map(
        on_device, mesh=mesh, in_specs=in_specs, out_specs=out_specs, check_vma=False
    )
```

```python
import functools
import math

import jax
import jax.numpy as jnp
from jax import lax
from jax.experimental import pallas as pl
from jax.experimental.pallas import tpu as pltpu
from jax.sharding import PartitionSpec as P

BLK = 256
HD = 64
EPSILON = 1e-05
MESH = pl.DeviceIdType.MESH
f32, bf16 = jnp.float32, jnp.bfloat16

def geometry():
    F, S = lax.axis_size("fsdp"), lax.axis_size("seq")
    return F, S, 4, F // 4, S // 2


class Place:
    def __init__(self):
        self.F, self.S, self.H, self.L, self.X = geometry()
        self.f, self.s = lax.axis_index("fsdp"), lax.axis_index("seq")
        self.h, self.l = self.f // self.L, self.f % self.L
        self.x, self.c = self.s // 2, self.s % 2

    def shard(self, k, j):
        return lax.rem(self.h + self.H - k, self.H) * self.L + lax.rem(self.l + self.L - j, self.L)

    def hi(self, k):
        return (lax.rem(self.h + k, self.H) * self.L + self.l, self.s)

    def lo(self, j):
        return (self.h * self.L + lax.rem(self.l + j, self.L), self.s)

    def across(self, i):
        return (self.f, lax.rem(self.x + i, self.X) * 2 + self.c)

    def sibling(self):
        return (self.f, self.x * 2 + 1 - self.c)

    def everyone(self):
        return (
            [self.hi(k) for k in range(1, self.H)]
            + [self.lo(j) for j in range(1, self.L)]
            + [(self.f, lax.rem(self.s + i, self.S)) for i in range(1, self.S)]
        )


def greet(place):
    barrier = pltpu.get_barrier_semaphore()
    peers = place.everyone()
    for peer in peers:
        pl.semaphore_signal(barrier, inc=1, device_id=peer, device_id_type=MESH)
    pl.semaphore_wait(barrier, len(peers))


def vector(ref, places, name):
    at, size = places[name]
    parts = []
    for f in range(ref.shape[0]):
        pos = at
        while pos < at + size:
            row, lane = divmod(pos, 128)
            count = min(128 - lane, at + size - pos)
            parts.append(ref[f, row : row + 1, lane : lane + count])
            pos += count
    return jnp.concatenate(parts, axis=1)


def normalised(x):
    centre = x - jnp.mean(x, axis=-1, keepdims=True)
    return centre * lax.rsqrt(jnp.mean(centre * centre, axis=-1, keepdims=True) + EPSILON)


def gelu_and_slope(u):
    root = 0.7978845608028654
    square = u * u
    t = jnp.tanh(u * (root + root * 0.044715 * square))
    half = 0.5 * (1.0 + t)
    return u * half, half + u * (0.5 * (1.0 - t * t)) * (root + 3.0 * root * 0.044715 * square)


NT = (((1,), (1,)), ((), ()))
TN = (((0,), (0,)), ((), ()))


def head_lanes(shape, parity):
    lane = lax.broadcasted_iota(jnp.int32, shape, 1)
    return (lane // HD) == parity

def pick(rows, parity):
    return jnp.where(head_lanes(rows.shape, parity), rows, jnp.zeros_like(rows))

def turn(rows):
    return rows.astype(f32).T

def attend_block(i, wide, qkv, vT, scores, oT, lse):
    rows = pl.ds(i * BLK, BLK)
    @pl.loop(0, wide // HD)
    def _(h):
        pair = pl.multiple_of(h // 2 * 128, 128)
        q = pick(qkv[rows, pl.ds(pair, 128)], h % 2) * jnp.asarray(HD ** -0.5, bf16)
        top = jnp.full((8, BLK), -jnp.inf, f32)
        for j in range(i + 1):
            k = qkv[pl.ds(j * BLK, BLK), pl.ds(pl.multiple_of(wide + pair, 128), 128)]
            s = lax.dot_general(k, q, NT, preferred_element_type=f32)
            scores[pl.ds(j * BLK, BLK), :] = s
            top = jnp.maximum(top, jnp.max(s.reshape(BLK // 8, 8, BLK), axis=0))
        top = jnp.max(top, axis=0, keepdims=True)
        total = jnp.zeros((8, BLK), f32)
        out = jnp.zeros((HD, BLK), f32)
        for j in range(i + 1):
            p = jnp.exp(scores[pl.ds(j * BLK, BLK), :] - top)
            total = total + jnp.sum(p.reshape(BLK // 8, 8, BLK), axis=0)
            out = out + jnp.dot(vT[pl.ds(pl.multiple_of(h * HD, HD), HD), pl.ds(j * BLK, BLK)], p.astype(bf16), preferred_element_type=f32)
        total = jnp.sum(total, axis=0, keepdims=True)
        oT[pl.ds(pl.multiple_of(h * HD, HD), HD), :] = out * (1.0 / total)
        lse[pl.ds(h, 1), rows] = top + jnp.log(total)

def attend_back_block(i, pair, wide, qkv, grad, kT, lse, delta, dqT, dk, dv):
    rows = pl.ds(i * BLK, BLK)
    here = pl.ds(pair * 128, 128)

    @pl.loop(0, 128 // HD)
    def _(parity):
        h = pair * (128 // HD) + parity
        out_rows = pl.ds(pl.multiple_of(parity * HD, HD), HD)
        q = pick(qkv[rows, here], parity) * jnp.asarray(HD**-0.5, bf16)
        g = pick(grad[rows, here], parity)
        low = lse[pl.ds(h, 1), rows]
        mean = delta[pl.ds(h, 1), rows]
        out = jnp.zeros((HD, BLK), f32)
        for j in range(i + 1):
            keys = pl.ds(j * BLK, BLK)
            k = qkv[keys, wide + pair * 128 : wide + (pair + 1) * 128]
            v = qkv[keys, 2 * wide + pair * 128 : 2 * wide + (pair + 1) * 128]
            p = jnp.exp(lax.dot_general(k, q, NT, preferred_element_type=f32) - low)
            dp = lax.dot_general(v, g, NT, preferred_element_type=f32)
            ds = (p * (dp - mean)).astype(bf16)
            dv[keys, :] += jnp.dot(p.astype(bf16), g, preferred_element_type=f32)
            dk[keys, :] += jnp.dot(ds, q, preferred_element_type=f32)
            kT_rows = kT[pl.ds(pl.multiple_of(h * HD, HD), HD), keys]
            out = out + jnp.dot(kT_rows, ds, preferred_element_type=f32)
        dqT[out_rows, :] = out * HD**-0.5


SCHEDULE = (
    "s0",
    "H01 L00 s1 H02 L01 H03 L02 L03 H11 s2 H12 H13 x0 c0",
    "h21 l10 l11 l12 l13 h22 l20 s3 h23 l21",
    "l22 q22 h31",
    "l23 q23",
    "h32 x1",
    "c1",
    "h33",
    "",
    "",
    "x2 c2 p31 p32 p33 l30 q30 l31 q31",
    "l32 q32 l33 q33 x3 c3",
    "q10 q11 q12 q13 p21 p22 p23 q20 q21",
)


def forward_kernel(places, *refs):
    refs = list(refs)

    def take(count):
        got = refs[:count]
        del refs[:count]
        return got

    tokens, cot, small = take(3)
    shards = take(4)
    big_outs = take(4)
    (small_out, one_out, qkv_out, lse_out, heads_out, mixed_out, middle_out, two_out, act_out,
     slope_out, result_out, stats_out, cot_out) = take(13)
    wholes = take(4)
    (smalls, smalls_f, one, split, qkv, vT, scores, oT, lse, heads, mixed, middle, two, act, slope,
     result, stats, vectors, wide_bias) = take(19)
    (own_sem, send_sem, save_sem, hi_sem, lo_sem, x_sem, core_sem, sm_hi_sem, sm_lo_sem, there_sem,
     back_sem, pair_sem) = refs
    p = Place()
    S, H, L, X, F = p.S, p.H, p.L, p.X, p.F
    rows_here, D = tokens.shape
    wide = D // S
    saved = []

    def push(src, dst, sem, peer, kind=0):
        pltpu.make_async_remote_copy(
            src_ref=src, dst_ref=dst, send_sem=send_sem.at[kind], recv_sem=sem, device_id=peer,
            device_id_type=MESH,
        ).start()

    def arrived(dst, sem):
        pltpu.make_async_copy(dst, dst, sem).wait()

    def save(src, dst):
        cp = pltpu.make_async_copy(src, dst, save_sem.at[len(saved)])
        cp.start()
        saved.append(cp)

    def share(src, dst, index):
        save(src, dst.at[0:rows_here])
        push(src, dst.at[rows_here:], pair_sem.at[index], p.sibling())

    own = []
    for w in range(4):
        own.append(pltpu.make_async_copy(shards[w], wholes[w].at[p.f], own_sem.at[w]))
    own.append(pltpu.make_async_copy(small, smalls.at[p.f], own_sem.at[4]))
    for cp in own:
        cp.start()
    greet(p)

    wide_first = X == 2
    widths = [2 if wide_first and w == 0 else 5 - X for w in range(4)]
    onlys = [2 if wide_first and w == 0 else 1 for w in range(4)]

    def first(w, x):
        return x * 2 if wide_first and w == 0 else x

    def first_only(w, x):
        if wide_first and w == 0:
            return x * 2
        return x * (3 // (X - 1)) if X > 1 else x

    def fetched(w):
        return cols(w, first(w, p.x), widths[w])

    def cols(w, start, count):
        C = shards[w].shape[-1]
        return pl.ds(pl.multiple_of(p.c * (C // 2) + start * (C // 8), 128), count * (C // 8))

    def half(w, core):
        C = shards[w].shape[-1]
        return pl.ds(pl.multiple_of(core * (C // 2), 128), C // 2)

    def up():
        return ((p.h + 1) * L + p.l, p.s)

    def down():
        return ((p.h - 1) * L + p.l, p.s)

    def start(w):
        mine = fetched(w)
        src, dst = shards[w].at[:, mine], wholes[w].at[p.f, :, mine]

        @pl.when(p.h < H - 1)
        def _():
            push(src, dst, hi_sem.at[w, 0, 0], up(), 1)

        @pl.when(p.h > 0)
        def _():
            push(src, dst, hi_sem.at[w, 1, 0], down(), 1)

        for j in range(1, L):
            push(src, dst, lo_sem.at[w, j - 1, p.h], p.lo(j))

    def over_x(w, f):
        piece = wholes[w].at[f, :, cols(w, first_only(w, p.x), onlys[w])]
        for i in range(1, X):
            push(piece, piece, x_sem.at[w, i - 1, f], p.across(i))

    def from_hi(w, d, below):
        origin = p.h - d if below else p.h + d

        @pl.when(origin >= 0 if below else origin < H)
        def _():
            piece = wholes[w].at[origin * L + p.l, :, fetched(w)]
            side = 0 if below else 1
            arrived(piece, hi_sem.at[w, side, d - 1])
            if d < H - 1:

                @pl.when(p.h < H - 1 if below else p.h > 0)
                def _():
                    push(piece, piece, hi_sem.at[w, side, d], up() if below else down(), 1)

            for j in range(1, L):
                push(piece, piece, lo_sem.at[w, j - 1, origin], p.lo(j))

    def origins(visit, own):
        if own:
            visit(p.h)
        for d in range(1, H):

            @pl.when(p.h >= d)
            def _():
                visit(p.h - d)

            @pl.when(p.h + d < H)
            def _():
                visit(p.h + d)

    def from_lo(w, d, below):
        def visit(origin):
            for j in range(1, L):
                f = origin * L + lax.rem(p.l + L - j, L)
                arrived(wholes[w].at[f, :, fetched(w)], lo_sem.at[w, j - 1, origin])

        at_distance(d, below, visit)

    def at_distance(d, below, visit):
        if d == 0:
            visit(p.h)
            return
        origin = p.h - d if below else p.h + d
        pl.when(origin >= 0 if below else origin < H)(lambda: visit(origin))

    def out_x(w, d, below, lo):
        def visit(origin):
            for j in range(1, L) if lo else [0]:
                over_x(w, origin * L + lax.rem(p.l + L - j, L))

        at_distance(d, below, visit)

    def from_x(w, j):
        def visit(origin):
            f = origin * L + lax.rem(p.l + L - j, L)
            for i in range(1, X):
                theirs = cols(w, first_only(w, lax.rem(p.x + X - i, X)), onlys[w])
                arrived(wholes[w].at[f, :, theirs], x_sem.at[w, i - 1, f])
            piece = wholes[w].at[f, :, half(w, p.c)]
            push(piece, piece, core_sem.at[w, f], p.sibling())

        origins(visit, j > 0)

    def from_core(w):
        for j in range(L):

            def visit(origin):
                f = origin * L + lax.rem(p.l + L - j, L)
                arrived(wholes[w].at[f, :, half(w, 1 - p.c)], core_sem.at[w, f])

            origins(visit, j > 0)
        own[w].wait()
        save(wholes[w], big_outs[w])

    def run(names):
        for name in names.split():
            kind, w, d = name[0], int(name[1]), int(name[2:] or 0)
            sides = (True, False) if d else (True,)
            if kind == "s":
                start(w)
            elif kind == "x":
                for j in range(L):
                    from_x(w, j)
            elif kind == "c":
                from_core(w)
            else:
                for below in sides:
                    if kind in "hH":
                        from_hi(w, d, below)
                    if kind in "lL":
                        from_lo(w, d, below)
                    if kind in "pqHL":
                        out_x(w, d, below, kind in "qL")

    save(cot.at[:, pl.ds(pl.multiple_of(p.c * (D // 2), 128), D // 2)], cot_out.at[0:rows_here])
    push(
        cot.at[:, pl.ds(pl.multiple_of((1 - p.c) * (D // 2), 128), D // 2)],
        cot_out.at[rows_here:], pair_sem.at[4], p.sibling(),
    )
    for k in range(1, H):
        push(small, smalls.at[p.f], sm_hi_sem.at[k - 1], p.hi(k))
    for j in range(1, L):
        push(small, smalls.at[p.f], sm_lo_sem.at[j - 1, 0], p.lo(j))
    run(SCHEDULE[0])
    for k in range(1, H):
        piece = smalls.at[p.shard(k, 0)]
        arrived(piece, sm_hi_sem.at[k - 1])
        for j in range(1, L):
            push(piece, piece, sm_lo_sem.at[j - 1, k], p.lo(j))
    for j in range(1, L):
        for k in range(H):
            arrived(smalls.at[p.shard(k, j)], sm_lo_sem.at[j - 1, k])
    own[4].wait()
    smalls_f[...] = smalls[...].astype(f32)
    save(smalls_f, small_out)
    vec = functools.partial(vector, smalls_f, places)

    chunk = 128
    stats[...] = jnp.zeros_like(stats)
    gain, shift = vec("ln1_gain"), vec("ln1_bias")

    @pl.loop(0, rows_here // chunk)
    def _(t):
        at = pl.ds(pl.multiple_of(t * chunk, chunk), chunk)
        x = tokens[at, :].astype(f32)
        stats[0:1, :] += jnp.sum(x * x, axis=0, keepdims=True)
        one[at, :] = (normalised(x) * gain + shift).astype(bf16)

    share(one, one_out, 0)
    run(SCHEDULE[1])

    bias_qv = vec("b_qv")

    def project(kind, target):
        at = pl.multiple_of(kind * D + target * wide, 128)
        w = wholes[0][:, :, pl.ds(at, wide)].reshape(D, wide)
        return jnp.dot(one[...], w, preferred_element_type=f32)

    vectors[0:1, :] = bias_qv[:, :D]
    vectors[1:2, :] = bias_qv[:, D:]

    def heads_of(target):
        lanes = pl.ds(pl.multiple_of(target * wide, 128), wide)
        return [
            (project(0, target) + vectors[0:1, lanes]).astype(bf16),
            project(1, target).astype(bf16),
            (project(2, target) + vectors[1:2, lanes]).astype(bf16),
        ]

    mine = pl.ds(pl.multiple_of(p.s * rows_here, 128), rows_here)
    for i in list(range(1, S)) + [0]:
        target = lax.rem(p.s + i, S)
        for kind, values in enumerate(heads_of(target)):
            if i == 0:
                qkv[mine, kind * wide : (kind + 1) * wide] = values
            else:
                split[i - 1, :, kind * wide : (kind + 1) * wide] = values
        if i:
            push(split.at[i - 1], qkv.at[mine, :], there_sem.at[i - 1], (p.f, target))
    run(SCHEDULE[2])
    for i in range(1, S):
        source = lax.rem(p.s + S - i, S)
        arrived(qkv.at[pl.ds(pl.multiple_of(source * rows_here, 128), rows_here), :], there_sem.at[i - 1])
    save(qkv, qkv_out)
    run(SCHEDULE[12])

    length = qkv.shape[0]
    blocks = length // BLK
    for b in range(blocks):
        at = pl.ds(b * BLK, BLK)
        vT[:, at] = turn(qkv[at, 2 * wide :]).astype(bf16)
    lse[...] = jnp.zeros_like(lse)
    sent_back = 0
    for i in range(blocks):
        attend_block(i, wide, qkv, vT, scores, oT, lse)
        heads[pl.ds(i * BLK, BLK), :] = turn(oT[...]).astype(bf16)
        while (sent_back + 1) * rows_here <= (i + 1) * BLK:
            rows = pl.ds(sent_back * rows_here, rows_here)
            lanes = pl.ds(pl.multiple_of(p.s * wide, 128), wide)

            @pl.when(p.s != sent_back)
            def _():
                pltpu.make_async_remote_copy(
                    src_ref=heads.at[rows], dst_ref=mixed.at[:, lanes], send_sem=send_sem.at[2],
                    recv_sem=back_sem.at[p.s], device_id=(p.f, jnp.int32(sent_back)),
                    device_id_type=MESH,
                ).start()

            @pl.when(p.s == sent_back)
            def _():
                mixed[:, lanes] = heads[rows, :]

            sent_back += 1
        if i % (blocks // 6) == 0:
            run(SCHEDULE[3 + i // (blocks // 6)])
    save(heads, heads_out)
    save(lse, lse_out)
    run(SCHEDULE[9])
    for i in range(1, S):
        source = lax.rem(p.s + S - i, S)
        arrived(mixed.at[:, pl.ds(pl.multiple_of(source * wide, 128), wide)], back_sem.at[source])
    share(mixed, mixed_out, 1)

    tile = 256
    vectors[0:1, :] = vec("b_out")

    @pl.loop(0, D // tile)
    def _(t):
        at = pl.ds(pl.multiple_of(t * tile, tile), tile)
        w = wholes[1][:, :, at].reshape(D, tile)
        branch = jnp.dot(mixed[...], w, preferred_element_type=f32) + vectors[0:1, at]
        middle[:, at] = tokens[:, at].astype(f32) + branch

    save(middle, middle_out)
    gain_two, shift_two = vec("ln2_gain"), vec("ln2_bias")

    @pl.loop(0, rows_here // chunk)
    def _(t):
        at = pl.ds(pl.multiple_of(t * chunk, chunk), chunk)
        x = middle[at, :]
        stats[1:2, :] += jnp.sum(x * x, axis=0, keepdims=True)
        two[at, :] = (normalised(x) * gain_two + shift_two).astype(bf16)

    share(two, two_out, 2)
    run(SCHEDULE[10])
    wide_bias[0:1, :] = vec("b_fc")

    FF = act.shape[1]

    @pl.loop(0, FF // tile)
    def _(t):
        at = pl.ds(pl.multiple_of(t * tile, tile), tile)
        w = wholes[2][:, :, at].reshape(D, tile)
        u = jnp.dot(two[...], w, preferred_element_type=f32) + wide_bias[0:1, at]
        act_rows, slope_rows = gelu_and_slope(u)
        act[:, at] = act_rows.astype(bf16)
        slope[:, at] = slope_rows.astype(bf16)

    share(act, act_out, 3)
    save(slope, slope_out)
    run(SCHEDULE[11])
    vectors[0:1, :] = vec("b_proj")

    @pl.loop(0, D // tile)
    def _(t):
        at = pl.ds(pl.multiple_of(t * tile, tile), tile)
        w = wholes[3][:, :, at].reshape(FF, tile)
        stream = middle[:, at] + (jnp.dot(act[...], w, preferred_element_type=f32) + vectors[0:1, at])
        stats[2:3, at] = jnp.sum(stream * stream, axis=0, keepdims=True)
        result[:, at] = stream.astype(bf16)

    save(result, result_out)
    save(stats, stats_out)
    for index, there in enumerate((one_out, mixed_out, two_out, act_out, cot_out)):
        arrived(there.at[rows_here:], pair_sem.at[index])
    moves = jnp.where(p.h < H - 1, p.h + 1, 0) + jnp.where(p.h > 0, H - p.h, 0)
    for w in range(4):
        piece = wholes[w].at[0, :, fetched(w)]

        @pl.loop(0, moves)
        def _(_):
            arrived(piece, send_sem.at[1])

        for _ in range(H * (L - 1)):
            arrived(piece, send_sem.at[0])
        for _ in range((F - 1) * (X - 1)):
            arrived(wholes[w].at[0, :, cols(w, 0, onlys[w])], send_sem.at[0])
        for _ in range(F - 1):
            arrived(wholes[w].at[0, :, half(w, 0)], send_sem.at[0])
    for _ in range(H - 1 + H * (L - 1)):
        arrived(smalls.at[0], send_sem.at[0])
    for i in range(S - 1):
        arrived(split.at[i], send_sem.at[0])
        arrived(heads.at[pl.ds(0, rows_here)], send_sem.at[2])
    for there in (one_out, mixed_out, two_out, act_out, cot_out):
        arrived(there.at[rows_here:], send_sem.at[0])
    for cp in saved:
        cp.wait()


def forward(tokens, cotangent, packed, places, shards):
    F, S, H, L, X = geometry()
    rows_here, D = tokens.shape
    wide, length, FF = D // S, rows_here * S, shards[2].shape[1]
    heads = max(8, wide // HD)
    lead = max(X - 1, 1)
    any_spec = pl.BlockSpec(memory_space=pl.ANY)
    V, D_SEM = pltpu.VMEM, pltpu.SemaphoreType.DMA
    shaped = jax.ShapeDtypeStruct
    wholes = [(F,) + a.shape for a in shards]
    outs = [shaped(s, bf16) for s in wholes] + [
        shaped((F,) + packed.shape, f32),
        shaped((2 * rows_here, D), bf16),
        shaped((length, 3 * wide), bf16),
        shaped((heads, length), f32),
        shaped((length, wide), bf16),
        shaped((2 * rows_here, D), bf16),
        shaped((rows_here, D), f32),
        shaped((2 * rows_here, D), bf16),
        shaped((2 * rows_here, FF), bf16),
        shaped((rows_here, FF), bf16),
        shaped((rows_here, D), bf16),
        shaped((8, D), f32),
        shaped((2 * rows_here, D // 2), bf16),
    ]
    return pl.pallas_call(
        functools.partial(forward_kernel, places),
        out_shape=outs,
        in_specs=[pl.BlockSpec(memory_space=pltpu.VMEM)] + [any_spec] * 6,
        out_specs=[any_spec] * len(outs),
        scratch_shapes=[V(s, bf16) for s in wholes]
        + [
            V((F,) + packed.shape, bf16),
            V((F,) + packed.shape, f32),
            V((rows_here, D), bf16),
            V((S - 1, rows_here, 3 * wide), bf16),
            V((length, 3 * wide), bf16),
            V((wide, length), bf16),
            V((length, BLK), f32),
            V((wide, BLK), f32),
            V((heads, length), f32),
            V((length, wide), bf16),
            V((rows_here, D), bf16),
            V((rows_here, D), f32),
            V((rows_here, D), bf16),
            V((rows_here, FF), bf16),
            V((rows_here, FF), bf16),
            V((rows_here, D), bf16),
            V((8, D), f32),
            V((8, D), f32),
            V((8, FF), f32),
            D_SEM((5,)),
            D_SEM((3,)),
            D_SEM((len(outs) + 8,)),
            D_SEM((4, 2, H - 1)),
            D_SEM((4, L - 1, H)),
            D_SEM((4, lead, F)),
            D_SEM((4, F)),
            D_SEM((H - 1,)),
            D_SEM((L - 1, H)),
            D_SEM((S - 1,)),
            D_SEM((S,)),
            D_SEM((5,)),
        ],
        compiler_params=pltpu.CompilerParams(
            collective_id=1, has_side_effects=True, vmem_limit_bytes=60 * 2**20
        ),
    )(tokens, cotangent, packed, *shards)


BACK = dict(
    feed=("", "x0", "", "x1", "y0", "x2", "y1", "x3"),
    norm="z0 y2",
    mixed="",
    fc=("", "x4", "z1 y3", "x5"),
    out=("", "", "", ""),
    attention=("z2 y4", "x6", "", "z3 y5", "v0 x7", "", "z4 y6", "e0", "", "z5 y7", "x8 x9 x10 x11", ""),
    sent="z6 y8",
    back="z7 y9 z8 y10",
    qkv=("x12", "x13 z9 y11", "x14 z10 y12", "x15 z11 y13 v1"),
    input="v2 z12 y14",
    norm1="z13 y15 e1 e2",
    small="z14 z15 v3",
    end="e3",
)


def backward_kernel(places, *refs):
    refs = list(refs)

    def take(count):
        got = refs[:count]
        del refs[:count]
        return got

    cot, = take(1)
    (tokens, smalls, wq_in, wo_in, wf_in, wp_in, one_in, qkv_in, lse_in, heads_in, mixed_in,
     middle_in, two_in, act_in, slope_in, stats, cot_in) = take(17)
    grad_tokens, = take(1)
    outs = take(4)
    small_out, = take(1)
    parts, from_x, from_lo, from_hi, value, from_x_end, half_out = (take(4) for _ in range(7))
    (cot_pair, gbh, gb_other, grad_middle, branch, branch_pair, leaving, grad_heads, grad_qkv,
     grad_proj, proj_pair, sums, fc_sum, smalls_f, stats_v) = take(15)
    sm_mine, sm_core, sm_x, sm_sum, sm_lo, sm_hi = take(6)
    (load_sem, slot_sem, send_sem, x_sem, lo_sem, hi_sem, end_sem, out_sem, core_sem, pair_sem, to_sem,
     from_sem, sm_sem, smx_sem, smlo_sem, smhi_sem, gb_sem) = refs
    p = Place()
    S, H, L, X, F = p.S, p.H, p.L, p.X, p.F
    R, D = cot.shape
    FF = fc_sum.shape[1]
    wide = D // S
    N = R * S
    width = 5 - X
    step = 3 // (X - 1) if X > 1 else 0
    sent = []

    def push(src, dst, sem, peer):
        pltpu.make_async_remote_copy(
            src_ref=src, dst_ref=dst, send_sem=send_sem.at[0], recv_sem=sem, device_id=peer,
            device_id_type=MESH,
        ).start()
        sent.append(math.prod(src.shape) * src.dtype.itemsize)

    def arrived(dst, sem):
        pltpu.make_async_copy(dst, dst, sem).wait()

    loads = {}

    def load(index, src, dst):
        loads[index] = pltpu.make_async_copy(src, dst, load_sem.at[index])
        loads[index].start()

    def unit(w):
        return parts[w].shape[-1] // 4

    def span(w, start, count):
        return pl.ds(pl.multiple_of(start * unit(w), 128), count * unit(w))

    def ahead(k, j):
        return lax.rem(p.h + k, H) * L + lax.rem(p.l + j, L)

    steps = list(range(1, H)) + [0]
    slots = [(w, k) for w in range(4) for k in steps]

    def shards_of(k):
        return pl.ds(lax.rem(p.h + k, H) * L, L)

    def send_x(w, k):
        for i in range(1, X):
            push(
                parts[w].at[shards_of(k), :, span(w, lax.rem(p.x + i, X) * step, 1)],
                from_x[w].at[i - 1, shards_of(k)], x_sem.at[w, i - 1, k], p.across(i),
            )

    def send_lo(w, k):
        cols = span(w, p.x * step, 1)
        if X > 1:
            total = parts[w][shards_of(k), :, cols].astype(f32)
            for i in range(1, X):
                came = from_x[w].at[i - 1, shards_of(k)]
                arrived(came, x_sem.at[w, i - 1, k])
                total = total + came[...].astype(f32)
            parts[w][shards_of(k), :, cols] = total.astype(bf16)
        for j in range(1, L):
            push(
                parts[w].at[ahead(k, j), :, span(w, p.x, width)],
                from_lo[w].at[j - 1, lax.rem(p.h + k, H)], lo_sem.at[w, j - 1, k], p.lo(j),
            )

    def add_lo(w, k):
        f = ahead(k, 0)
        cols = span(w, p.x, width)
        total = parts[w][f, :, cols].astype(f32)
        for j in range(1, L):
            came = from_lo[w].at[j - 1, lax.rem(p.h + k, H)]
            arrived(came, lo_sem.at[w, j - 1, k])
            total = total + came[...].astype(f32)
        parts[w][f, :, cols] = total.astype(bf16)
        if k > 0:
            push(parts[w].at[f, :, cols], from_hi[w].at[k - 1], hi_sem.at[w, k - 1], p.hi(k))

    def add_hi(w):
        cols = span(w, p.x, width)
        total = parts[w][p.f, :, cols].astype(f32)
        for k in range(1, H):
            arrived(from_hi[w].at[k - 1], hi_sem.at[w, k - 1])
            total = total + from_hi[w][k - 1].astype(f32)
        value[w][:, cols] = total.astype(bf16)
        for i in range(1, X):
            push(
                value[w].at[:, cols], from_x_end[w].at[i - 1, :, cols], end_sem.at[w, i - 1],
                p.across(i),
            )

    def finish(w):
        mine = span(w, p.x * step, 1)
        half_out[w][:, mine] = value[w][:, mine].astype(f32)
        for i in range(1, X):
            source = lax.rem(p.x + X - i, X)
            cols = span(w, source, width)
            arrived(from_x_end[w].at[i - 1, :, cols], end_sem.at[w, i - 1])
            theirs = span(w, source * step, 1)
            half_out[w][:, theirs] = from_x_end[w][i - 1, :, theirs].astype(f32)
        if X < 4:
            both = pl.ds(unit(w), (4 - X) * unit(w))
            total = value[w][:, both].astype(f32)
            for i in range(1, X):
                total = total + from_x_end[w][i - 1, :, both].astype(f32)
            half_out[w][:, both] = total
        there = outs[w].at[:, pl.ds(pl.multiple_of(p.c * 4 * unit(w), 128), 4 * unit(w))]
        push(half_out[w], there, core_sem.at[w], p.sibling())
        pltpu.make_async_copy(half_out[w], there, out_sem.at[w]).start()

    ran = []

    def run(names):
        for name in names.split():
            kind, n = name[0], int(name[1:])
            ran.append(name)
            if kind == "x":
                send_x(*slots[n])
            elif kind == "y":
                send_lo(*slots[n])
            elif kind == "z":
                add_lo(*slots[n])
            elif kind == "v":
                add_hi(n)
            else:
                finish(n)

    load(0, cot_in, cot_pair)
    load(1, smalls, smalls_f)
    load(2, stats, stats_v)
    greet(p)

    tile = FF // F
    grad_middle[...] = jnp.zeros_like(grad_middle)
    loads[0].wait()

    def feed_forward(wp, wf, act, slope):
        tiles = [lax.rem(p.h + k, H) * L + j for k in steps for j in range(L)]

        def fetch(t, f):
            slot = t % 2
            cols = pl.ds(pl.multiple_of(f * tile, 128), tile)
            return [
                pltpu.make_async_copy(wp_in.at[f], wp.at[slot], slot_sem.at[slot, 0]),
                pltpu.make_async_copy(wf_in.at[:, :, cols], wf.at[slot], slot_sem.at[slot, 1]),
                pltpu.make_async_copy(act_in.at[:, cols], act.at[slot], slot_sem.at[slot, 2]),
                pltpu.make_async_copy(slope_in.at[:, cols], slope.at[slot], slot_sem.at[slot, 3]),
            ]

        coming = fetch(0, tiles[0])
        for cp in coming:
            cp.start()
        for t, f in enumerate(tiles):
            for cp in coming:
                cp.wait()
            if t + 1 < len(tiles):
                coming = fetch(t + 1, tiles[t + 1])
                for cp in coming:
                    cp.start()
            slot = t % 2
            parts[0][f] = lax.dot_general(
                act[slot], cot_pair[...], TN, preferred_element_type=f32
            ).astype(bf16)
            grad_act = lax.dot_general(cot[...], wp[slot], NT, preferred_element_type=f32)
            before = (slope[slot].astype(f32) * grad_act).astype(bf16)
            fc_sum[0:1, pl.ds(pl.multiple_of(f * tile, 128), tile)] = jnp.sum(
                before.astype(f32), axis=0, keepdims=True
            )
            at = pl.ds(pl.multiple_of(lax.rem(f, F // 2) * tile, 128), tile)

            @pl.when(f // (F // 2) == p.c)
            def _():
                gbh[0:R, at] = before

            @pl.when(f // (F // 2) != p.c)
            def _():
                gb_other[:, at] = before
                pltpu.make_async_remote_copy(
                    src_ref=gb_other.at[:, at], dst_ref=gbh.at[R : 2 * R, at], send_sem=gb_sem.at[0],
                    recv_sem=gb_sem.at[1], device_id=p.sibling(), device_id_type=MESH,
                ).start()

            grad_middle[...] += lax.dot_general(
                before, wf[slot].reshape(D, tile), NT, preferred_element_type=f32
            )
            if (2 * t + 2) % L == 0:
                run(BACK["feed"][(2 * t + 2) // L - 1])

    pl.run_scoped(
        feed_forward,
        pltpu.VMEM((2,) + wp_in.shape[1:], bf16),
        pltpu.VMEM((2,) + wf_in.shape[:2] + (tile,), bf16),
        pltpu.VMEM((2, 2 * R, tile), bf16),
        pltpu.VMEM((2, R, tile), bf16),
    )

    chunk = 128
    sums[...] = jnp.zeros_like(sums)
    loads[1].wait()
    loads[2].wait()

    def norm_back(rows, grad, gain, first):
        centre = rows - jnp.mean(rows, axis=-1, keepdims=True)
        scale = lax.rsqrt(jnp.mean(centre * centre, axis=-1, keepdims=True) + EPSILON)
        n = centre * scale
        sums[first : first + 1, :] += jnp.sum(grad * n, axis=0, keepdims=True)
        sums[first + 1 : first + 2, :] += jnp.sum(grad, axis=0, keepdims=True)
        scaled = grad * gain
        return scale * (
            scaled
            - jnp.mean(scaled, axis=-1, keepdims=True)
            - n * jnp.mean(scaled * n, axis=-1, keepdims=True)
        )

    def weight_grad(w, rows_pair, columns_pair, hook):
        r = parts[w].shape[1]
        for t, k in enumerate(steps):
            at = pl.ds(pl.multiple_of(lax.rem(p.h + k, H) * (L * r), 128), L * r)
            grad = lax.dot_general(
                rows_pair[:, at], columns_pair[...], TN, preferred_element_type=f32
            )
            parts[w][shards_of(k)] = grad.astype(bf16).reshape(L, r, grad.shape[1])
            run(BACK[hook][t])

    def attention_output(middle, wo, two, mixed):
        load(3, middle_in, middle)
        load(4, wo_in, wo)
        load(5, two_in, two)
        load(6, mixed_in, mixed)
        gain = vector(smalls_f, places, "ln2_gain")
        loads[3].wait()

        @pl.loop(0, R // chunk)
        def _(t):
            at = pl.ds(pl.multiple_of(t * chunk, chunk), chunk)
            out = cot[at, :].astype(f32)
            sums[5:6, :] += jnp.sum(out, axis=0, keepdims=True)
            total = out + norm_back(middle[at, :], grad_middle[at, :], gain, 0)
            grad_middle[at, :] = total
            rounded = total.astype(bf16)
            branch[at, :] = rounded
            sums[4:5, :] += jnp.sum(rounded.astype(f32), axis=0, keepdims=True)

        half = D // 2
        run(BACK["norm"])
        branch_pair[0:R, :] = branch[:, pl.ds(pl.multiple_of(p.c * half, 128), half)]
        push(
            branch.at[:, pl.ds(pl.multiple_of((1 - p.c) * half, 128), half)],
            branch_pair.at[R : 2 * R, :], pair_sem.at[0], p.sibling(),
        )
        loads[4].wait()
        r = wo.shape[1]
        mine = pl.ds(pl.multiple_of(p.s * R, 128), R)
        for i in list(range(1, S)) + [0]:
            target = lax.rem(p.s + i, S)
            rows = wo[pl.ds(target * (wide // r), wide // r)].reshape(wide, D)
            grad = lax.dot_general(branch[...], rows, NT, preferred_element_type=f32).astype(bf16)
            if i:
                leaving[i - 1] = grad
                push(leaving.at[i - 1], grad_heads.at[mine, :], to_sem.at[i - 1], (p.f, target))
            else:
                grad_heads[mine, :] = grad
        run(BACK["mixed"])
        loads[5].wait()
        arrived(gbh.at[R : 2 * R, :], gb_sem.at[1])
        weight_grad(1, two, gbh, "fc")
        loads[6].wait()
        arrived(branch_pair.at[R : 2 * R, :], pair_sem.at[0])
        weight_grad(2, mixed, branch_pair, "out")

    pl.run_scoped(
        attention_output,
        pltpu.VMEM((R, D), f32),
        pltpu.VMEM(wo_in.shape, bf16),
        pltpu.VMEM((2 * R, D), bf16),
        pltpu.VMEM((2 * R, D), bf16),
    )

    pairs = wide // 128

    def attention(qkv, heads, lse, kT, delta, dqT, dk, dv):
        load(7, qkv_in, qkv)
        load(8, heads_in, heads)
        load(9, lse_in, lse)
        for i in range(1, S):
            source = lax.rem(p.s + S - i, S)
            arrived(grad_heads.at[pl.ds(pl.multiple_of(source * R, 128), R), :], to_sem.at[i - 1])
        for index in (7, 8, 9):
            loads[index].wait()
        shape = (lse.shape[0], wide)
        chosen = lax.broadcasted_iota(jnp.int32, shape, 1) // HD == lax.broadcasted_iota(jnp.int32, shape, 0)
        chosen = jnp.where(chosen, 1.0, 0.0).astype(bf16)
        for b in range(N // BLK):
            at = pl.ds(b * BLK, BLK)
            kT[:, at] = turn(qkv[at, wide : 2 * wide]).astype(bf16)
            product = grad_heads[at, :].astype(f32) * heads[at, :].astype(f32)
            high = product.astype(bf16)
            low = (product - high.astype(f32)).astype(bf16)
            delta[:, at] = lax.dot_general(chosen, high, NT, preferred_element_type=f32) + lax.dot_general(
                chosen, low, NT, preferred_element_type=f32
            )
        for pair in range(pairs):
            dk[...] = jnp.zeros_like(dk)
            dv[...] = jnp.zeros_like(dv)
            for i in range(N // BLK):
                attend_back_block(i, pair, wide, qkv, grad_heads, kT, lse, delta, dqT, dk, dv)
                grad_qkv[pair, pl.ds(i * BLK, BLK), 0:128] = turn(dqT[...]).astype(bf16)
                at = (pair * (N // BLK) + i) * 12 // (pairs * (N // BLK))
                run(BACK["attention"][at] if at not in passed else "")
                passed.add(at)
            grad_qkv[pair, :, 128:256] = dk[...].astype(bf16)
            grad_qkv[pair, :, 256:384] = dv[...].astype(bf16)
            for i in list(range(1, S)) + [0]:
                target = lax.rem(p.s + i, S)
                rows = pl.ds(pl.multiple_of(target * R, 128), R)
                for kind in range(3):
                    lanes = pl.ds(pl.multiple_of(kind * D + p.s * wide + pair * 128, 128), 128)
                    block = grad_qkv.at[pair, rows, kind * 128 : (kind + 1) * 128]
                    if i:
                        push(block, grad_proj.at[:, lanes], from_sem.at[i - 1, pair, kind], (p.f, target))
                    else:
                        grad_proj[:, lanes] = block[...]
        run(BACK["sent"])

    passed = set()
    pl.run_scoped(
        attention,
        pltpu.VMEM((N, 3 * wide), bf16),
        pltpu.VMEM((N, wide), bf16),
        pltpu.VMEM(lse_in.shape, f32),
        pltpu.VMEM((wide, N), bf16),
        pltpu.VMEM(lse_in.shape, f32),
        pltpu.VMEM((128, BLK), f32),
        pltpu.VMEM((N, 128), f32),
        pltpu.VMEM((N, 128), f32),
    )

    def projections(wq, one, tokens_v, result, qv_sum):
        load(10, wq_in, wq)
        load(11, one_in, one)
        load(12, tokens, tokens_v)
        for i in range(1, S):
            source = lax.rem(p.s + S - i, S)
            for pair in range(pairs):
                for kind in range(3):
                    lanes = pl.ds(pl.multiple_of(kind * D + source * wide + pair * 128, 128), 128)
                    arrived(grad_proj.at[:, lanes], from_sem.at[i - 1, pair, kind])
        run(BACK["back"])
        half = 3 * D // 2
        push(
            grad_proj.at[:, pl.ds(pl.multiple_of((1 - p.c) * half, 128), half)],
            proj_pair.at[R : 2 * R, :], pair_sem.at[1], p.sibling(),
        )
        proj_pair[0:R, :] = grad_proj[:, pl.ds(pl.multiple_of(p.c * half, 128), half)]
        qv_sum[0:1, 0:D] = jnp.sum(grad_proj[:, 0:D].astype(f32), axis=0, keepdims=True)
        qv_sum[0:1, D:] = jnp.sum(grad_proj[:, 2 * D :].astype(f32), axis=0, keepdims=True)
        loads[11].wait()
        arrived(proj_pair.at[R : 2 * R, :], pair_sem.at[1])
        weight_grad(3, one, proj_pair, "qkv")
        run(BACK["input"])
        loads[10].wait()
        rows = 256
        r = wq.shape[1]

        @pl.loop(0, D // rows)
        def _(t):
            w = wq[pl.ds(t * (rows // r), rows // r)].reshape(rows, 3 * D)
            result[:, pl.ds(pl.multiple_of(t * rows, rows), rows)] = lax.dot_general(
                grad_proj[...], w, NT, preferred_element_type=f32
            )

        run(BACK["norm1"])
        loads[12].wait()
        gain = vector(smalls_f, places, "ln1_gain")

        @pl.loop(0, R // chunk)
        def _(t):
            at = pl.ds(pl.multiple_of(t * chunk, chunk), chunk)
            moved = norm_back(tokens_v[at, :].astype(f32), result[at, :], gain, 2)
            tokens_v[at, :] = (grad_middle[at, :] + moved).astype(bf16)

        cp = pltpu.make_async_copy(tokens_v, grad_tokens, load_sem.at[13])
        cp.start()
        values = dict(
            ln2_gain=sums[0:1, :], ln2_bias=sums[1:2, :], ln1_gain=sums[2:3, :],
            ln1_bias=sums[3:4, :], b_out=sums[4:5, :], b_proj=sums[5:6, :], b_fc=fc_sum[0:1, :],
            b_qv=qv_sum[0:1, :],
        )
        sm_mine[...] = jnp.zeros_like(sm_mine)
        last = 0
        for name, (start, size) in places.items():
            whole = values[name]
            for f in range(F):
                pos = start
                while pos < start + size:
                    row, lane = divmod(pos, 128)
                    count = min(128 - lane, start + size - pos)
                    at = f * size + pos - start
                    sm_mine[f, row : row + 1, lane : lane + count] = whole[:, at : at + count]
                    pos += count
            last = max(last, start + size)
        row = -(-last // 128)
        lane = lax.broadcasted_iota(jnp.int32, (1, 128), 1)
        line = jnp.zeros((1, 128), f32)
        for i in range(3):
            line = jnp.where(lane == i, jnp.sum(stats_v[i : i + 1, :], axis=1, keepdims=True), line)
        for f in range(F):
            sm_mine[f, row : row + 1, :] = line
        push(sm_mine, sm_core, sm_sem.at[0], p.sibling())
        run(BACK["small"])
        arrived(sm_core, sm_sem.at[0])
        sm_x[p.x] = sm_mine[...] + sm_core[...]
        for i in range(1, X):
            push(sm_x.at[p.x], sm_x.at[p.x], smx_sem.at[i - 1], p.across(i))
        cp.wait()

    pl.run_scoped(
        projections,
        pltpu.VMEM(wq_in.shape, bf16),
        pltpu.VMEM((2 * R, D), bf16),
        pltpu.VMEM((R, D), bf16),
        pltpu.VMEM((R, D), f32),
        pltpu.VMEM((8, 2 * D), f32),
    )
    for i in range(1, X):
        arrived(sm_x.at[lax.rem(p.x + X - i, X)], smx_sem.at[i - 1])
    total = sm_x[0]
    for i in range(1, X):
        total = total + sm_x[i]
    sm_sum[...] = total
    for j in range(1, L):
        for k in range(H):
            h = lax.rem(p.h + k, H)
            push(sm_sum.at[ahead(k, j)], sm_lo.at[p.l, h], smlo_sem.at[j - 1, k], p.lo(j))
    run(BACK["end"])
    assert len(set(ran)) == len(ran) == 3 * len(slots) + 8
    for k in list(range(1, H)) + [0]:
        h = lax.rem(p.h + k, H)
        sm_lo[p.l, h] = sm_sum[h * L + p.l]
        for j in range(1, L):
            arrived(sm_lo.at[lax.rem(p.l + L - j, L), h], smlo_sem.at[j - 1, k])
        total = sm_lo[0, h]
        for j in range(1, L):
            total = total + sm_lo[j, h]
        if k > 0:
            sm_core[h] = total
            push(sm_core.at[h], sm_hi.at[p.h], smhi_sem.at[k - 1], p.hi(k))
        else:
            sm_hi[p.h] = total
    for k in range(1, H):
        arrived(sm_hi.at[lax.rem(p.h + H - k, H)], smhi_sem.at[k - 1])
    total = sm_hi[0]
    for k in range(1, H):
        total = total + sm_hi[k]
    small_out[...] = total
    for w in range(4):
        arrived(half_out[w], core_sem.at[w])
        arrived(half_out[w], out_sem.at[w])
    arrived(gb_other, gb_sem.at[0])
    left = sum(sent)
    for rows in (2 * R, 256, 16):
        for lanes in (gbh.shape[1], 128):
            block = gbh.at[0:rows, 0:lanes]
            for _ in range(left // (2 * rows * lanes)):
                arrived(block, send_sem.at[0])
            left %= 2 * rows * lanes
    assert left == 0


def backward(cotangent, tokens, places, saved):
    F, S, H, L, X = geometry()
    R, D = tokens.shape
    wide, N, FF = D // S, R * S, saved[3].shape[2]
    pairs = wide // 128
    lead = max(X - 1, 1)
    width = 5 - X
    shapes = [(F, saved[i].shape[1], saved[i].shape[2] // 2) for i in (4, 3, 2, 1)]
    used = max(a + size for a, size in places.values())
    small_rows = -(-(-(-used // 128) + 1) // 8) * 8
    any_spec = pl.BlockSpec(memory_space=pl.ANY)
    vmem_spec = pl.BlockSpec(memory_space=pltpu.VMEM)
    V, D_SEM, shaped = pltpu.VMEM, pltpu.SemaphoreType.DMA, jax.ShapeDtypeStruct

    def each(shape_of, kind):
        return [V(shape_of(r, c // 4), kind) for f, r, c in shapes]

    res = pl.pallas_call(
        functools.partial(backward_kernel, places),
        out_shape=[shaped((R, D), bf16)]
        + [shaped((r, 2 * c), f32) for f, r, c in shapes]
        + [shaped((small_rows, 128), f32)],
        in_specs=[vmem_spec] + [any_spec] * 17,
        out_specs=[any_spec] * 5 + [vmem_spec],
        scratch_shapes=[V(s, bf16) for s in shapes]
        + each(lambda r, u: (lead, F, r, u), bf16)
        + each(lambda r, u: (L - 1, H, r, width * u), bf16)
        + each(lambda r, u: (H - 1, r, width * u), bf16)
        + each(lambda r, u: (r, 4 * u), bf16)
        + each(lambda r, u: (lead, r, 4 * u), bf16)
        + each(lambda r, u: (r, 4 * u), f32)
        + [
            V((2 * R, D // 2), bf16),
            V((2 * R, FF // 2), bf16),
            V((R, FF // 2), bf16),
            V((R, D), f32),
            V((R, D), bf16),
            V((2 * R, D // 2), bf16),
            V((S - 1, R, wide), bf16),
            V((N, wide), bf16),
            V((pairs, N, 384), bf16),
            V((R, 3 * D), bf16),
            V((2 * R, 3 * D // 2), bf16),
            V((8, D), f32),
            V((8, FF), f32),
            V(saved[0].shape, f32),
            V((8, D), f32),
            V((F, small_rows, 128), f32),
            V((F, small_rows, 128), f32),
            V((X, F, small_rows, 128), f32),
            V((F, small_rows, 128), f32),
            V((L, H, small_rows, 128), f32),
            V((max(H, F), small_rows, 128), f32),
            D_SEM((14,)),
            D_SEM((2, 4)),
            D_SEM((1,)),
            D_SEM((4, lead, H)),
            D_SEM((4, L - 1, H)),
            D_SEM((4, H - 1)),
            D_SEM((4, lead)),
            D_SEM((4,)),
            D_SEM((4,)),
            D_SEM((2,)),
            D_SEM((S - 1,)),
            D_SEM((S - 1, pairs, 3)),
            D_SEM((1,)),
            D_SEM((lead,)),
            D_SEM((L - 1, H)),
            D_SEM((H - 1,)),
            D_SEM((2,)),
        ],
        compiler_params=pltpu.CompilerParams(
            collective_id=2, has_side_effects=True, vmem_limit_bytes=63 * 2**20
        ),
    )(cotangent, tokens, *saved)
    return res[0], res[1:5], res[5]


def on_device(
    tokens, cotangent, ln1_gain, ln1_bias, w_qkv, b_qv, w_out, b_out,
    ln2_gain, ln2_bias, w_fc, b_fc, w_proj, b_proj,
):
    F, S = lax.axis_size("fsdp"), lax.axis_size("seq")
    row_count, D = tokens.shape
    named = dict(
        b_fc=b_fc, b_qv=b_qv, ln1_gain=ln1_gain, ln1_bias=ln1_bias, b_out=b_out,
        ln2_gain=ln2_gain, ln2_bias=ln2_bias, b_proj=b_proj,
    )
    places, at = {}, 0
    for name, value in named.items():
        places[name] = (at, value.shape[0])
        at += value.shape[0]
    small_rows = -(-at // 2048) * 16
    total = small_rows * 128
    flat = sum(
        jnp.pad(value, (a, total - a - size))
        for value, (a, size) in zip(named.values(), places.values())
    ).reshape(small_rows, 128)
    outs = forward(tokens, cotangent, flat, places, [w_qkv, w_out, w_fc, w_proj])
    wholes, saved, output, stats, cot_pair = outs[:4], outs[5:14], outs[14], outs[15], outs[16]
    grad_tokens, (grad_w_proj, grad_w_fc, grad_w_out, grad_w_qkv), reduced = backward(
        cotangent, tokens, places, [outs[4], *wholes, *saved, stats, cot_pair]
    )
    reduced = reduced.reshape(-1)
    got = {name: reduced[a : a + size] for name, (a, size) in places.items()}
    at = -(-at // 128) * 128
    rms_values = jnp.sqrt(reduced[at : at + 3] / float(row_count * D * S * F))
    return (
        output, grad_tokens, got["ln1_gain"], got["ln1_bias"], grad_w_qkv, got["b_qv"],
        grad_w_out, got["b_out"], got["ln2_gain"], got["ln2_bias"], grad_w_fc, got["b_fc"],
        grad_w_proj, got["b_proj"], rms_values,
    )


def solution(mesh):
    in_specs = (
        P(("fsdp", "seq"), None),
        P(("fsdp", "seq"), None),
        P("fsdp"),
        P("fsdp"),
        P("fsdp", None),
        P("fsdp"),
        P("fsdp", None),
        P("fsdp"),
        P("fsdp"),
        P("fsdp"),
        P("fsdp", None),
        P("fsdp"),
        P("fsdp", None),
        P("fsdp"),
    )
    out_specs = (
        P(("fsdp", "seq"), None),
        P(("fsdp", "seq"), None),
        P("fsdp"),
        P("fsdp"),
        P("fsdp", None),
        P("fsdp"),
        P("fsdp", None),
        P("fsdp"),
        P("fsdp"),
        P("fsdp"),
        P("fsdp", None),
        P("fsdp"),
        P("fsdp", None),
        P("fsdp"),
        P(),
    )
    return jax.shard_map(
        on_device, mesh=mesh, in_specs=in_specs, out_specs=out_specs, check_vma=False
    )
```

```python
import functools
import math

import jax
import jax.numpy as jnp
from jax import lax
from jax.experimental import pallas as pl
from jax.experimental.pallas import tpu as pltpu
from jax.sharding import PartitionSpec as P

BLK = 256
HD = 64
EPSILON = 1e-05
MESH = pl.DeviceIdType.MESH
f32, bf16 = jnp.float32, jnp.bfloat16

def geometry():
    F, S = lax.axis_size("fsdp"), lax.axis_size("seq")
    return F, S, 4, F // 4, S // 2


class Place:
    def __init__(self):
        self.F, self.S, self.H, self.L, self.X = geometry()
        self.f, self.s = lax.axis_index("fsdp"), lax.axis_index("seq")
        self.h, self.l = self.f // self.L, self.f % self.L
        self.x, self.c = self.s // 2, self.s % 2

    def shard(self, k, j):
        return lax.rem(self.h + self.H - k, self.H) * self.L + lax.rem(self.l + self.L - j, self.L)

    def hi(self, k):
        return (lax.rem(self.h + k, self.H) * self.L + self.l, self.s)

    def lo(self, j):
        return (self.h * self.L + lax.rem(self.l + j, self.L), self.s)

    def across(self, i):
        return (self.f, lax.rem(self.x + i, self.X) * 2 + self.c)

    def sibling(self):
        return (self.f, self.x * 2 + 1 - self.c)

    def everyone(self):
        return (
            [self.hi(k) for k in range(1, self.H)]
            + [self.lo(j) for j in range(1, self.L)]
            + [(self.f, lax.rem(self.s + i, self.S)) for i in range(1, self.S)]
        )


def column_plan(X, eighths):
    if X == 2:
        return eighths, 8 - eighths, 8 - eighths, eighths
    return 8 // X, 8 // X, 8 // X, 8 // X


def greet(place):
    barrier = pltpu.get_barrier_semaphore()
    peers = place.everyone()
    for peer in peers:
        pl.semaphore_signal(barrier, inc=1, device_id=peer, device_id_type=MESH)
    pl.semaphore_wait(barrier, len(peers))


def vector(ref, places, name):
    at, size = places[name]
    parts = []
    for f in range(ref.shape[0]):
        pos = at
        while pos < at + size:
            row, lane = divmod(pos, 128)
            count = min(128 - lane, at + size - pos)
            parts.append(ref[f, row : row + 1, lane : lane + count])
            pos += count
    return jnp.concatenate(parts, axis=1)


def normalised(x):
    centre = x - jnp.mean(x, axis=-1, keepdims=True)
    return centre * lax.rsqrt(jnp.mean(centre * centre, axis=-1, keepdims=True) + EPSILON)


def gelu_and_slope(u):
    root = 0.7978845608028654
    square = u * u
    t = jnp.tanh(u * (root + root * 0.044715 * square))
    half = 0.5 * (1.0 + t)
    return u * half, half + u * (0.5 * (1.0 - t * t)) * (root + 3.0 * root * 0.044715 * square)


NT = (((1,), (1,)), ((), ()))
TN = (((0,), (0,)), ((), ()))


def head_lanes(shape, parity):
    lane = lax.broadcasted_iota(jnp.int32, shape, 1)
    return (lane // HD) == parity

def pick(rows, parity):
    return jnp.where(head_lanes(rows.shape, parity), rows, jnp.zeros_like(rows))

def turn(rows):
    return rows.astype(f32).T

def attend_block(i, pair, qkv, vT, scores, oT, lse):
    rows = pl.ds(i * BLK, BLK)

    @pl.loop(0, 128 // HD)
    def _(parity):
        h = pair * (128 // HD) + parity
        q = pick(qkv[pair, rows, 0:128], parity) * jnp.asarray(HD**-0.5, bf16)
        top = jnp.full((8, BLK), -jnp.inf, f32)
        for j in range(i + 1):
            k = qkv[pair, pl.ds(j * BLK, BLK), 128:256]
            s = lax.dot_general(k, q, NT, preferred_element_type=f32)
            scores[pl.ds(j * BLK, BLK), :] = s
            top = jnp.maximum(top, jnp.max(s.reshape(BLK // 8, 8, BLK), axis=0))
        top = jnp.max(top, axis=0, keepdims=True)
        total = jnp.zeros((8, BLK), f32)
        out = jnp.zeros((HD, BLK), f32)
        for j in range(i + 1):
            p = jnp.exp(scores[pl.ds(j * BLK, BLK), :] - top)
            total = total + jnp.sum(p.reshape(BLK // 8, 8, BLK), axis=0)
            v = vT[pl.ds(pl.multiple_of(h * HD, HD), HD), pl.ds(j * BLK, BLK)]
            out = out + jnp.dot(v, p.astype(bf16), preferred_element_type=f32)
        total = jnp.sum(total, axis=0, keepdims=True)
        oT[pl.ds(pl.multiple_of(parity * HD, HD), HD), :] = out * (1.0 / total)
        lse[pl.ds(h, 1), rows] = top + jnp.log(total)


def attend_back_block(i, pair, qkv, grad, kT, lse, delta, dqT, dk, dv):
    rows = pl.ds(i * BLK, BLK)
    here = pl.ds(pair * 128, 128)

    @pl.loop(0, 128 // HD)
    def _(parity):
        h = pair * (128 // HD) + parity
        out_rows = pl.ds(pl.multiple_of(parity * HD, HD), HD)
        q = pick(qkv[pair, rows, 0:128], parity) * jnp.asarray(HD**-0.5, bf16)
        g = pick(grad[rows, here], parity)
        low = lse[pl.ds(h, 1), rows]
        mean = delta[pl.ds(h, 1), rows]
        out = jnp.zeros((HD, BLK), f32)
        for j in range(i + 1):
            keys = pl.ds(j * BLK, BLK)
            k = qkv[pair, keys, 128:256]
            v = qkv[pair, keys, 256:384]
            p = jnp.exp(lax.dot_general(k, q, NT, preferred_element_type=f32) - low)
            dp = lax.dot_general(v, g, NT, preferred_element_type=f32)
            ds = (p * (dp - mean)).astype(bf16)
            dv[keys, :] += jnp.dot(p.astype(bf16), g, preferred_element_type=f32)
            dk[keys, :] += jnp.dot(ds, q, preferred_element_type=f32)
            kT_rows = kT[pl.ds(pl.multiple_of(h * HD, HD), HD), keys]
            out = out + jnp.dot(kT_rows, ds, preferred_element_type=f32)
        dqT[out_rows, :] = out * HD**-0.5


SHARES = (4, 2, 1, 2)
L_FIRST = (True, False, False, False)
SCHEDULE = (
    "y0 s0",
    "L00 y1 y2 y3 H01 H02 s1 H03 H11 H12 s2 H13 x0 c0 L10 L20 L30",
    "H21 L11",
    ("", "H22", "", "L21", "H23", "", "L22", "H31", "L23", "x1", "H32 c1", "L31"),
    ("L12 L13 s3", ""),
    "",
    "H33 L32 x2 c2",
    "L33",
)


def forward_kernel(places, *refs):
    refs = list(refs)

    def take(count):
        got = refs[:count]
        del refs[:count]
        return got

    tokens, cot, small = take(3)
    shards = take(4)
    big_outs = take(4)
    (small_out, one_out, qkv_out, lse_out, heads_out, mixed_out, middle_out, two_out, act_out,
     slope_out, result_out, stats_out, cot_out) = take(13)
    wholes = take(4)
    (smalls, smalls_f, one, split, qkv, vT, scores, oT, lse, heads, mixed, middle, two, act, slope,
     result, stats, vectors, wide_bias, stream) = take(20)
    (own_sem, send_sem, save_sem, hi_sem, lo_sem, x_sem, core_sem, sm_hi_sem, sm_lo_sem, there_sem,
     back_sem, pair_sem, last_sem) = refs
    p = Place()
    S, H, L, X, F = p.S, p.H, p.L, p.X, p.F
    rows_here, D = tokens.shape
    wide = D // S
    saved = []

    def push(src, dst, sem, peer, kind=0):
        pltpu.make_async_remote_copy(
            src_ref=src, dst_ref=dst, send_sem=send_sem.at[kind], recv_sem=sem, device_id=peer,
            device_id_type=MESH,
        ).start()

    def arrived(dst, sem):
        pltpu.make_async_copy(dst, dst, sem).wait()

    def save(src, dst):
        cp = pltpu.make_async_copy(src, dst, save_sem.at[len(saved)])
        cp.start()
        saved.append(cp)

    def share(src, dst, index):
        save(src, dst.at[0:rows_here])
        push(src, dst.at[rows_here:], pair_sem.at[index], p.sibling())

    own = []
    for w in range(4):
        own.append(pltpu.make_async_copy(shards[w], wholes[w].at[p.f], own_sem.at[w]))
    own.append(pltpu.make_async_copy(small, smalls.at[p.f], own_sem.at[4]))
    for cp in own:
        cp.start()
    greet(p)

    plans = [column_plan(X, eighths) for eighths in SHARES]

    def cols(w, start, count):
        C = shards[w].shape[-1]
        return pl.ds(pl.multiple_of(p.c * (C // 2) + start * (C // 16), 128), count * (C // 16))

    def fetched(w):
        return cols(w, plans[w][0] * p.x, plans[w][1])

    def only(w, x):
        return cols(w, plans[w][2] * x, plans[w][3])

    def half(w, core):
        C = shards[w].shape[-1]
        return pl.ds(pl.multiple_of(core * (C // 2), 128), C // 2)

    def up():
        return ((p.h + 1) * L + p.l, p.s)

    def down():
        return ((p.h - 1) * L + p.l, p.s)

    def both_ways(w, src, f, j):
        dst = wholes[w].at[f, :, fetched(w)]

        @pl.when(p.h < H - 1)
        def _():
            push(src, dst, hi_sem.at[w, 0, 0, j], up(), 1)

        @pl.when(p.h > 0)
        def _():
            push(src, dst, hi_sem.at[w, 1, 0, j], down(), 1)

    def start(w):
        both_ways(w, shards[w].at[:, fetched(w)], p.f, 0)

    def start_lo(w):
        src, dst = shards[w].at[:, fetched(w)], wholes[w].at[p.f, :, fetched(w)]
        for j in range(1, L):
            push(src, dst, lo_sem.at[w, j - 1, p.h], p.lo(j))

    def over_x(w, f):
        piece = wholes[w].at[f, :, only(w, p.x)]
        for i in range(1, X):
            push(piece, piece, x_sem.at[w, i - 1, f], p.across(i))

    def from_hi(w, d, below):
        origin = p.h - d if below else p.h + d
        side = 0 if below else 1

        @pl.when(origin >= 0 if below else origin < H)
        def _():
            for j in range(L) if L_FIRST[w] else [0]:
                f = origin * L + lax.rem(p.l + L - j, L)
                piece = wholes[w].at[f, :, fetched(w)]
                arrived(piece, hi_sem.at[w, side, d - 1, j])
                if d < H - 1:

                    @pl.when(p.h < H - 1 if below else p.h > 0)
                    def _():
                        push(piece, piece, hi_sem.at[w, side, d, j], up() if below else down(), 1)

            if not L_FIRST[w]:
                for j in range(1, L):
                    push(piece, piece, lo_sem.at[w, j - 1, origin], p.lo(j))

    def origins(visit, own):
        if own:
            visit(p.h)
        for d in range(1, H):

            @pl.when(p.h >= d)
            def _():
                visit(p.h - d)

            @pl.when(p.h + d < H)
            def _():
                visit(p.h + d)

    def from_lo(w, d, below):
        def visit(origin):
            for j in range(1, L):
                f = origin * L + lax.rem(p.l + L - j, L)
                piece = wholes[w].at[f, :, fetched(w)]
                arrived(piece, lo_sem.at[w, j - 1, origin])
                if L_FIRST[w]:
                    both_ways(w, piece, f, j)

        at_distance(d, below, visit)

    def at_distance(d, below, visit):
        if d == 0:
            visit(p.h)
            return
        origin = p.h - d if below else p.h + d
        pl.when(origin >= 0 if below else origin < H)(lambda: visit(origin))

    def out_x(w, d, below, lo):
        def visit(origin):
            for j in range(1, L) if lo else [0]:
                over_x(w, origin * L + lax.rem(p.l + L - j, L))

        at_distance(d, below, visit)

    def from_x(w, j):
        def visit(origin):
            f = origin * L + lax.rem(p.l + L - j, L)
            for i in range(1, X):
                theirs = only(w, lax.rem(p.x + X - i, X))
                arrived(wholes[w].at[f, :, theirs], x_sem.at[w, i - 1, f])
            piece = wholes[w].at[f, :, half(w, p.c)]
            push(piece, piece, core_sem.at[w, f], p.sibling())

        origins(visit, j > 0)

    def from_core(w):
        for j in range(L):

            def visit(origin):
                f = origin * L + lax.rem(p.l + L - j, L)
                arrived(wholes[w].at[f, :, half(w, 1 - p.c)], core_sem.at[w, f])

            origins(visit, j > 0)
        own[w].wait()
        save(wholes[w], big_outs[w])

    def run(names):
        for name in names.split():
            kind, w, d = name[0], int(name[1]), int(name[2:] or 0)
            sides = (True, False) if d else (True,)
            if kind == "s":
                start(w)
            elif kind == "y":
                start_lo(w)
            elif kind == "x":
                for j in range(L):
                    from_x(w, j)
            elif kind == "c":
                from_core(w)
            else:
                for below in sides:
                    if kind in "hH":
                        from_hi(w, d, below)
                    if kind in "lL":
                        from_lo(w, d, below)
                    if kind in "pH":
                        out_x(w, d, below, False)
                    if kind in "qL" or kind == "H" and L_FIRST[w]:
                        out_x(w, d, below, True)

    push(
        cot.at[:, pl.ds(pl.multiple_of((1 - p.c) * (D // 2), 128), D // 2)],
        cot_out, pair_sem.at[4], p.sibling(),
    )
    for k in range(1, H):
        push(small, smalls.at[p.f], sm_hi_sem.at[k - 1], p.hi(k))
    for j in range(1, L):
        push(small, smalls.at[p.f], sm_lo_sem.at[j - 1, 0], p.lo(j))
    run(SCHEDULE[0])
    for k in range(1, H):
        piece = smalls.at[p.shard(k, 0)]
        arrived(piece, sm_hi_sem.at[k - 1])
        for j in range(1, L):
            push(piece, piece, sm_lo_sem.at[j - 1, k], p.lo(j))
    for j in range(1, L):
        for k in range(H):
            arrived(smalls.at[p.shard(k, j)], sm_lo_sem.at[j - 1, k])
    own[4].wait()
    smalls_f[...] = smalls[...].astype(f32)
    save(smalls_f, small_out)
    vec = functools.partial(vector, smalls_f, places)

    chunk = 128
    stats[...] = jnp.zeros_like(stats)
    gain, shift = vec("ln1_gain"), vec("ln1_bias")

    @pl.loop(0, rows_here // chunk)
    def _(t):
        at = pl.ds(pl.multiple_of(t * chunk, chunk), chunk)
        x = tokens[at, :].astype(f32)
        stats[0:1, :] += jnp.sum(x * x, axis=0, keepdims=True)
        one[at, :] = (normalised(x) * gain + shift).astype(bf16)

    share(one, one_out, 0)
    run(SCHEDULE[1])

    bias_qv = vec("b_qv")

    def project(kind, target):
        at = pl.multiple_of(kind * D + target * wide, 128)
        w = wholes[0][:, :, pl.ds(at, wide)].reshape(D, wide)
        return jnp.dot(one[...], w, preferred_element_type=f32)

    vectors[0:1, :] = bias_qv[:, :D]
    vectors[1:2, :] = bias_qv[:, D:]

    def heads_of(target):
        lanes = pl.ds(pl.multiple_of(target * wide, 128), wide)
        return [
            (project(0, target) + vectors[0:1, lanes]).astype(bf16),
            project(1, target).astype(bf16),
            (project(2, target) + vectors[1:2, lanes]).astype(bf16),
        ]

    mine = pl.ds(pl.multiple_of(p.s * rows_here, 128), rows_here)
    pairs = wide // 128

    def send_pair(i, pair):
        push(
            split.at[i - 1, pair], qkv.at[pair, mine, :], there_sem.at[i - 1, pair],
            (p.f, lax.rem(p.s + i, S)),
        )

    for i in list(range(1, S)) + [0]:
        target = lax.rem(p.s + i, S)
        for kind, values in enumerate(heads_of(target)):
            for pair in range(pairs):
                block = values[:, pair * 128 : (pair + 1) * 128]
                if i == 0:
                    qkv[pair, mine, kind * 128 : (kind + 1) * 128] = block
                else:
                    split[i - 1, pair, :, kind * 128 : (kind + 1) * 128] = block
        if i:
            send_pair(i, 0)
    run(SCHEDULE[2])

    length = qkv.shape[1]
    blocks = length // BLK
    lse[...] = jnp.zeros_like(lse)
    passed = set()
    for pair in range(pairs):
        for i in range(1, S):
            source = lax.rem(p.s + S - i, S)
            there = pl.ds(pl.multiple_of(source * rows_here, 128), rows_here)
            arrived(qkv.at[pair, there, :], there_sem.at[i - 1, pair])
        if pair + 1 < pairs:
            for i in range(1, S):
                send_pair(i, pair + 1)
        else:
            save(qkv, qkv_out)
        run(SCHEDULE[4][pair] if pair < 2 else "")
        for b in range(blocks):
            at = pl.ds(b * BLK, BLK)
            vT[pair * 128 : (pair + 1) * 128, at] = turn(qkv[pair, at, 256:384]).astype(bf16)
        lanes = pl.ds(pl.multiple_of(p.s * wide + pair * 128, 128), 128)
        here = pl.ds(pair * 128, 128)
        sent_back = 0
        for i in range(blocks):
            attend_block(i, pair, qkv, vT, scores, oT, lse)
            heads[pl.ds(i * BLK, BLK), here] = turn(oT[...]).astype(bf16)
            while (sent_back + 1) * rows_here <= (i + 1) * BLK:
                rows = pl.ds(sent_back * rows_here, rows_here)

                @pl.when(p.s != sent_back)
                def _():
                    pltpu.make_async_remote_copy(
                        src_ref=heads.at[rows, here], dst_ref=mixed.at[:, lanes],
                        send_sem=send_sem.at[2], recv_sem=back_sem.at[p.s, pair],
                        device_id=(p.f, jnp.int32(sent_back)), device_id_type=MESH,
                    ).start()

                @pl.when(p.s == sent_back)
                def _():
                    mixed[:, lanes] = heads[rows, here]

                sent_back += 1
            at = (pair * blocks + i) * 12 // (pairs * blocks)
            run(SCHEDULE[3][at] if at not in passed else "")
            passed.add(at)
    if pairs == 1:
        run(SCHEDULE[4][1])
    save(heads, heads_out)
    save(lse, lse_out)
    run(SCHEDULE[5])
    for i in range(1, S):
        source = lax.rem(p.s + S - i, S)
        for pair in range(pairs):
            lanes = pl.ds(pl.multiple_of(source * wide + pair * 128, 128), 128)
            arrived(mixed.at[:, lanes], back_sem.at[source, pair])
    share(mixed, mixed_out, 1)

    tile = 256
    vectors[0:1, :] = vec("b_out")

    @pl.loop(0, D // tile)
    def _(t):
        at = pl.ds(pl.multiple_of(t * tile, tile), tile)
        w = wholes[1][:, :, at].reshape(D, tile)
        branch = jnp.dot(mixed[...], w, preferred_element_type=f32) + vectors[0:1, at]
        middle[:, at] = tokens[:, at].astype(f32) + branch

    save(middle, middle_out)
    gain_two, shift_two = vec("ln2_gain"), vec("ln2_bias")

    @pl.loop(0, rows_here // chunk)
    def _(t):
        at = pl.ds(pl.multiple_of(t * chunk, chunk), chunk)
        x = middle[at, :]
        stats[1:2, :] += jnp.sum(x * x, axis=0, keepdims=True)
        two[at, :] = (normalised(x) * gain_two + shift_two).astype(bf16)

    share(two, two_out, 2)
    run(SCHEDULE[6])
    wide_bias[0:1, :] = vec("b_fc")

    FF = act.shape[1]

    @pl.loop(0, FF // tile)
    def _(t):
        at = pl.ds(pl.multiple_of(t * tile, tile), tile)
        w = wholes[2][:, :, at].reshape(D, tile)
        u = jnp.dot(two[...], w, preferred_element_type=f32) + wide_bias[0:1, at]
        act_rows, slope_rows = gelu_and_slope(u)
        act[:, at] = act_rows.astype(bf16)
        slope[:, at] = slope_rows.astype(bf16)

    share(act, act_out, 3)
    save(slope, slope_out)
    vectors[0:1, :] = vec("b_proj")
    stream[...] = middle[...] + vectors[0:1, :]

    def multiply(f):
        lanes = pl.ds(pl.multiple_of(f * (FF // F), 128), FF // F)
        stream[...] += jnp.dot(act[:, lanes], wholes[3][f], preferred_element_type=f32)
        pltpu.make_async_copy(wholes[3].at[f], big_outs[3].at[f], last_sem.at[0]).start()

    own[3].wait()
    multiply(p.f)
    run(SCHEDULE[7])
    for j in range(L):
        from_x(3, j)

        @pl.loop(0 if j else 1, 2 * H - 1)
        def _(q):
            d = lax.div(q + 1, 2)
            origin = jnp.where(lax.rem(q, 2) == 1, p.h - d, p.h + d)

            @pl.when((origin >= 0) & (origin < H))
            def _():
                f = origin * L + lax.rem(p.l + L - j, L)
                arrived(wholes[3].at[f, :, half(3, 1 - p.c)], core_sem.at[3, f])
                multiply(f)

    @pl.loop(0, rows_here // chunk)
    def _(t):
        at = pl.ds(pl.multiple_of(t * chunk, chunk), chunk)
        x = stream[at, :]
        stats[2:3, :] += jnp.sum(x * x, axis=0, keepdims=True)
        result[at, :] = x.astype(bf16)

    save(result, result_out)
    save(stats, stats_out)
    for index, there in enumerate((one_out, mixed_out, two_out, act_out)):
        arrived(there.at[rows_here:], pair_sem.at[index])
    arrived(cot_out, pair_sem.at[4])
    moves = jnp.where(p.h < H - 1, p.h + 1, 0) + jnp.where(p.h > 0, H - p.h, 0)
    for w in range(4):
        piece = wholes[w].at[0, :, fetched(w)]

        @pl.loop(0, moves * (L if L_FIRST[w] else 1))
        def _(_):
            arrived(piece, send_sem.at[1])

        for _ in range((1 if L_FIRST[w] else H) * (L - 1)):
            arrived(piece, send_sem.at[0])
        for _ in range((F - 1) * (X - 1)):
            arrived(wholes[w].at[0, :, only(w, 0)], send_sem.at[0])
        for _ in range(F - 1):
            arrived(wholes[w].at[0, :, half(w, 0)], send_sem.at[0])
    for _ in range(H - 1 + H * (L - 1)):
        arrived(smalls.at[0], send_sem.at[0])
    for i in range(S - 1):
        arrived(split.at[i], send_sem.at[0])
        arrived(heads.at[pl.ds(0, rows_here)], send_sem.at[2])
    for there in (one_out, mixed_out, two_out, act_out):
        arrived(there.at[rows_here:], send_sem.at[0])
    arrived(cot_out, send_sem.at[0])
    arrived(wholes[3], last_sem.at[0])
    for cp in saved:
        cp.wait()


def forward(tokens, cotangent, packed, places, shards):
    F, S, H, L, X = geometry()
    rows_here, D = tokens.shape
    wide, length, FF = D // S, rows_here * S, shards[2].shape[1]
    heads = max(8, wide // HD)
    lead = max(X - 1, 1)
    any_spec = pl.BlockSpec(memory_space=pl.ANY)
    V, D_SEM = pltpu.VMEM, pltpu.SemaphoreType.DMA
    shaped = jax.ShapeDtypeStruct
    wholes = [(F,) + a.shape for a in shards]
    outs = [shaped(s, bf16) for s in wholes] + [
        shaped((F,) + packed.shape, f32),
        shaped((2 * rows_here, D), bf16),
        shaped((wide // 128, length, 384), bf16),
        shaped((heads, length), f32),
        shaped((length, wide), bf16),
        shaped((2 * rows_here, D), bf16),
        shaped((rows_here, D), f32),
        shaped((2 * rows_here, D), bf16),
        shaped((2 * rows_here, FF), bf16),
        shaped((rows_here, FF), bf16),
        shaped((rows_here, D), bf16),
        shaped((8, D), f32),
        shaped((rows_here, D // 2), bf16),
    ]
    return pl.pallas_call(
        functools.partial(forward_kernel, places),
        out_shape=outs,
        in_specs=[pl.BlockSpec(memory_space=pltpu.VMEM)] + [any_spec] * 6,
        out_specs=[any_spec] * len(outs),
        scratch_shapes=[V(s, bf16) for s in wholes]
        + [
            V((F,) + packed.shape, bf16),
            V((F,) + packed.shape, f32),
            V((rows_here, D), bf16),
            V((S - 1, wide // 128, rows_here, 384), bf16),
            V((wide // 128, length, 384), bf16),
            V((wide, length), bf16),
            V((length, BLK), f32),
            V((128, BLK), f32),
            V((heads, length), f32),
            V((length, wide), bf16),
            V((rows_here, D), bf16),
            V((rows_here, D), f32),
            V((rows_here, D), bf16),
            V((rows_here, FF), bf16),
            V((rows_here, FF), bf16),
            V((rows_here, D), bf16),
            V((8, D), f32),
            V((8, D), f32),
            V((8, FF), f32),
            V((rows_here, D), f32),
            D_SEM((5,)),
            D_SEM((3,)),
            D_SEM((len(outs) + 8,)),
            D_SEM((4, 2, H - 1, L)),
            D_SEM((4, L - 1, H)),
            D_SEM((4, lead, F)),
            D_SEM((4, F)),
            D_SEM((H - 1,)),
            D_SEM((L - 1, H)),
            D_SEM((S - 1, wide // 128)),
            D_SEM((S, wide // 128)),
            D_SEM((5,)),
            D_SEM((1,)),
        ],
        compiler_params=pltpu.CompilerParams(
            collective_id=1, has_side_effects=True, vmem_limit_bytes=60 * 2**20
        ),
    )(tokens, cotangent, packed, *shards)


BACK_SHARES = (2, 1, 2, 2)
BACK = dict(
    first="x0",
    feed=("y0", "x1", "", "y1 x2", "", "x3 z0 y2", "", ""),
    norm="",
    mixed="z1 y3",
    fc=("", "x4", "", "z2 y4"),
    out=("", "", "", ""),
    attention=("x5", "", "z3 y5", "", "x6 v0", "", "z4 y6", "e0", "x7", "", "z5 y7", "x8 x9"),
    sent="x10 x11 z6 y8",
    back="z7 y9",
    qkv=("x12 z8", "x13 y12", "x14 z9 y13", "x15 v1"),
    input="z12 y14",
    norm1="z13 y15 e1",
    small=("z14 y10 y11", "z15", "v3 z10 z11 v2"),
    end="e3 e2",
)


def backward_kernel(places, *refs):
    refs = list(refs)

    def take(count):
        got = refs[:count]
        del refs[:count]
        return got

    cot, = take(1)
    (tokens, smalls, wq_in, wo_in, wf_in, wp_in, one_in, qkv_in, lse_in, heads_in, mixed_in,
     middle_in, two_in, act_in, slope_in, stats, cot_in) = take(17)
    grad_tokens, = take(1)
    outs = take(4)
    small_out, = take(1)
    parts, from_x, from_lo, from_hi, value, from_x_end, half_out = (take(4) for _ in range(7))
    (cot_pair, gbh, gb_other, grad_middle, branch, branch_pair, leaving, grad_heads, grad_qkv,
     grad_proj, proj_pair, sums, fc_sum, smalls_f, stats_v) = take(15)
    sm_mine, sm_core, sm_x, sm_sum, sm_lo, sm_hi = take(6)
    (load_sem, slot_sem, send_sem, x_sem, lo_sem, hi_sem, end_sem, out_sem, core_sem, pair_sem, to_sem,
     from_sem, sm_sem, smx_sem, smlo_sem, smhi_sem, gb_sem) = refs
    p = Place()
    S, H, L, X, F = p.S, p.H, p.L, p.X, p.F
    R, D = cot.shape
    FF = fc_sum.shape[1]
    wide = D // S
    N = R * S
    plans = [column_plan(X, eighths) for eighths in BACK_SHARES]
    sent = []

    def push(src, dst, sem, peer):
        pltpu.make_async_remote_copy(
            src_ref=src, dst_ref=dst, send_sem=send_sem.at[0], recv_sem=sem, device_id=peer,
            device_id_type=MESH,
        ).start()
        sent.append(math.prod(src.shape) * src.dtype.itemsize)

    def arrived(dst, sem):
        pltpu.make_async_copy(dst, dst, sem).wait()

    loads = {}

    def load(index, src, dst):
        loads[index] = pltpu.make_async_copy(src, dst, load_sem.at[index])
        loads[index].start()

    def eighths(w, start, count):
        unit = parts[w].shape[-1] // 8
        return pl.ds(pl.multiple_of(start * unit, 128), count * unit)

    def reach(w, x):
        return eighths(w, plans[w][0] * x, plans[w][1])

    def only(w, x):
        return eighths(w, plans[w][2] * x, plans[w][3])

    def ahead(k, j):
        return lax.rem(p.h + k, H) * L + lax.rem(p.l + j, L)

    steps = list(range(1, H)) + [0]
    slots = [(w, k) for w in range(4) for k in steps]

    def shards_of(k):
        return pl.ds(lax.rem(p.h + k, H) * L, L)

    def send_x(w, k):
        for j in list(range(1, L)) + [0]:
            f = ahead(k, j)
            for i in range(1, X):
                push(
                    parts[w].at[f, :, only(w, lax.rem(p.x + i, X))], from_x[w].at[i - 1, f],
                    x_sem.at[w, i - 1, k, j], p.across(i),
                )

    def add_x(w, k, j):
        f = ahead(k, j)
        if X > 1:
            total = parts[w][f, :, only(w, p.x)].astype(f32)
            for i in range(1, X):
                came = from_x[w].at[i - 1, f]
                arrived(came, x_sem.at[w, i - 1, k, j])
                total = total + came[...].astype(f32)
            parts[w][f, :, only(w, p.x)] = total.astype(bf16)

    def send_lo(w, k):
        for j in range(1, L):
            add_x(w, k, j)
            push(
                parts[w].at[ahead(k, j), :, reach(w, p.x)],
                from_lo[w].at[j - 1, lax.rem(p.h + k, H)], lo_sem.at[w, j - 1, k], p.lo(j),
            )

    def add_lo(w, k):
        f = ahead(k, 0)
        add_x(w, k, 0)
        cols = reach(w, p.x)
        total = parts[w][f, :, cols].astype(f32)
        for j in range(1, L):
            came = from_lo[w].at[j - 1, lax.rem(p.h + k, H)]
            arrived(came, lo_sem.at[w, j - 1, k])
            total = total + came[...].astype(f32)
        parts[w][f, :, cols] = total.astype(bf16)
        if k > 0:
            push(parts[w].at[f, :, cols], from_hi[w].at[k - 1], hi_sem.at[w, k - 1], p.hi(k))

    def add_hi(w):
        cols = reach(w, p.x)
        total = parts[w][p.f, :, cols].astype(f32)
        for k in range(1, H):
            arrived(from_hi[w].at[k - 1], hi_sem.at[w, k - 1])
            total = total + from_hi[w][k - 1].astype(f32)
        value[w][:, cols] = total.astype(bf16)
        for i in range(1, X):
            push(
                value[w].at[:, cols], from_x_end[w].at[i - 1, :, cols], end_sem.at[w, i - 1],
                p.across(i),
            )

    def finish(w):
        mine = only(w, p.x)
        half_out[w][:, mine] = value[w][:, mine].astype(f32)
        for i in range(1, X):
            source = lax.rem(p.x + X - i, X)
            cols = reach(w, source)
            arrived(from_x_end[w].at[i - 1, :, cols], end_sem.at[w, i - 1])
            theirs = only(w, source)
            half_out[w][:, theirs] = from_x_end[w][i - 1, :, theirs].astype(f32)
        if X == 2 and plans[w][3] < 4:
            both = eighths(w, plans[w][3], 8 - 2 * plans[w][3])
            total = value[w][:, both].astype(f32)
            for i in range(1, X):
                total = total + from_x_end[w][i - 1, :, both].astype(f32)
            half_out[w][:, both] = total
        there = outs[w].at[:, eighths(w, p.c * 8, 8)]
        push(half_out[w], there, core_sem.at[w], p.sibling())
        pltpu.make_async_copy(half_out[w], there, out_sem.at[w]).start()

    ran = []

    def run(names):
        for name in names.split():
            kind, n = name[0], int(name[1:])
            ran.append(name)
            if kind == "x":
                send_x(*slots[n])
            elif kind == "y":
                send_lo(*slots[n])
            elif kind == "z":
                add_lo(*slots[n])
            elif kind == "v":
                add_hi(n)
            else:
                finish(n)

    load(0, cot_in, cot_pair.at[R : 2 * R])
    cot_pair[0:R, :] = cot[:, pl.ds(pl.multiple_of(p.c * (D // 2), 128), D // 2)]
    load(1, smalls, smalls_f)
    load(2, stats, stats_v)
    greet(p)

    tile = FF // F
    grad_middle[...] = jnp.zeros_like(grad_middle)

    def feed_forward(wp, wf, act, slope):
        tiles = [lax.rem(p.h + k, H) * L + j for k in steps for j in range(L)]

        def fetch(t, f):
            slot = t % 2
            cols = pl.ds(pl.multiple_of(f * tile, 128), tile)
            return [
                pltpu.make_async_copy(wp_in.at[f], wp.at[slot], slot_sem.at[slot, 0]),
                pltpu.make_async_copy(wf_in.at[:, :, cols], wf.at[slot], slot_sem.at[slot, 1]),
                pltpu.make_async_copy(slope_in.at[:, cols], slope.at[slot], slot_sem.at[slot, 3]),
            ]

        def fetch_act(t):
            if t < len(tiles):
                cols = pl.ds(pl.multiple_of(tiles[t] * tile, 128), tile)
                arriving[t] = pltpu.make_async_copy(
                    act_in.at[:, cols], act.at[t % 2], slot_sem.at[t % 2, 2]
                )
                arriving[t].start()

        def proj_grad(t):
            if t < len(tiles):
                arriving[t].wait()
                grad = lax.dot_general(act[t % 2], cot_pair[...], TN, preferred_element_type=f32)
                parts[0][tiles[t]] = grad.astype(bf16)
                fetch_act(t + 2)

        arriving = {}
        fetch_act(0)
        fetch_act(1)
        coming = fetch(0, tiles[0])
        for cp in coming:
            cp.start()
        loads[0].wait()
        for t in range(L):
            proj_grad(t)
        run(BACK["first"])
        for t, f in enumerate(tiles):
            for cp in coming:
                cp.wait()
            if t + 1 < len(tiles):
                coming = fetch(t + 1, tiles[t + 1])
                for cp in coming:
                    cp.start()
            slot = t % 2
            proj_grad(t + L)
            grad_act = lax.dot_general(cot[...], wp[slot], NT, preferred_element_type=f32)
            before = (slope[slot].astype(f32) * grad_act).astype(bf16)
            fc_sum[0:1, pl.ds(pl.multiple_of(f * tile, 128), tile)] = jnp.sum(
                before.astype(f32), axis=0, keepdims=True
            )
            at = pl.ds(pl.multiple_of(lax.rem(f, F // 2) * tile, 128), tile)

            @pl.when(f // (F // 2) == p.c)
            def _():
                gbh[0:R, at] = before

            @pl.when(f // (F // 2) != p.c)
            def _():
                gb_other[:, at] = before
                pltpu.make_async_remote_copy(
                    src_ref=gb_other.at[:, at], dst_ref=gbh.at[R : 2 * R, at], send_sem=gb_sem.at[0],
                    recv_sem=gb_sem.at[1], device_id=p.sibling(), device_id_type=MESH,
                ).start()

            grad_middle[...] += lax.dot_general(
                before, wf[slot].reshape(D, tile), NT, preferred_element_type=f32
            )
            if (2 * t + 2) % L == 0:
                run(BACK["feed"][(2 * t + 2) // L - 1])

    pl.run_scoped(
        feed_forward,
        pltpu.VMEM((2,) + wp_in.shape[1:], bf16),
        pltpu.VMEM((2,) + wf_in.shape[:2] + (tile,), bf16),
        pltpu.VMEM((2, 2 * R, tile), bf16),
        pltpu.VMEM((2, R, tile), bf16),
    )

    chunk = 128
    sums[...] = jnp.zeros_like(sums)
    loads[1].wait()
    loads[2].wait()

    def norm_back(rows, grad, gain, first):
        centre = rows - jnp.mean(rows, axis=-1, keepdims=True)
        scale = lax.rsqrt(jnp.mean(centre * centre, axis=-1, keepdims=True) + EPSILON)
        n = centre * scale
        sums[first : first + 1, :] += jnp.sum(grad * n, axis=0, keepdims=True)
        sums[first + 1 : first + 2, :] += jnp.sum(grad, axis=0, keepdims=True)
        scaled = grad * gain
        return scale * (
            scaled
            - jnp.mean(scaled, axis=-1, keepdims=True)
            - n * jnp.mean(scaled * n, axis=-1, keepdims=True)
        )

    def weight_grad(w, rows_pair, columns_pair, hook):
        r = parts[w].shape[1]
        for t, k in enumerate(steps):
            at = pl.ds(pl.multiple_of(lax.rem(p.h + k, H) * (L * r), 128), L * r)
            grad = lax.dot_general(
                rows_pair[:, at], columns_pair[...], TN, preferred_element_type=f32
            )
            parts[w][shards_of(k)] = grad.astype(bf16).reshape(L, r, grad.shape[1])
            run(BACK[hook][t])

    def attention_output(middle, wo, two, mixed):
        load(3, middle_in, middle)
        load(4, wo_in, wo)
        load(5, two_in, two)
        load(6, mixed_in, mixed)
        gain = vector(smalls_f, places, "ln2_gain")
        loads[3].wait()

        @pl.loop(0, R // chunk)
        def _(t):
            at = pl.ds(pl.multiple_of(t * chunk, chunk), chunk)
            out = cot[at, :].astype(f32)
            sums[5:6, :] += jnp.sum(out, axis=0, keepdims=True)
            total = out + norm_back(middle[at, :], grad_middle[at, :], gain, 0)
            grad_middle[at, :] = total
            rounded = total.astype(bf16)
            branch[at, :] = rounded
            sums[4:5, :] += jnp.sum(rounded.astype(f32), axis=0, keepdims=True)

        half = D // 2
        run(BACK["norm"])
        branch_pair[0:R, :] = branch[:, pl.ds(pl.multiple_of(p.c * half, 128), half)]
        push(
            branch.at[:, pl.ds(pl.multiple_of((1 - p.c) * half, 128), half)],
            branch_pair.at[R : 2 * R, :], pair_sem.at[0], p.sibling(),
        )
        loads[4].wait()
        r = wo.shape[1]
        mine = pl.ds(pl.multiple_of(p.s * R, 128), R)
        for i in list(range(1, S)) + [0]:
            target = lax.rem(p.s + i, S)
            rows = wo[pl.ds(target * (wide // r), wide // r)].reshape(wide, D)
            grad = lax.dot_general(branch[...], rows, NT, preferred_element_type=f32).astype(bf16)
            if i:
                leaving[i - 1] = grad
                push(leaving.at[i - 1], grad_heads.at[mine, :], to_sem.at[i - 1], (p.f, target))
            else:
                grad_heads[mine, :] = grad
        run(BACK["mixed"])
        loads[5].wait()
        arrived(gbh.at[R : 2 * R, :], gb_sem.at[1])
        weight_grad(1, two, gbh, "fc")
        loads[6].wait()
        arrived(branch_pair.at[R : 2 * R, :], pair_sem.at[0])
        weight_grad(2, mixed, branch_pair, "out")

    pl.run_scoped(
        attention_output,
        pltpu.VMEM((R, D), f32),
        pltpu.VMEM(wo_in.shape, bf16),
        pltpu.VMEM((2 * R, D), bf16),
        pltpu.VMEM((2 * R, D), bf16),
    )

    pairs = wide // 128

    def attention(qkv, heads, lse, kT, delta, dqT, dk, dv):
        load(7, qkv_in, qkv)
        load(8, heads_in, heads)
        load(9, lse_in, lse)
        for i in range(1, S):
            source = lax.rem(p.s + S - i, S)
            arrived(grad_heads.at[pl.ds(pl.multiple_of(source * R, 128), R), :], to_sem.at[i - 1])
        for index in (7, 8, 9):
            loads[index].wait()
        shape = (lse.shape[0], wide)
        chosen = lax.broadcasted_iota(jnp.int32, shape, 1) // HD == lax.broadcasted_iota(jnp.int32, shape, 0)
        chosen = jnp.where(chosen, 1.0, 0.0).astype(bf16)
        for b in range(N // BLK):
            at = pl.ds(b * BLK, BLK)
            for pair in range(pairs):
                kT[pair * 128 : (pair + 1) * 128, at] = turn(qkv[pair, at, 128:256]).astype(bf16)
            product = grad_heads[at, :].astype(f32) * heads[at, :].astype(f32)
            high = product.astype(bf16)
            low = (product - high.astype(f32)).astype(bf16)
            delta[:, at] = lax.dot_general(chosen, high, NT, preferred_element_type=f32) + lax.dot_general(
                chosen, low, NT, preferred_element_type=f32
            )
        for pair in range(pairs):
            dk[...] = jnp.zeros_like(dk)
            dv[...] = jnp.zeros_like(dv)
            for i in range(N // BLK):
                attend_back_block(i, pair, qkv, grad_heads, kT, lse, delta, dqT, dk, dv)
                grad_qkv[pair, pl.ds(i * BLK, BLK), 0:128] = turn(dqT[...]).astype(bf16)
                at = (pair * (N // BLK) + i) * 12 // (pairs * (N // BLK))
                run(BACK["attention"][at] if at not in passed else "")
                passed.add(at)
            grad_qkv[pair, :, 128:256] = dk[...].astype(bf16)
            grad_qkv[pair, :, 256:384] = dv[...].astype(bf16)
            for i in list(range(1, S)) + [0]:
                target = lax.rem(p.s + i, S)
                rows = pl.ds(pl.multiple_of(target * R, 128), R)
                for kind in range(3):
                    lanes = pl.ds(pl.multiple_of(kind * D + p.s * wide + pair * 128, 128), 128)
                    block = grad_qkv.at[pair, rows, kind * 128 : (kind + 1) * 128]
                    if i:
                        push(block, grad_proj.at[:, lanes], from_sem.at[i - 1, pair, kind], (p.f, target))
                    else:
                        grad_proj[:, lanes] = block[...]
        run(BACK["sent"])

    passed = set()
    pl.run_scoped(
        attention,
        pltpu.VMEM(qkv_in.shape, bf16),
        pltpu.VMEM((N, wide), bf16),
        pltpu.VMEM(lse_in.shape, f32),
        pltpu.VMEM((wide, N), bf16),
        pltpu.VMEM(lse_in.shape, f32),
        pltpu.VMEM((128, BLK), f32),
        pltpu.VMEM((N, 128), f32),
        pltpu.VMEM((N, 128), f32),
    )

    def projections(wq, one, tokens_v, result, qv_sum):
        load(10, wq_in, wq)
        load(11, one_in, one)
        load(12, tokens, tokens_v)
        for i in range(1, S):
            source = lax.rem(p.s + S - i, S)
            for pair in range(pairs):
                for kind in range(3):
                    lanes = pl.ds(pl.multiple_of(kind * D + source * wide + pair * 128, 128), 128)
                    arrived(grad_proj.at[:, lanes], from_sem.at[i - 1, pair, kind])
        run(BACK["back"])
        half = 3 * D // 2
        push(
            grad_proj.at[:, pl.ds(pl.multiple_of((1 - p.c) * half, 128), half)],
            proj_pair.at[R : 2 * R, :], pair_sem.at[1], p.sibling(),
        )
        proj_pair[0:R, :] = grad_proj[:, pl.ds(pl.multiple_of(p.c * half, 128), half)]
        qv_sum[0:1, 0:D] = jnp.sum(grad_proj[:, 0:D].astype(f32), axis=0, keepdims=True)
        qv_sum[0:1, D:] = jnp.sum(grad_proj[:, 2 * D :].astype(f32), axis=0, keepdims=True)
        loads[11].wait()
        arrived(proj_pair.at[R : 2 * R, :], pair_sem.at[1])
        weight_grad(3, one, proj_pair, "qkv")
        run(BACK["input"])
        loads[10].wait()
        rows = 256
        r = wq.shape[1]

        @pl.loop(0, D // rows)
        def _(t):
            w = wq[pl.ds(t * (rows // r), rows // r)].reshape(rows, 3 * D)
            result[:, pl.ds(pl.multiple_of(t * rows, rows), rows)] = lax.dot_general(
                grad_proj[...], w, NT, preferred_element_type=f32
            )

        run(BACK["norm1"])
        loads[12].wait()
        gain = vector(smalls_f, places, "ln1_gain")

        @pl.loop(0, R // chunk)
        def _(t):
            at = pl.ds(pl.multiple_of(t * chunk, chunk), chunk)
            moved = norm_back(tokens_v[at, :].astype(f32), result[at, :], gain, 2)
            tokens_v[at, :] = (grad_middle[at, :] + moved).astype(bf16)

        cp = pltpu.make_async_copy(tokens_v, grad_tokens, load_sem.at[13])
        cp.start()
        values = dict(
            ln2_gain=sums[0:1, :], ln2_bias=sums[1:2, :], ln1_gain=sums[2:3, :],
            ln1_bias=sums[3:4, :], b_out=sums[4:5, :], b_proj=sums[5:6, :], b_fc=fc_sum[0:1, :],
            b_qv=qv_sum[0:1, :],
        )
        sm_mine[...] = jnp.zeros_like(sm_mine)
        last = 0
        for name, (start, size) in places.items():
            whole = values[name]
            for f in range(F):
                pos = start
                while pos < start + size:
                    row, lane = divmod(pos, 128)
                    count = min(128 - lane, start + size - pos)
                    at = f * size + pos - start
                    sm_mine[f, row : row + 1, lane : lane + count] = whole[:, at : at + count]
                    pos += count
            last = max(last, start + size)
        row = -(-last // 128)
        lane = lax.broadcasted_iota(jnp.int32, (1, 128), 1)
        line = jnp.zeros((1, 128), f32)
        for i in range(3):
            line = jnp.where(lane == i, jnp.sum(stats_v[i : i + 1, :], axis=1, keepdims=True), line)
        for f in range(F):
            sm_mine[f, row : row + 1, :] = line
        push(sm_mine, sm_core, sm_sem.at[0], p.sibling())
        run(BACK["small"][0])
        arrived(sm_core, sm_sem.at[0])
        sm_x[p.x] = sm_mine[...] + sm_core[...]
        for i in range(1, X):
            push(sm_x.at[p.x], sm_x.at[p.x], smx_sem.at[i - 1], p.across(i))
        run(BACK["small"][1])
        cp.wait()

    pl.run_scoped(
        projections,
        pltpu.VMEM(wq_in.shape, bf16),
        pltpu.VMEM((2 * R, D), bf16),
        pltpu.VMEM((R, D), bf16),
        pltpu.VMEM((R, D), f32),
        pltpu.VMEM((8, 2 * D), f32),
    )
    for i in range(1, X):
        arrived(sm_x.at[lax.rem(p.x + X - i, X)], smx_sem.at[i - 1])
    total = sm_x[0]
    for i in range(1, X):
        total = total + sm_x[i]
    sm_sum[...] = total
    for j in range(1, L):
        for k in range(H):
            h = lax.rem(p.h + k, H)
            push(sm_sum.at[ahead(k, j)], sm_lo.at[p.l, h], smlo_sem.at[j - 1, k], p.lo(j))
    run(BACK["small"][2])
    for k in list(range(1, H)) + [0]:
        h = lax.rem(p.h + k, H)
        sm_lo[p.l, h] = sm_sum[h * L + p.l]
        for j in range(1, L):
            arrived(sm_lo.at[lax.rem(p.l + L - j, L), h], smlo_sem.at[j - 1, k])
        total = sm_lo[0, h]
        for j in range(1, L):
            total = total + sm_lo[j, h]
        if k > 0:
            sm_core[h] = total
            push(sm_core.at[h], sm_hi.at[p.h], smhi_sem.at[k - 1], p.hi(k))
        else:
            sm_hi[p.h] = total
    run(BACK["end"])
    assert len(set(ran)) == len(ran) == 3 * len(slots) + 8
    for k in range(1, H):
        arrived(sm_hi.at[lax.rem(p.h + H - k, H)], smhi_sem.at[k - 1])
    total = sm_hi[0]
    for k in range(1, H):
        total = total + sm_hi[k]
    small_out[...] = total
    for w in range(4):
        arrived(half_out[w], core_sem.at[w])
        arrived(half_out[w], out_sem.at[w])
    arrived(gb_other, gb_sem.at[0])
    left = sum(sent)
    for rows in (2 * R, 256, 16):
        for lanes in (gbh.shape[1], 128):
            block = gbh.at[0:rows, 0:lanes]
            for _ in range(left // (2 * rows * lanes)):
                arrived(block, send_sem.at[0])
            left %= 2 * rows * lanes
    assert left == 0


def backward(cotangent, tokens, places, saved):
    F, S, H, L, X = geometry()
    R, D = tokens.shape
    wide, N, FF = D // S, R * S, saved[3].shape[2]
    pairs = wide // 128
    lead = max(X - 1, 1)
    plans = [column_plan(X, eighths) for eighths in BACK_SHARES]
    shapes = [(F, saved[i].shape[1], saved[i].shape[2] // 2) for i in (4, 3, 2, 1)]
    used = max(a + size for a, size in places.values())
    small_rows = -(-(-(-used // 128) + 1) // 8) * 8
    any_spec = pl.BlockSpec(memory_space=pl.ANY)
    vmem_spec = pl.BlockSpec(memory_space=pltpu.VMEM)
    V, D_SEM, shaped = pltpu.VMEM, pltpu.SemaphoreType.DMA, jax.ShapeDtypeStruct

    def each(shape_of, kind):
        return [
            V(shape_of(r, c, plan[1] * c // 8, plan[3] * c // 8), kind)
            for (f, r, c), plan in zip(shapes, plans)
        ]

    res = pl.pallas_call(
        functools.partial(backward_kernel, places),
        out_shape=[shaped((R, D), bf16)]
        + [shaped((r, 2 * c), f32) for f, r, c in shapes]
        + [shaped((small_rows, 128), f32)],
        in_specs=[vmem_spec] + [any_spec] * 17,
        out_specs=[any_spec] * 5 + [vmem_spec],
        scratch_shapes=[V(s, bf16) for s in shapes]
        + each(lambda r, c, reach, only: (lead, F, r, only), bf16)
        + each(lambda r, c, reach, only: (L - 1, H, r, reach), bf16)
        + each(lambda r, c, reach, only: (H - 1, r, reach), bf16)
        + each(lambda r, c, reach, only: (r, c), bf16)
        + each(lambda r, c, reach, only: (lead, r, c), bf16)
        + each(lambda r, c, reach, only: (r, c), f32)
        + [
            V((2 * R, D // 2), bf16),
            V((2 * R, FF // 2), bf16),
            V((R, FF // 2), bf16),
            V((R, D), f32),
            V((R, D), bf16),
            V((2 * R, D // 2), bf16),
            V((S - 1, R, wide), bf16),
            V((N, wide), bf16),
            V((pairs, N, 384), bf16),
            V((R, 3 * D), bf16),
            V((2 * R, 3 * D // 2), bf16),
            V((8, D), f32),
            V((8, FF), f32),
            V(saved[0].shape, f32),
            V((8, D), f32),
            V((F, small_rows, 128), f32),
            V((F, small_rows, 128), f32),
            V((X, F, small_rows, 128), f32),
            V((F, small_rows, 128), f32),
            V((L, H, small_rows, 128), f32),
            V((max(H, F), small_rows, 128), f32),
            D_SEM((14,)),
            D_SEM((2, 4)),
            D_SEM((1,)),
            D_SEM((4, lead, H, L)),
            D_SEM((4, L - 1, H)),
            D_SEM((4, H - 1)),
            D_SEM((4, lead)),
            D_SEM((4,)),
            D_SEM((4,)),
            D_SEM((2,)),
            D_SEM((S - 1,)),
            D_SEM((S - 1, pairs, 3)),
            D_SEM((1,)),
            D_SEM((lead,)),
            D_SEM((L - 1, H)),
            D_SEM((H - 1,)),
            D_SEM((2,)),
        ],
        compiler_params=pltpu.CompilerParams(
            collective_id=2, has_side_effects=True, vmem_limit_bytes=63 * 2**20
        ),
    )(cotangent, tokens, *saved)
    return res[0], res[1:5], res[5]


def hand_over(arrays, reduced, places, cells, pieces):
    used = max(a + size for a, size in places.values())
    row_of_sums = -(-used // 128)

    def kernel(*refs):
        n = len(arrays)
        given, small = refs[:n], refs[n]
        outs, vectors = refs[n + 1 : 2 * n + 1], refs[2 * n + 1 : 2 * n + 1 + len(places)]
        rms, held, in_sem, out_sem = refs[2 * n + 1 + len(places)], refs[-n - 2 : -2], refs[-2], refs[-1]
        coming, going = [], []
        for q in range(pieces):
            for i in range(n):
                rows = given[i].shape[0] // pieces
                at = pl.ds(q * rows, rows)
                coming.append(pltpu.make_async_copy(given[i].at[at], held[i].at[at], in_sem.at[i, q]))
                going.append(pltpu.make_async_copy(held[i].at[at], outs[i].at[at], out_sem.at[i, q]))
        for cp in coming:
            cp.start()
        for out, (start, size) in zip(vectors, places.values()):
            row, lane = divmod(start, 128)
            out[...] = small[row : row + out.shape[0], lane : lane + out.shape[1]]
        rms[...] = jnp.sqrt(small[row_of_sums : row_of_sums + 1, 0:3] / cells)
        for before, after in zip(coming, going):
            before.wait()
            after.start()
        for cp in going:
            cp.wait()

    any_spec, vmem_spec = pl.BlockSpec(memory_space=pl.ANY), pl.BlockSpec(memory_space=pltpu.VMEM)
    shaped = jax.ShapeDtypeStruct
    small_shapes = [shaped((max(1, s // 128), min(s, 128)), f32) for _, s in places.values()]
    res = pl.pallas_call(
        kernel,
        out_shape=[shaped(a.shape, a.dtype) for a in arrays] + small_shapes + [shaped((1, 3), f32)],
        in_specs=[any_spec] * len(arrays) + [vmem_spec],
        out_specs=[any_spec] * len(arrays) + [vmem_spec] * (len(places) + 1),
        scratch_shapes=[pltpu.VMEM(a.shape, a.dtype) for a in arrays]
        + [pltpu.SemaphoreType.DMA((len(arrays), pieces))] * 2,
        compiler_params=pltpu.CompilerParams(vmem_limit_bytes=62 * 2**20),
    )(*arrays, reduced)
    n = len(arrays)
    got = {name: v.reshape(-1) for name, v in zip(places, res[n:-1])}
    return res[:n], got, res[-1].reshape(-1)


def on_device(
    tokens, cotangent, ln1_gain, ln1_bias, w_qkv, b_qv, w_out, b_out,
    ln2_gain, ln2_bias, w_fc, b_fc, w_proj, b_proj,
):
    F, S = lax.axis_size("fsdp"), lax.axis_size("seq")
    row_count, D = tokens.shape
    named = dict(
        b_fc=b_fc, b_qv=b_qv, ln1_gain=ln1_gain, ln1_bias=ln1_bias, b_out=b_out,
        ln2_gain=ln2_gain, ln2_bias=ln2_bias, b_proj=b_proj,
    )
    places, at = {}, 0
    for name, value in named.items():
        places[name] = (at, value.shape[0])
        at += value.shape[0]
    small_rows = -(-at // 2048) * 16
    total = small_rows * 128
    flat = sum(
        jnp.pad(value, (a, total - a - size))
        for value, (a, size) in zip(named.values(), places.values())
    ).reshape(small_rows, 128)
    outs = forward(tokens, cotangent, flat, places, [w_qkv, w_out, w_fc, w_proj])
    wholes, saved, output, stats, cot_pair = outs[:4], outs[5:14], outs[14], outs[15], outs[16]
    grad_tokens, (grad_w_proj, grad_w_fc, grad_w_out, grad_w_qkv), reduced = backward(
        cotangent, tokens, places, [outs[4], *wholes, *saved, stats, cot_pair]
    )
    arrays, got, rms_values = hand_over(
        [output, grad_tokens, grad_w_qkv, grad_w_out, grad_w_fc, grad_w_proj], reduced, places,
        float(row_count * D * S * F), 2,
    )
    output, grad_tokens, grad_w_qkv, grad_w_out, grad_w_fc, grad_w_proj = arrays
    return (
        output, grad_tokens, got["ln1_gain"], got["ln1_bias"], grad_w_qkv, got["b_qv"],
        grad_w_out, got["b_out"], got["ln2_gain"], got["ln2_bias"], grad_w_fc, got["b_fc"],
        grad_w_proj, got["b_proj"], rms_values,
    )


def solution(mesh):
    in_specs = (
        P(("fsdp", "seq"), None),
        P(("fsdp", "seq"), None),
        P("fsdp"),
        P("fsdp"),
        P("fsdp", None),
        P("fsdp"),
        P("fsdp", None),
        P("fsdp"),
        P("fsdp"),
        P("fsdp"),
        P("fsdp", None),
        P("fsdp"),
        P("fsdp", None),
        P("fsdp"),
    )
    out_specs = (
        P(("fsdp", "seq"), None),
        P(("fsdp", "seq"), None),
        P("fsdp"),
        P("fsdp"),
        P("fsdp", None),
        P("fsdp"),
        P("fsdp", None),
        P("fsdp"),
        P("fsdp"),
        P("fsdp"),
        P("fsdp", None),
        P("fsdp"),
        P("fsdp", None),
        P("fsdp"),
        P(),
    )
    return jax.shard_map(
        on_device, mesh=mesh, in_specs=in_specs, out_specs=out_specs, check_vma=False
    )
```

```python
import functools
import math

import jax
import jax.numpy as jnp
from jax import lax
from jax.experimental import pallas as pl
from jax.experimental.pallas import tpu as pltpu
from jax.sharding import PartitionSpec as P

BLK = 256
HD = 64
EPSILON = 1e-05
MESH = pl.DeviceIdType.MESH
f32, bf16 = jnp.float32, jnp.bfloat16

def geometry():
    F, S = lax.axis_size("fsdp"), lax.axis_size("seq")
    return F, S, 4, F // 4, S // 2


class Place:
    def __init__(self):
        self.F, self.S, self.H, self.L, self.X = geometry()
        self.f, self.s = lax.axis_index("fsdp"), lax.axis_index("seq")
        self.h, self.l = self.f // self.L, self.f % self.L
        self.x, self.c = self.s // 2, self.s % 2

    def shard(self, k, j):
        return lax.rem(self.h + self.H - k, self.H) * self.L + lax.rem(self.l + self.L - j, self.L)

    def hi(self, k):
        return (lax.rem(self.h + k, self.H) * self.L + self.l, self.s)

    def lo(self, j):
        return (self.h * self.L + lax.rem(self.l + j, self.L), self.s)

    def across(self, i):
        return (self.f, lax.rem(self.x + i, self.X) * 2 + self.c)

    def sibling(self):
        return (self.f, self.x * 2 + 1 - self.c)

    def everyone(self):
        return (
            [self.hi(k) for k in range(1, self.H)]
            + [self.lo(j) for j in range(1, self.L)]
            + [(self.f, lax.rem(self.s + i, self.S)) for i in range(1, self.S)]
        )


def column_plan(X, eighths):
    if X == 2:
        return eighths, 8 - eighths, 8 - eighths, eighths
    return 8 // X, 8 // X, 8 // X, 8 // X


def greet(place):
    barrier = pltpu.get_barrier_semaphore()
    peers = place.everyone()
    for peer in peers:
        pl.semaphore_signal(barrier, inc=1, device_id=peer, device_id_type=MESH)
    pl.semaphore_wait(barrier, len(peers))


def vector(ref, places, name):
    at, size = places[name]
    parts = []
    for f in range(ref.shape[0]):
        pos = at
        while pos < at + size:
            row, lane = divmod(pos, 128)
            count = min(128 - lane, at + size - pos)
            parts.append(ref[f, row : row + 1, lane : lane + count])
            pos += count
    return jnp.concatenate(parts, axis=1)


def normalised(x):
    centre = x - jnp.mean(x, axis=-1, keepdims=True)
    return centre * lax.rsqrt(jnp.mean(centre * centre, axis=-1, keepdims=True) + EPSILON)


def gelu_and_slope(u):
    root = 0.7978845608028654
    square = u * u
    t = jnp.tanh(u * (root + root * 0.044715 * square))
    half = 0.5 * (1.0 + t)
    return u * half, half + u * (0.5 * (1.0 - t * t)) * (root + 3.0 * root * 0.044715 * square)


NT = (((1,), (1,)), ((), ()))
TN = (((0,), (0,)), ((), ()))


def head_lanes(shape, parity):
    lane = lax.broadcasted_iota(jnp.int32, shape, 1)
    return (lane // HD) == parity

def pick(rows, parity):
    return jnp.where(head_lanes(rows.shape, parity), rows, jnp.zeros_like(rows))

def turn(rows):
    return rows.astype(f32).T

def attend_block(i, pair, qkv, vT, scores, oT, lse):
    rows = pl.ds(i * BLK, BLK)

    @pl.loop(0, 128 // HD)
    def _(parity):
        h = pair * (128 // HD) + parity
        q = pick(qkv[pair, rows, 0:128], parity) * jnp.asarray(HD**-0.5, bf16)
        top = jnp.full((8, BLK), -jnp.inf, f32)
        for j in range(i + 1):
            k = qkv[pair, pl.ds(j * BLK, BLK), 128:256]
            s = lax.dot_general(k, q, NT, preferred_element_type=f32)
            scores[pl.ds(j * BLK, BLK), :] = s
            top = jnp.maximum(top, jnp.max(s.reshape(BLK // 8, 8, BLK), axis=0))
        top = jnp.max(top, axis=0, keepdims=True)
        total = jnp.zeros((8, BLK), f32)
        out = jnp.zeros((HD, BLK), f32)
        for j in range(i + 1):
            p = jnp.exp(scores[pl.ds(j * BLK, BLK), :] - top)
            total = total + jnp.sum(p.reshape(BLK // 8, 8, BLK), axis=0)
            v = vT[pl.ds(pl.multiple_of(h * HD, HD), HD), pl.ds(j * BLK, BLK)]
            out = out + jnp.dot(v, p.astype(bf16), preferred_element_type=f32)
        total = jnp.sum(total, axis=0, keepdims=True)
        oT[pl.ds(pl.multiple_of(parity * HD, HD), HD), :] = out * (1.0 / total)
        lse[pl.ds(h, 1), rows] = top + jnp.log(total)


def attend_back_block(i, pair, qkv, grad, kT, lse, delta, dqT, dk, dv):
    rows = pl.ds(i * BLK, BLK)
    here = pl.ds(pair * 128, 128)

    @pl.loop(0, 128 // HD)
    def _(parity):
        h = pair * (128 // HD) + parity
        out_rows = pl.ds(pl.multiple_of(parity * HD, HD), HD)
        q = pick(qkv[pair, rows, 0:128], parity) * jnp.asarray(HD**-0.5, bf16)
        g = pick(grad[rows, here], parity)
        low = lse[pl.ds(h, 1), rows]
        mean = delta[pl.ds(h, 1), rows]
        out = jnp.zeros((HD, BLK), f32)
        for j in range(i + 1):
            keys = pl.ds(j * BLK, BLK)
            k = qkv[pair, keys, 128:256]
            v = qkv[pair, keys, 256:384]
            p = jnp.exp(lax.dot_general(k, q, NT, preferred_element_type=f32) - low)
            dp = lax.dot_general(v, g, NT, preferred_element_type=f32)
            ds = (p * (dp - mean)).astype(bf16)
            dv[keys, :] += jnp.dot(p.astype(bf16), g, preferred_element_type=f32)
            dk[keys, :] += jnp.dot(ds, q, preferred_element_type=f32)
            kT_rows = kT[pl.ds(pl.multiple_of(h * HD, HD), HD), keys]
            out = out + jnp.dot(kT_rows, ds, preferred_element_type=f32)
        dqT[out_rows, :] = out * HD**-0.5


SHARES = (4, 2, 1, 2)
L_FIRST = (True, False, False, False)
SCHEDULE = (
    "y0 s0",
    "L00 y1 y2 y3 H01 H02 s1 H03 H11 H12 s2 H13 x0 c0 L10 L20 L30",
    "H21 L11",
    ("", "H22", "", "L21", "H23", "", "L22", "H31", "L23", "x1", "H32 c1", "L31"),
    ("L12 L13 s3", ""),
    "",
    "H33 L32 x2 c2",
    "L33",
)


def forward_kernel(places, *refs):
    refs = list(refs)

    def take(count):
        got = refs[:count]
        del refs[:count]
        return got

    tokens, cot, small = take(3)
    shards = take(4)
    big_outs = take(4)
    (small_out, one_out, qkv_out, lse_out, heads_out, mixed_out, middle_out, two_out, act_out,
     slope_out, result_out, stats_out, cot_out) = take(13)
    wholes = take(4)
    (smalls, smalls_f, one, split, qkv, vT, scores, oT, lse, heads, mixed, middle, two, act, slope,
     result, stats, vectors, wide_bias, stream) = take(20)
    (own_sem, send_sem, save_sem, hi_sem, lo_sem, x_sem, core_sem, sm_hi_sem, sm_lo_sem, there_sem,
     back_sem, pair_sem, last_sem) = refs
    p = Place()
    S, H, L, X, F = p.S, p.H, p.L, p.X, p.F
    rows_here, D = tokens.shape
    wide = D // S
    saved = []

    def push(src, dst, sem, peer, kind=0):
        pltpu.make_async_remote_copy(
            src_ref=src, dst_ref=dst, send_sem=send_sem.at[kind], recv_sem=sem, device_id=peer,
            device_id_type=MESH,
        ).start()

    def arrived(dst, sem):
        pltpu.make_async_copy(dst, dst, sem).wait()

    def save(src, dst):
        cp = pltpu.make_async_copy(src, dst, save_sem.at[len(saved)])
        cp.start()
        saved.append(cp)

    def share(src, dst, index):
        save(src, dst.at[0:rows_here])
        push(src, dst.at[rows_here:], pair_sem.at[index], p.sibling())

    own = []
    for w in range(4):
        own.append(pltpu.make_async_copy(shards[w], wholes[w].at[p.f], own_sem.at[w]))
    own.append(pltpu.make_async_copy(small, smalls.at[p.f], own_sem.at[4]))
    for cp in own:
        cp.start()
    greet(p)

    plans = [column_plan(X, eighths) for eighths in SHARES]

    def cols(w, start, count):
        C = shards[w].shape[-1]
        return pl.ds(pl.multiple_of(p.c * (C // 2) + start * (C // 16), 128), count * (C // 16))

    def fetched(w):
        return cols(w, plans[w][0] * p.x, plans[w][1])

    def only(w, x):
        return cols(w, plans[w][2] * x, plans[w][3])

    def half(w, core):
        C = shards[w].shape[-1]
        return pl.ds(pl.multiple_of(core * (C // 2), 128), C // 2)

    def up():
        return ((p.h + 1) * L + p.l, p.s)

    def down():
        return ((p.h - 1) * L + p.l, p.s)

    def both_ways(w, src, f, j):
        dst = wholes[w].at[f, :, fetched(w)]

        @pl.when(p.h < H - 1)
        def _():
            push(src, dst, hi_sem.at[w, 0, 0, j], up(), 1)

        @pl.when(p.h > 0)
        def _():
            push(src, dst, hi_sem.at[w, 1, 0, j], down(), 1)

    def start(w):
        both_ways(w, shards[w].at[:, fetched(w)], p.f, 0)

    def start_lo(w):
        src, dst = shards[w].at[:, fetched(w)], wholes[w].at[p.f, :, fetched(w)]
        for j in range(1, L):
            push(src, dst, lo_sem.at[w, j - 1, p.h], p.lo(j))

    def over_x(w, f):
        piece = wholes[w].at[f, :, only(w, p.x)]
        for i in range(1, X):
            push(piece, piece, x_sem.at[w, i - 1, f], p.across(i))

    def from_hi(w, d, below):
        origin = p.h - d if below else p.h + d
        side = 0 if below else 1

        @pl.when(origin >= 0 if below else origin < H)
        def _():
            for j in range(L) if L_FIRST[w] else [0]:
                f = origin * L + lax.rem(p.l + L - j, L)
                piece = wholes[w].at[f, :, fetched(w)]
                arrived(piece, hi_sem.at[w, side, d - 1, j])
                if d < H - 1:

                    @pl.when(p.h < H - 1 if below else p.h > 0)
                    def _():
                        push(piece, piece, hi_sem.at[w, side, d, j], up() if below else down(), 1)

            if not L_FIRST[w]:
                for j in range(1, L):
                    push(piece, piece, lo_sem.at[w, j - 1, origin], p.lo(j))

    def origins(visit, own):
        if own:
            visit(p.h)
        for d in range(1, H):

            @pl.when(p.h >= d)
            def _():
                visit(p.h - d)

            @pl.when(p.h + d < H)
            def _():
                visit(p.h + d)

    def from_lo(w, d, below):
        def visit(origin):
            for j in range(1, L):
                f = origin * L + lax.rem(p.l + L - j, L)
                piece = wholes[w].at[f, :, fetched(w)]
                arrived(piece, lo_sem.at[w, j - 1, origin])
                if L_FIRST[w]:
                    both_ways(w, piece, f, j)

        at_distance(d, below, visit)

    def at_distance(d, below, visit):
        if d == 0:
            visit(p.h)
            return
        origin = p.h - d if below else p.h + d
        pl.when(origin >= 0 if below else origin < H)(lambda: visit(origin))

    def out_x(w, d, below, lo):
        def visit(origin):
            for j in range(1, L) if lo else [0]:
                over_x(w, origin * L + lax.rem(p.l + L - j, L))

        at_distance(d, below, visit)

    def from_x(w, j):
        def visit(origin):
            f = origin * L + lax.rem(p.l + L - j, L)
            for i in range(1, X):
                theirs = only(w, lax.rem(p.x + X - i, X))
                arrived(wholes[w].at[f, :, theirs], x_sem.at[w, i - 1, f])
            piece = wholes[w].at[f, :, half(w, p.c)]
            push(piece, piece, core_sem.at[w, f], p.sibling())

        origins(visit, j > 0)

    def from_core(w):
        for j in range(L):

            def visit(origin):
                f = origin * L + lax.rem(p.l + L - j, L)
                arrived(wholes[w].at[f, :, half(w, 1 - p.c)], core_sem.at[w, f])

            origins(visit, j > 0)
        own[w].wait()
        save(wholes[w], big_outs[w])

    def run(names):
        for name in names.split():
            kind, w, d = name[0], int(name[1]), int(name[2:] or 0)
            sides = (True, False) if d else (True,)
            if kind == "s":
                start(w)
            elif kind == "y":
                start_lo(w)
            elif kind == "x":
                for j in range(L):
                    from_x(w, j)
            elif kind == "c":
                from_core(w)
            else:
                for below in sides:
                    if kind in "hH":
                        from_hi(w, d, below)
                    if kind in "lL":
                        from_lo(w, d, below)
                    if kind in "pH":
                        out_x(w, d, below, False)
                    if kind in "qL" or kind == "H" and L_FIRST[w]:
                        out_x(w, d, below, True)

    push(
        cot.at[:, pl.ds(pl.multiple_of((1 - p.c) * (D // 2), 128), D // 2)],
        cot_out, pair_sem.at[4], p.sibling(),
    )
    for k in range(1, H):
        push(small, smalls.at[p.f], sm_hi_sem.at[k - 1], p.hi(k))
    for j in range(1, L):
        push(small, smalls.at[p.f], sm_lo_sem.at[j - 1, 0], p.lo(j))
    run(SCHEDULE[0])
    for k in range(1, H):
        piece = smalls.at[p.shard(k, 0)]
        arrived(piece, sm_hi_sem.at[k - 1])
        for j in range(1, L):
            push(piece, piece, sm_lo_sem.at[j - 1, k], p.lo(j))
    for j in range(1, L):
        for k in range(H):
            arrived(smalls.at[p.shard(k, j)], sm_lo_sem.at[j - 1, k])
    own[4].wait()
    smalls_f[...] = smalls[...].astype(f32)
    save(smalls_f, small_out)
    vec = functools.partial(vector, smalls_f, places)

    chunk = 128
    stats[...] = jnp.zeros_like(stats)
    gain, shift = vec("ln1_gain"), vec("ln1_bias")

    @pl.loop(0, rows_here // chunk)
    def _(t):
        at = pl.ds(pl.multiple_of(t * chunk, chunk), chunk)
        x = tokens[at, :].astype(f32)
        stats[0:1, :] += jnp.sum(x * x, axis=0, keepdims=True)
        one[at, :] = (normalised(x) * gain + shift).astype(bf16)

    share(one, one_out, 0)
    run(SCHEDULE[1])

    bias_qv = vec("b_qv")

    def project(kind, target):
        at = pl.multiple_of(kind * D + target * wide, 128)
        w = wholes[0][:, :, pl.ds(at, wide)].reshape(D, wide)
        return jnp.dot(one[...], w, preferred_element_type=f32)

    vectors[0:1, :] = bias_qv[:, :D]
    vectors[1:2, :] = bias_qv[:, D:]

    def heads_of(target):
        lanes = pl.ds(pl.multiple_of(target * wide, 128), wide)
        return [
            (project(0, target) + vectors[0:1, lanes]).astype(bf16),
            project(1, target).astype(bf16),
            (project(2, target) + vectors[1:2, lanes]).astype(bf16),
        ]

    mine = pl.ds(pl.multiple_of(p.s * rows_here, 128), rows_here)
    pairs = wide // 128

    def send_pair(i, pair):
        push(
            split.at[i - 1, pair], qkv.at[pair, mine, :], there_sem.at[i - 1, pair],
            (p.f, lax.rem(p.s + i, S)),
        )

    for i in list(range(1, S)) + [0]:
        target = lax.rem(p.s + i, S)
        for kind, values in enumerate(heads_of(target)):
            for pair in range(pairs):
                block = values[:, pair * 128 : (pair + 1) * 128]
                if i == 0:
                    qkv[pair, mine, kind * 128 : (kind + 1) * 128] = block
                else:
                    split[i - 1, pair, :, kind * 128 : (kind + 1) * 128] = block
        if i:
            send_pair(i, 0)
    run(SCHEDULE[2])

    length = qkv.shape[1]
    blocks = length // BLK
    lse[...] = jnp.zeros_like(lse)
    passed = set()
    for pair in range(pairs):
        for i in range(1, S):
            source = lax.rem(p.s + S - i, S)
            there = pl.ds(pl.multiple_of(source * rows_here, 128), rows_here)
            arrived(qkv.at[pair, there, :], there_sem.at[i - 1, pair])
        if pair + 1 < pairs:
            for i in range(1, S):
                send_pair(i, pair + 1)
        else:
            save(qkv, qkv_out)
        run(SCHEDULE[4][pair] if pair < 2 else "")
        for b in range(blocks):
            at = pl.ds(b * BLK, BLK)
            vT[pair * 128 : (pair + 1) * 128, at] = turn(qkv[pair, at, 256:384]).astype(bf16)
        lanes = pl.ds(pl.multiple_of(p.s * wide + pair * 128, 128), 128)
        here = pl.ds(pair * 128, 128)
        sent_back = 0
        for i in range(blocks):
            attend_block(i, pair, qkv, vT, scores, oT, lse)
            heads[pl.ds(i * BLK, BLK), here] = turn(oT[...]).astype(bf16)
            while (sent_back + 1) * rows_here <= (i + 1) * BLK:
                rows = pl.ds(sent_back * rows_here, rows_here)

                @pl.when(p.s != sent_back)
                def _():
                    pltpu.make_async_remote_copy(
                        src_ref=heads.at[rows, here], dst_ref=mixed.at[:, lanes],
                        send_sem=send_sem.at[2], recv_sem=back_sem.at[p.s, pair],
                        device_id=(p.f, jnp.int32(sent_back)), device_id_type=MESH,
                    ).start()

                @pl.when(p.s == sent_back)
                def _():
                    mixed[:, lanes] = heads[rows, here]

                sent_back += 1
            at = (pair * blocks + i) * 12 // (pairs * blocks)
            run(SCHEDULE[3][at] if at not in passed else "")
            passed.add(at)
    if pairs == 1:
        run(SCHEDULE[4][1])
    save(heads, heads_out)
    save(lse, lse_out)
    run(SCHEDULE[5])
    for i in range(1, S):
        source = lax.rem(p.s + S - i, S)
        for pair in range(pairs):
            lanes = pl.ds(pl.multiple_of(source * wide + pair * 128, 128), 128)
            arrived(mixed.at[:, lanes], back_sem.at[source, pair])
    share(mixed, mixed_out, 1)

    tile = 256
    vectors[0:1, :] = vec("b_out")

    @pl.loop(0, D // tile)
    def _(t):
        at = pl.ds(pl.multiple_of(t * tile, tile), tile)
        w = wholes[1][:, :, at].reshape(D, tile)
        branch = jnp.dot(mixed[...], w, preferred_element_type=f32) + vectors[0:1, at]
        middle[:, at] = tokens[:, at].astype(f32) + branch

    save(middle, middle_out)
    gain_two, shift_two = vec("ln2_gain"), vec("ln2_bias")

    @pl.loop(0, rows_here // chunk)
    def _(t):
        at = pl.ds(pl.multiple_of(t * chunk, chunk), chunk)
        x = middle[at, :]
        stats[1:2, :] += jnp.sum(x * x, axis=0, keepdims=True)
        two[at, :] = (normalised(x) * gain_two + shift_two).astype(bf16)

    share(two, two_out, 2)
    run(SCHEDULE[6])
    wide_bias[0:1, :] = vec("b_fc")

    FF = act.shape[1]

    @pl.loop(0, FF // tile)
    def _(t):
        at = pl.ds(pl.multiple_of(t * tile, tile), tile)
        w = wholes[2][:, :, at].reshape(D, tile)
        u = jnp.dot(two[...], w, preferred_element_type=f32) + wide_bias[0:1, at]
        act_rows, slope_rows = gelu_and_slope(u)
        act[:, at] = act_rows.astype(bf16)
        slope[:, at] = slope_rows.astype(bf16)

    share(act, act_out, 3)
    save(slope, slope_out)
    vectors[0:1, :] = vec("b_proj")
    stream[...] = middle[...] + vectors[0:1, :]

    def multiply(f):
        lanes = pl.ds(pl.multiple_of(f * (FF // F), 128), FF // F)
        stream[...] += jnp.dot(act[:, lanes], wholes[3][f], preferred_element_type=f32)
        pltpu.make_async_copy(wholes[3].at[f], big_outs[3].at[f], last_sem.at[0]).start()

    own[3].wait()
    multiply(p.f)
    run(SCHEDULE[7])
    for j in range(L):
        from_x(3, j)

        @pl.loop(0 if j else 1, 2 * H - 1)
        def _(q):
            d = lax.div(q + 1, 2)
            origin = jnp.where(lax.rem(q, 2) == 1, p.h - d, p.h + d)

            @pl.when((origin >= 0) & (origin < H))
            def _():
                f = origin * L + lax.rem(p.l + L - j, L)
                arrived(wholes[3].at[f, :, half(3, 1 - p.c)], core_sem.at[3, f])
                multiply(f)

    @pl.loop(0, rows_here // chunk)
    def _(t):
        at = pl.ds(pl.multiple_of(t * chunk, chunk), chunk)
        x = stream[at, :]
        stats[2:3, :] += jnp.sum(x * x, axis=0, keepdims=True)
        result[at, :] = x.astype(bf16)

    save(result, result_out)
    save(stats, stats_out)
    for index, there in enumerate((one_out, mixed_out, two_out, act_out)):
        arrived(there.at[rows_here:], pair_sem.at[index])
    arrived(cot_out, pair_sem.at[4])
    moves = jnp.where(p.h < H - 1, p.h + 1, 0) + jnp.where(p.h > 0, H - p.h, 0)
    for w in range(4):
        piece = wholes[w].at[0, :, fetched(w)]

        @pl.loop(0, moves * (L if L_FIRST[w] else 1))
        def _(_):
            arrived(piece, send_sem.at[1])

        for _ in range((1 if L_FIRST[w] else H) * (L - 1)):
            arrived(piece, send_sem.at[0])
        for _ in range((F - 1) * (X - 1)):
            arrived(wholes[w].at[0, :, only(w, 0)], send_sem.at[0])
        for _ in range(F - 1):
            arrived(wholes[w].at[0, :, half(w, 0)], send_sem.at[0])
    for _ in range(H - 1 + H * (L - 1)):
        arrived(smalls.at[0], send_sem.at[0])
    for i in range(S - 1):
        arrived(split.at[i], send_sem.at[0])
        arrived(heads.at[pl.ds(0, rows_here)], send_sem.at[2])
    for there in (one_out, mixed_out, two_out, act_out):
        arrived(there.at[rows_here:], send_sem.at[0])
    arrived(cot_out, send_sem.at[0])
    arrived(wholes[3], last_sem.at[0])
    for cp in saved:
        cp.wait()


def forward(tokens, cotangent, packed, places, shards):
    F, S, H, L, X = geometry()
    rows_here, D = tokens.shape
    wide, length, FF = D // S, rows_here * S, shards[2].shape[1]
    heads = max(8, wide // HD)
    lead = max(X - 1, 1)
    any_spec = pl.BlockSpec(memory_space=pl.ANY)
    V, D_SEM = pltpu.VMEM, pltpu.SemaphoreType.DMA
    shaped = jax.ShapeDtypeStruct
    wholes = [(F,) + a.shape for a in shards]
    outs = [shaped(s, bf16) for s in wholes] + [
        shaped((F,) + packed.shape, f32),
        shaped((2 * rows_here, D), bf16),
        shaped((wide // 128, length, 384), bf16),
        shaped((heads, length), f32),
        shaped((length, wide), bf16),
        shaped((2 * rows_here, D), bf16),
        shaped((rows_here, D), f32),
        shaped((2 * rows_here, D), bf16),
        shaped((2 * rows_here, FF), bf16),
        shaped((rows_here, FF), bf16),
        shaped((rows_here, D), bf16),
        shaped((8, D), f32),
        shaped((rows_here, D // 2), bf16),
    ]
    return pl.pallas_call(
        functools.partial(forward_kernel, places),
        out_shape=outs,
        in_specs=[pl.BlockSpec(memory_space=pltpu.VMEM)] + [any_spec] * 6,
        out_specs=[any_spec] * len(outs),
        scratch_shapes=[V(s, bf16) for s in wholes]
        + [
            V((F,) + packed.shape, bf16),
            V((F,) + packed.shape, f32),
            V((rows_here, D), bf16),
            V((S - 1, wide // 128, rows_here, 384), bf16),
            V((wide // 128, length, 384), bf16),
            V((wide, length), bf16),
            V((length, BLK), f32),
            V((128, BLK), f32),
            V((heads, length), f32),
            V((length, wide), bf16),
            V((rows_here, D), bf16),
            V((rows_here, D), f32),
            V((rows_here, D), bf16),
            V((rows_here, FF), bf16),
            V((rows_here, FF), bf16),
            V((rows_here, D), bf16),
            V((8, D), f32),
            V((8, D), f32),
            V((8, FF), f32),
            V((rows_here, D), f32),
            D_SEM((5,)),
            D_SEM((3,)),
            D_SEM((len(outs) + 8,)),
            D_SEM((4, 2, H - 1, L)),
            D_SEM((4, L - 1, H)),
            D_SEM((4, lead, F)),
            D_SEM((4, F)),
            D_SEM((H - 1,)),
            D_SEM((L - 1, H)),
            D_SEM((S - 1, wide // 128)),
            D_SEM((S, wide // 128)),
            D_SEM((5,)),
            D_SEM((1,)),
        ],
        compiler_params=pltpu.CompilerParams(
            collective_id=1, has_side_effects=True, vmem_limit_bytes=60 * 2**20
        ),
    )(tokens, cotangent, packed, *shards)


BACK_SHARES = (2, 1, 2, 2)
BACK = dict(
    first="x0",
    feed=("y0", "x1", "", "y1 x2", "", "x3 z0 y2", "", ""),
    norm="",
    mixed="z1 y3",
    fc=("", "x4", "", "z2 y4"),
    out=("", "", "", ""),
    attention=("x5", "", "z3 y5", "", "x6 v0", "", "z4 y6", "e0", "x7", "", "z5 y7", "x8 x9"),
    sent="x10 x11 z6 y8",
    back="z7 y9",
    qkv=("x12 z8", "x13 y12", "x14 z9 y13", "x15"),
    input="z12 y14 v1",
    norm1="z13 y15",
    small=("z14 y10 y11 e1", "z15", "v3 z10 z11 v2"),
    end="e3 e2",
)


def backward_kernel(places, *refs):
    refs = list(refs)

    def take(count):
        got = refs[:count]
        del refs[:count]
        return got

    cot, = take(1)
    (tokens, smalls, wq_in, wo_in, wf_in, wp_in, one_in, qkv_in, lse_in, heads_in, mixed_in,
     middle_in, two_in, act_in, slope_in, stats, cot_in) = take(17)
    grad_tokens, = take(1)
    outs = take(4)
    small_out, = take(1)
    parts, from_x, from_lo, from_hi, value, from_x_end, half_out = (take(4) for _ in range(7))
    (cot_pair, gbh, gb_other, grad_middle, branch, branch_pair, leaving, grad_heads, grad_qkv,
     grad_proj, proj_pair, sums, fc_sum, smalls_f, stats_v) = take(15)
    sm_mine, sm_core, sm_x, sm_sum, sm_lo, sm_hi = take(6)
    (load_sem, slot_sem, send_sem, x_sem, lo_sem, hi_sem, end_sem, out_sem, core_sem, pair_sem, to_sem,
     from_sem, sm_sem, smx_sem, smlo_sem, smhi_sem, gb_sem) = refs
    p = Place()
    S, H, L, X, F = p.S, p.H, p.L, p.X, p.F
    R, D = cot.shape
    FF = fc_sum.shape[1]
    wide = D // S
    N = R * S
    plans = [column_plan(X, eighths) for eighths in BACK_SHARES]
    sent = []

    def push(src, dst, sem, peer):
        pltpu.make_async_remote_copy(
            src_ref=src, dst_ref=dst, send_sem=send_sem.at[0], recv_sem=sem, device_id=peer,
            device_id_type=MESH,
        ).start()
        sent.append(math.prod(src.shape) * src.dtype.itemsize)

    def arrived(dst, sem):
        pltpu.make_async_copy(dst, dst, sem).wait()

    loads = {}

    def load(index, src, dst):
        loads[index] = pltpu.make_async_copy(src, dst, load_sem.at[index])
        loads[index].start()

    def eighths(w, start, count):
        unit = parts[w].shape[-1] // 8
        return pl.ds(pl.multiple_of(start * unit, 128), count * unit)

    def reach(w, x):
        return eighths(w, plans[w][0] * x, plans[w][1])

    def only(w, x):
        return eighths(w, plans[w][2] * x, plans[w][3])

    def ahead(k, j):
        return lax.rem(p.h + k, H) * L + lax.rem(p.l + j, L)

    steps = [H // 2] + [k for k in range(1, H) if k != H // 2] + [0]
    slots = [(w, k) for w in range(4) for k in steps]

    def shards_of(k):
        return pl.ds(lax.rem(p.h + k, H) * L, L)

    def send_x(w, k):
        for j in list(range(1, L)) + [0]:
            f = ahead(k, j)
            for i in range(1, X):
                push(
                    parts[w].at[f, :, only(w, lax.rem(p.x + i, X))], from_x[w].at[i - 1, f],
                    x_sem.at[w, i - 1, k, j], p.across(i),
                )

    def add_x(w, k, j):
        f = ahead(k, j)
        if X > 1:
            total = parts[w][f, :, only(w, p.x)].astype(f32)
            for i in range(1, X):
                came = from_x[w].at[i - 1, f]
                arrived(came, x_sem.at[w, i - 1, k, j])
                total = total + came[...].astype(f32)
            parts[w][f, :, only(w, p.x)] = total.astype(bf16)

    def send_lo(w, k):
        for j in range(1, L):
            add_x(w, k, j)
            push(
                parts[w].at[ahead(k, j), :, reach(w, p.x)],
                from_lo[w].at[j - 1, lax.rem(p.h + k, H)], lo_sem.at[w, j - 1, k], p.lo(j),
            )

    def add_lo(w, k):
        f = ahead(k, 0)
        add_x(w, k, 0)
        cols = reach(w, p.x)
        total = parts[w][f, :, cols].astype(f32)
        for j in range(1, L):
            came = from_lo[w].at[j - 1, lax.rem(p.h + k, H)]
            arrived(came, lo_sem.at[w, j - 1, k])
            total = total + came[...].astype(f32)
        parts[w][f, :, cols] = total.astype(bf16)
        if k > 0:
            push(parts[w].at[f, :, cols], from_hi[w].at[k - 1], hi_sem.at[w, k - 1], p.hi(k))

    def add_hi(w):
        cols = reach(w, p.x)
        total = parts[w][p.f, :, cols].astype(f32)
        for k in range(1, H):
            arrived(from_hi[w].at[k - 1], hi_sem.at[w, k - 1])
            total = total + from_hi[w][k - 1].astype(f32)
        value[w][:, cols] = total.astype(bf16)
        for i in range(1, X):
            push(
                value[w].at[:, cols], from_x_end[w].at[i - 1, :, cols], end_sem.at[w, i - 1],
                p.across(i),
            )

    def finish(w):
        mine = only(w, p.x)
        half_out[w][:, mine] = value[w][:, mine].astype(f32)
        for i in range(1, X):
            source = lax.rem(p.x + X - i, X)
            cols = reach(w, source)
            arrived(from_x_end[w].at[i - 1, :, cols], end_sem.at[w, i - 1])
            theirs = only(w, source)
            half_out[w][:, theirs] = from_x_end[w][i - 1, :, theirs].astype(f32)
        if X == 2 and plans[w][3] < 4:
            both = eighths(w, plans[w][3], 8 - 2 * plans[w][3])
            total = value[w][:, both].astype(f32)
            for i in range(1, X):
                total = total + from_x_end[w][i - 1, :, both].astype(f32)
            half_out[w][:, both] = total
        there = outs[w].at[:, eighths(w, p.c * 8, 8)]
        push(half_out[w], there, core_sem.at[w], p.sibling())
        pltpu.make_async_copy(half_out[w], there, out_sem.at[w]).start()

    ran = []

    def run(names):
        for name in names.split():
            kind, n = name[0], int(name[1:])
            ran.append(name)
            if kind == "x":
                send_x(*slots[n])
            elif kind == "y":
                send_lo(*slots[n])
            elif kind == "z":
                add_lo(*slots[n])
            elif kind == "v":
                add_hi(n)
            else:
                finish(n)

    load(0, cot_in, cot_pair.at[R : 2 * R])
    cot_pair[0:R, :] = cot[:, pl.ds(pl.multiple_of(p.c * (D // 2), 128), D // 2)]
    load(1, smalls, smalls_f)
    load(2, stats, stats_v)
    greet(p)

    tile = FF // F
    grad_middle[...] = jnp.zeros_like(grad_middle)

    def feed_forward(wp, wf, act, slope):
        tiles = [lax.rem(p.h + k, H) * L + j for k in steps for j in range(L)]

        def fetch(t, f):
            slot = t % 2
            cols = pl.ds(pl.multiple_of(f * tile, 128), tile)
            return [
                pltpu.make_async_copy(wp_in.at[f], wp.at[slot], slot_sem.at[slot, 0]),
                pltpu.make_async_copy(wf_in.at[:, :, cols], wf.at[slot], slot_sem.at[slot, 1]),
                pltpu.make_async_copy(slope_in.at[:, cols], slope.at[slot], slot_sem.at[slot, 3]),
            ]

        def fetch_act(t):
            if t < len(tiles):
                cols = pl.ds(pl.multiple_of(tiles[t] * tile, 128), tile)
                arriving[t] = pltpu.make_async_copy(
                    act_in.at[:, cols], act.at[t % 2], slot_sem.at[t % 2, 2]
                )
                arriving[t].start()

        def proj_grad(t):
            if t < len(tiles):
                arriving[t].wait()
                grad = lax.dot_general(act[t % 2], cot_pair[...], TN, preferred_element_type=f32)
                parts[0][tiles[t]] = grad.astype(bf16)
                fetch_act(t + 2)

        arriving = {}
        fetch_act(0)
        fetch_act(1)
        coming = fetch(0, tiles[0])
        for cp in coming:
            cp.start()
        loads[0].wait()
        for t in range(L):
            proj_grad(t)
        run(BACK["first"])
        for t, f in enumerate(tiles):
            for cp in coming:
                cp.wait()
            if t + 1 < len(tiles):
                coming = fetch(t + 1, tiles[t + 1])
                for cp in coming:
                    cp.start()
            slot = t % 2
            proj_grad(t + L)
            grad_act = lax.dot_general(cot[...], wp[slot], NT, preferred_element_type=f32)
            before = (slope[slot].astype(f32) * grad_act).astype(bf16)
            fc_sum[0:1, pl.ds(pl.multiple_of(f * tile, 128), tile)] = jnp.sum(
                before.astype(f32), axis=0, keepdims=True
            )
            at = pl.ds(pl.multiple_of(lax.rem(f, F // 2) * tile, 128), tile)

            @pl.when(f // (F // 2) == p.c)
            def _():
                gbh[0:R, at] = before

            @pl.when(f // (F // 2) != p.c)
            def _():
                gb_other[:, at] = before
                pltpu.make_async_remote_copy(
                    src_ref=gb_other.at[:, at], dst_ref=gbh.at[R : 2 * R, at], send_sem=gb_sem.at[0],
                    recv_sem=gb_sem.at[1], device_id=p.sibling(), device_id_type=MESH,
                ).start()

            grad_middle[...] += lax.dot_general(
                before, wf[slot].reshape(D, tile), NT, preferred_element_type=f32
            )
            if (2 * t + 2) % L == 0:
                run(BACK["feed"][(2 * t + 2) // L - 1])

    pl.run_scoped(
        feed_forward,
        pltpu.VMEM((2,) + wp_in.shape[1:], bf16),
        pltpu.VMEM((2,) + wf_in.shape[:2] + (tile,), bf16),
        pltpu.VMEM((2, 2 * R, tile), bf16),
        pltpu.VMEM((2, R, tile), bf16),
    )

    chunk = 128
    sums[...] = jnp.zeros_like(sums)
    loads[1].wait()
    loads[2].wait()

    def norm_back(rows, grad, gain, first):
        centre = rows - jnp.mean(rows, axis=-1, keepdims=True)
        scale = lax.rsqrt(jnp.mean(centre * centre, axis=-1, keepdims=True) + EPSILON)
        n = centre * scale
        sums[first : first + 1, :] += jnp.sum(grad * n, axis=0, keepdims=True)
        sums[first + 1 : first + 2, :] += jnp.sum(grad, axis=0, keepdims=True)
        scaled = grad * gain
        return scale * (
            scaled
            - jnp.mean(scaled, axis=-1, keepdims=True)
            - n * jnp.mean(scaled * n, axis=-1, keepdims=True)
        )

    def weight_grad(w, rows_pair, columns_pair, hook):
        r = parts[w].shape[1]
        for t, k in enumerate(steps):
            at = pl.ds(pl.multiple_of(lax.rem(p.h + k, H) * (L * r), 128), L * r)
            grad = lax.dot_general(
                rows_pair[:, at], columns_pair[...], TN, preferred_element_type=f32
            )
            parts[w][shards_of(k)] = grad.astype(bf16).reshape(L, r, grad.shape[1])
            run(BACK[hook][t])

    def attention_output(middle, wo, two, mixed):
        load(3, middle_in, middle)
        load(4, wo_in, wo)
        load(5, two_in, two)
        load(6, mixed_in, mixed)
        gain = vector(smalls_f, places, "ln2_gain")
        loads[3].wait()

        @pl.loop(0, R // chunk)
        def _(t):
            at = pl.ds(pl.multiple_of(t * chunk, chunk), chunk)
            out = cot[at, :].astype(f32)
            sums[5:6, :] += jnp.sum(out, axis=0, keepdims=True)
            total = out + norm_back(middle[at, :], grad_middle[at, :], gain, 0)
            grad_middle[at, :] = total
            rounded = total.astype(bf16)
            branch[at, :] = rounded
            sums[4:5, :] += jnp.sum(rounded.astype(f32), axis=0, keepdims=True)

        half = D // 2
        run(BACK["norm"])
        branch_pair[0:R, :] = branch[:, pl.ds(pl.multiple_of(p.c * half, 128), half)]
        push(
            branch.at[:, pl.ds(pl.multiple_of((1 - p.c) * half, 128), half)],
            branch_pair.at[R : 2 * R, :], pair_sem.at[0], p.sibling(),
        )
        loads[4].wait()
        r = wo.shape[1]
        mine = pl.ds(pl.multiple_of(p.s * R, 128), R)
        for i in list(range(1, S)) + [0]:
            target = lax.rem(p.s + i, S)
            rows = wo[pl.ds(target * (wide // r), wide // r)].reshape(wide, D)
            grad = lax.dot_general(branch[...], rows, NT, preferred_element_type=f32).astype(bf16)
            if i:
                leaving[i - 1] = grad
                push(leaving.at[i - 1], grad_heads.at[mine, :], to_sem.at[i - 1], (p.f, target))
            else:
                grad_heads[mine, :] = grad
        run(BACK["mixed"])
        loads[5].wait()
        arrived(gbh.at[R : 2 * R, :], gb_sem.at[1])
        weight_grad(1, two, gbh, "fc")
        loads[6].wait()
        arrived(branch_pair.at[R : 2 * R, :], pair_sem.at[0])
        weight_grad(2, mixed, branch_pair, "out")

    pl.run_scoped(
        attention_output,
        pltpu.VMEM((R, D), f32),
        pltpu.VMEM(wo_in.shape, bf16),
        pltpu.VMEM((2 * R, D), bf16),
        pltpu.VMEM((2 * R, D), bf16),
    )

    pairs = wide // 128

    def attention(qkv, heads, lse, kT, delta, dqT, dk, dv):
        load(7, qkv_in, qkv)
        load(8, heads_in, heads)
        load(9, lse_in, lse)
        for i in range(1, S):
            source = lax.rem(p.s + S - i, S)
            arrived(grad_heads.at[pl.ds(pl.multiple_of(source * R, 128), R), :], to_sem.at[i - 1])
        for index in (7, 8, 9):
            loads[index].wait()
        shape = (lse.shape[0], wide)
        chosen = lax.broadcasted_iota(jnp.int32, shape, 1) // HD == lax.broadcasted_iota(jnp.int32, shape, 0)
        chosen = jnp.where(chosen, 1.0, 0.0).astype(bf16)
        for b in range(N // BLK):
            at = pl.ds(b * BLK, BLK)
            for pair in range(pairs):
                kT[pair * 128 : (pair + 1) * 128, at] = turn(qkv[pair, at, 128:256]).astype(bf16)
            product = grad_heads[at, :].astype(f32) * heads[at, :].astype(f32)
            high = product.astype(bf16)
            low = (product - high.astype(f32)).astype(bf16)
            delta[:, at] = lax.dot_general(chosen, high, NT, preferred_element_type=f32) + lax.dot_general(
                chosen, low, NT, preferred_element_type=f32
            )
        for pair in range(pairs):
            dk[...] = jnp.zeros_like(dk)
            dv[...] = jnp.zeros_like(dv)
            for i in range(N // BLK):
                attend_back_block(i, pair, qkv, grad_heads, kT, lse, delta, dqT, dk, dv)
                grad_qkv[pair, pl.ds(i * BLK, BLK), 0:128] = turn(dqT[...]).astype(bf16)
                at = (pair * (N // BLK) + i) * 12 // (pairs * (N // BLK))
                run(BACK["attention"][at] if at not in passed else "")
                passed.add(at)
            grad_qkv[pair, :, 128:256] = dk[...].astype(bf16)
            grad_qkv[pair, :, 256:384] = dv[...].astype(bf16)
            for i in list(range(1, S)) + [0]:
                target = lax.rem(p.s + i, S)
                rows = pl.ds(pl.multiple_of(target * R, 128), R)
                for kind in range(3):
                    lanes = pl.ds(pl.multiple_of(kind * D + p.s * wide + pair * 128, 128), 128)
                    block = grad_qkv.at[pair, rows, kind * 128 : (kind + 1) * 128]
                    if i:
                        push(block, grad_proj.at[:, lanes], from_sem.at[i - 1, pair, kind], (p.f, target))
                    else:
                        grad_proj[:, lanes] = block[...]
        run(BACK["sent"])

    passed = set()
    pl.run_scoped(
        attention,
        pltpu.VMEM(qkv_in.shape, bf16),
        pltpu.VMEM((N, wide), bf16),
        pltpu.VMEM(lse_in.shape, f32),
        pltpu.VMEM((wide, N), bf16),
        pltpu.VMEM(lse_in.shape, f32),
        pltpu.VMEM((128, BLK), f32),
        pltpu.VMEM((N, 128), f32),
        pltpu.VMEM((N, 128), f32),
    )

    def projections(wq, one, tokens_v, result, qv_sum):
        load(10, wq_in, wq)
        load(11, one_in, one)
        load(12, tokens, tokens_v)
        for i in range(1, S):
            source = lax.rem(p.s + S - i, S)
            for pair in range(pairs):
                for kind in range(3):
                    lanes = pl.ds(pl.multiple_of(kind * D + source * wide + pair * 128, 128), 128)
                    arrived(grad_proj.at[:, lanes], from_sem.at[i - 1, pair, kind])
        run(BACK["back"])
        half = 3 * D // 2
        push(
            grad_proj.at[:, pl.ds(pl.multiple_of((1 - p.c) * half, 128), half)],
            proj_pair.at[R : 2 * R, :], pair_sem.at[1], p.sibling(),
        )
        proj_pair[0:R, :] = grad_proj[:, pl.ds(pl.multiple_of(p.c * half, 128), half)]
        qv_sum[0:1, 0:D] = jnp.sum(grad_proj[:, 0:D].astype(f32), axis=0, keepdims=True)
        qv_sum[0:1, D:] = jnp.sum(grad_proj[:, 2 * D :].astype(f32), axis=0, keepdims=True)
        loads[11].wait()
        arrived(proj_pair.at[R : 2 * R, :], pair_sem.at[1])
        weight_grad(3, one, proj_pair, "qkv")
        run(BACK["input"])
        loads[10].wait()
        rows = 256
        r = wq.shape[1]

        @pl.loop(0, D // rows)
        def _(t):
            w = wq[pl.ds(t * (rows // r), rows // r)].reshape(rows, 3 * D)
            result[:, pl.ds(pl.multiple_of(t * rows, rows), rows)] = lax.dot_general(
                grad_proj[...], w, NT, preferred_element_type=f32
            )

        run(BACK["norm1"])
        loads[12].wait()
        gain = vector(smalls_f, places, "ln1_gain")

        @pl.loop(0, R // chunk)
        def _(t):
            at = pl.ds(pl.multiple_of(t * chunk, chunk), chunk)
            moved = norm_back(tokens_v[at, :].astype(f32), result[at, :], gain, 2)
            tokens_v[at, :] = (grad_middle[at, :] + moved).astype(bf16)

        cp = pltpu.make_async_copy(tokens_v, grad_tokens, load_sem.at[13])
        cp.start()
        values = dict(
            ln2_gain=sums[0:1, :], ln2_bias=sums[1:2, :], ln1_gain=sums[2:3, :],
            ln1_bias=sums[3:4, :], b_out=sums[4:5, :], b_proj=sums[5:6, :], b_fc=fc_sum[0:1, :],
            b_qv=qv_sum[0:1, :],
        )
        sm_mine[...] = jnp.zeros_like(sm_mine)
        last = 0
        for name, (start, size) in places.items():
            whole = values[name]
            for f in range(F):
                pos = start
                while pos < start + size:
                    row, lane = divmod(pos, 128)
                    count = min(128 - lane, start + size - pos)
                    at = f * size + pos - start
                    sm_mine[f, row : row + 1, lane : lane + count] = whole[:, at : at + count]
                    pos += count
            last = max(last, start + size)
        row = -(-last // 128)
        lane = lax.broadcasted_iota(jnp.int32, (1, 128), 1)
        line = jnp.zeros((1, 128), f32)
        for i in range(3):
            line = jnp.where(lane == i, jnp.sum(stats_v[i : i + 1, :], axis=1, keepdims=True), line)
        for f in range(F):
            sm_mine[f, row : row + 1, :] = line
        push(sm_mine, sm_core, sm_sem.at[0], p.sibling())
        run(BACK["small"][0])
        arrived(sm_core, sm_sem.at[0])
        sm_x[p.x] = sm_mine[...] + sm_core[...]
        for i in range(1, X):
            push(sm_x.at[p.x], sm_x.at[p.x], smx_sem.at[i - 1], p.across(i))
        run(BACK["small"][1])
        cp.wait()

    pl.run_scoped(
        projections,
        pltpu.VMEM(wq_in.shape, bf16),
        pltpu.VMEM((2 * R, D), bf16),
        pltpu.VMEM((R, D), bf16),
        pltpu.VMEM((R, D), f32),
        pltpu.VMEM((8, 2 * D), f32),
    )
    for i in range(1, X):
        arrived(sm_x.at[lax.rem(p.x + X - i, X)], smx_sem.at[i - 1])
    total = sm_x[0]
    for i in range(1, X):
        total = total + sm_x[i]
    sm_sum[...] = total
    for j in range(1, L):
        for k in range(H):
            h = lax.rem(p.h + k, H)
            push(sm_sum.at[ahead(k, j)], sm_lo.at[p.l, h], smlo_sem.at[j - 1, k], p.lo(j))
    run(BACK["small"][2])
    for k in list(range(1, H)) + [0]:
        h = lax.rem(p.h + k, H)
        sm_lo[p.l, h] = sm_sum[h * L + p.l]
        for j in range(1, L):
            arrived(sm_lo.at[lax.rem(p.l + L - j, L), h], smlo_sem.at[j - 1, k])
        total = sm_lo[0, h]
        for j in range(1, L):
            total = total + sm_lo[j, h]
        if k > 0:
            sm_core[h] = total
            push(sm_core.at[h], sm_hi.at[p.h], smhi_sem.at[k - 1], p.hi(k))
        else:
            sm_hi[p.h] = total
    run(BACK["end"])
    assert len(set(ran)) == len(ran) == 3 * len(slots) + 8
    for k in range(1, H):
        arrived(sm_hi.at[lax.rem(p.h + H - k, H)], smhi_sem.at[k - 1])
    total = sm_hi[0]
    for k in range(1, H):
        total = total + sm_hi[k]
    small_out[...] = total
    for w in range(4):
        arrived(half_out[w], core_sem.at[w])
        arrived(half_out[w], out_sem.at[w])
    arrived(gb_other, gb_sem.at[0])
    left = sum(sent)
    for rows in (2 * R, 256, 16):
        for lanes in (gbh.shape[1], 128):
            block = gbh.at[0:rows, 0:lanes]
            for _ in range(left // (2 * rows * lanes)):
                arrived(block, send_sem.at[0])
            left %= 2 * rows * lanes
    assert left == 0


def backward(cotangent, tokens, places, saved):
    F, S, H, L, X = geometry()
    R, D = tokens.shape
    wide, N, FF = D // S, R * S, saved[3].shape[2]
    pairs = wide // 128
    lead = max(X - 1, 1)
    plans = [column_plan(X, eighths) for eighths in BACK_SHARES]
    shapes = [(F, saved[i].shape[1], saved[i].shape[2] // 2) for i in (4, 3, 2, 1)]
    used = max(a + size for a, size in places.values())
    small_rows = -(-(-(-used // 128) + 1) // 8) * 8
    any_spec = pl.BlockSpec(memory_space=pl.ANY)
    vmem_spec = pl.BlockSpec(memory_space=pltpu.VMEM)
    V, D_SEM, shaped = pltpu.VMEM, pltpu.SemaphoreType.DMA, jax.ShapeDtypeStruct

    def each(shape_of, kind):
        return [
            V(shape_of(r, c, plan[1] * c // 8, plan[3] * c // 8), kind)
            for (f, r, c), plan in zip(shapes, plans)
        ]

    res = pl.pallas_call(
        functools.partial(backward_kernel, places),
        out_shape=[shaped((R, D), bf16)]
        + [shaped((r, 2 * c), f32) for f, r, c in shapes]
        + [shaped((small_rows, 128), f32)],
        in_specs=[vmem_spec] + [any_spec] * 17,
        out_specs=[any_spec] * 5 + [vmem_spec],
        scratch_shapes=[V(s, bf16) for s in shapes]
        + each(lambda r, c, reach, only: (lead, F, r, only), bf16)
        + each(lambda r, c, reach, only: (L - 1, H, r, reach), bf16)
        + each(lambda r, c, reach, only: (H - 1, r, reach), bf16)
        + each(lambda r, c, reach, only: (r, c), bf16)
        + each(lambda r, c, reach, only: (lead, r, c), bf16)
        + each(lambda r, c, reach, only: (r, c), f32)
        + [
            V((2 * R, D // 2), bf16),
            V((2 * R, FF // 2), bf16),
            V((R, FF // 2), bf16),
            V((R, D), f32),
            V((R, D), bf16),
            V((2 * R, D // 2), bf16),
            V((S - 1, R, wide), bf16),
            V((N, wide), bf16),
            V((pairs, N, 384), bf16),
            V((R, 3 * D), bf16),
            V((2 * R, 3 * D // 2), bf16),
            V((8, D), f32),
            V((8, FF), f32),
            V(saved[0].shape, f32),
            V((8, D), f32),
            V((F, small_rows, 128), f32),
            V((F, small_rows, 128), f32),
            V((X, F, small_rows, 128), f32),
            V((F, small_rows, 128), f32),
            V((L, H, small_rows, 128), f32),
            V((max(H, F), small_rows, 128), f32),
            D_SEM((14,)),
            D_SEM((2, 4)),
            D_SEM((1,)),
            D_SEM((4, lead, H, L)),
            D_SEM((4, L - 1, H)),
            D_SEM((4, H - 1)),
            D_SEM((4, lead)),
            D_SEM((4,)),
            D_SEM((4,)),
            D_SEM((2,)),
            D_SEM((S - 1,)),
            D_SEM((S - 1, pairs, 3)),
            D_SEM((1,)),
            D_SEM((lead,)),
            D_SEM((L - 1, H)),
            D_SEM((H - 1,)),
            D_SEM((2,)),
        ],
        compiler_params=pltpu.CompilerParams(
            collective_id=2, has_side_effects=True, vmem_limit_bytes=63 * 2**20
        ),
    )(cotangent, tokens, *saved)
    return res[0], res[1:5], res[5]


def hand_over(arrays, reduced, places, cells, pieces):
    used = max(a + size for a, size in places.values())
    row_of_sums = -(-used // 128)

    def kernel(*refs):
        n = len(arrays)
        given, small = refs[:n], refs[n]
        outs, vectors = refs[n + 1 : 2 * n + 1], refs[2 * n + 1 : 2 * n + 1 + len(places)]
        rms, held, in_sem, out_sem = refs[2 * n + 1 + len(places)], refs[-n - 2 : -2], refs[-2], refs[-1]
        coming, going = [], []
        for q in range(pieces):
            for i in range(n):
                rows = given[i].shape[0] // pieces
                at = pl.ds(q * rows, rows)
                coming.append(pltpu.make_async_copy(given[i].at[at], held[i].at[at], in_sem.at[i, q]))
                going.append(pltpu.make_async_copy(held[i].at[at], outs[i].at[at], out_sem.at[i, q]))
        for cp in coming:
            cp.start()
        for out, (start, size) in zip(vectors, places.values()):
            row, lane = divmod(start, 128)
            out[...] = small[row : row + out.shape[0], lane : lane + out.shape[1]]
        rms[...] = jnp.sqrt(small[row_of_sums : row_of_sums + 1, 0:3] / cells)
        for before, after in zip(coming, going):
            before.wait()
            after.start()
        for cp in going:
            cp.wait()

    any_spec, vmem_spec = pl.BlockSpec(memory_space=pl.ANY), pl.BlockSpec(memory_space=pltpu.VMEM)
    shaped = jax.ShapeDtypeStruct
    small_shapes = [shaped((max(1, s // 128), min(s, 128)), f32) for _, s in places.values()]
    res = pl.pallas_call(
        kernel,
        out_shape=[shaped(a.shape, a.dtype) for a in arrays] + small_shapes + [shaped((1, 3), f32)],
        in_specs=[any_spec] * len(arrays) + [vmem_spec],
        out_specs=[any_spec] * len(arrays) + [vmem_spec] * (len(places) + 1),
        scratch_shapes=[pltpu.VMEM(a.shape, a.dtype) for a in arrays]
        + [pltpu.SemaphoreType.DMA((len(arrays), pieces))] * 2,
        compiler_params=pltpu.CompilerParams(vmem_limit_bytes=62 * 2**20),
    )(*arrays, reduced)
    n = len(arrays)
    got = {name: v.reshape(-1) for name, v in zip(places, res[n:-1])}
    return res[:n], got, res[-1].reshape(-1)


def on_device(
    tokens, cotangent, ln1_gain, ln1_bias, w_qkv, b_qv, w_out, b_out,
    ln2_gain, ln2_bias, w_fc, b_fc, w_proj, b_proj,
):
    F, S = lax.axis_size("fsdp"), lax.axis_size("seq")
    row_count, D = tokens.shape
    named = dict(
        b_fc=b_fc, b_qv=b_qv, ln1_gain=ln1_gain, ln1_bias=ln1_bias, b_out=b_out,
        ln2_gain=ln2_gain, ln2_bias=ln2_bias, b_proj=b_proj,
    )
    places, at = {}, 0
    for name, value in named.items():
        places[name] = (at, value.shape[0])
        at += value.shape[0]
    small_rows = -(-at // 2048) * 16
    total = small_rows * 128
    flat = sum(
        jnp.pad(value, (a, total - a - size))
        for value, (a, size) in zip(named.values(), places.values())
    ).reshape(small_rows, 128)
    outs = forward(tokens, cotangent, flat, places, [w_qkv, w_out, w_fc, w_proj])
    wholes, saved, output, stats, cot_pair = outs[:4], outs[5:14], outs[14], outs[15], outs[16]
    grad_tokens, (grad_w_proj, grad_w_fc, grad_w_out, grad_w_qkv), reduced = backward(
        cotangent, tokens, places, [outs[4], *wholes, *saved, stats, cot_pair]
    )
    arrays, got, rms_values = hand_over(
        [output, grad_tokens, grad_w_qkv, grad_w_out, grad_w_fc, grad_w_proj], reduced, places,
        float(row_count * D * S * F), 2,
    )
    output, grad_tokens, grad_w_qkv, grad_w_out, grad_w_fc, grad_w_proj = arrays
    return (
        output, grad_tokens, got["ln1_gain"], got["ln1_bias"], grad_w_qkv, got["b_qv"],
        grad_w_out, got["b_out"], got["ln2_gain"], got["ln2_bias"], grad_w_fc, got["b_fc"],
        grad_w_proj, got["b_proj"], rms_values,
    )


def solution(mesh):
    in_specs = (
        P(("fsdp", "seq"), None),
        P(("fsdp", "seq"), None),
        P("fsdp"),
        P("fsdp"),
        P("fsdp", None),
        P("fsdp"),
        P("fsdp", None),
        P("fsdp"),
        P("fsdp"),
        P("fsdp"),
        P("fsdp", None),
        P("fsdp"),
        P("fsdp", None),
        P("fsdp"),
    )
    out_specs = (
        P(("fsdp", "seq"), None),
        P(("fsdp", "seq"), None),
        P("fsdp"),
        P("fsdp"),
        P("fsdp", None),
        P("fsdp"),
        P("fsdp", None),
        P("fsdp"),
        P("fsdp"),
        P("fsdp"),
        P("fsdp", None),
        P("fsdp"),
        P("fsdp", None),
        P("fsdp"),
        P(),
    )
    return jax.shard_map(
        on_device, mesh=mesh, in_specs=in_specs, out_specs=out_specs, check_vma=False
    )
```
